128 devices in a mesh: pipe: 2 (over z_lo), tensor: 8 (over x, z_hi), dp: 8 (over y, core).
Axes of the slice: x: 4, y: 4, z: 4 (z_hi: 2, z_lo: 2; z = z_hi * 2 + z_lo), core: 2. Of those that a mesh axis runs over, the one named last changes fastest.
Arguments:
- inputs: bfloat16 [2, 768, 8, 1024], P(None, 'tensor', 'dp'), may hold values from -6 to 6
- segment_ids: int32 [2, 8, 768], P(None, 'dp'), may hold values from 0 to 3, never falling along the last dimension, each value on 1 to 384 neighbouring positions
- cotangent: bfloat16 [2, 768, 8, 1024], P(None, 'tensor', 'dp'), may hold values from -6 to 6
- ln1_gain: bfloat16 [2, 1024], P('pipe'), may hold values from 0.099609375 to 1.8984375
- ln1_bias: bfloat16 [2, 1024], P('pipe'), may hold values from -1.5 to 1.5
- w_qkv: bfloat16 [2, 1024, 3, 1024], P('pipe', None, None, 'tensor'), may hold values from -0.1875 to 0.1875
- qv_bias: bfloat16 [2, 2, 1024], P('pipe', None, 'tensor'), may hold values from -1.5 to 1.5
- w_out: bfloat16 [2, 1024, 1024], P('pipe', 'tensor'), may hold values from -1 to 1
- out_bias: bfloat16 [2, 1024], P('pipe'), may hold values from -1.5 to 1.5
- ln2_gain: bfloat16 [2, 1024], P('pipe'), may hold values from 0.099609375 to 1.8984375
- ln2_bias: bfloat16 [2, 1024], P('pipe'), may hold values from -1.5 to 1.5
- w_fc: bfloat16 [2, 1024, 4096], P('pipe', None, 'tensor'), may hold values from -0.1875 to 0.1875
- fc_bias: bfloat16 [2, 4096], P('pipe', 'tensor'), may hold values from -1.5 to 1.5
- w_proj: bfloat16 [2, 4096, 1024], P('pipe', 'tensor'), may hold values from -0.125 to 0.125
- proj_bias: bfloat16 [2, 1024], P('pipe'), may hold values from -1.5 to 1.5
Outputs:
- activations: bfloat16 [2, 2, 768, 8, 1024], P('pipe', None, 'tensor', 'dp')
- in_grads: bfloat16 [2, 2, 768, 8, 1024], P('pipe', None, 'tensor', 'dp')
- ln1_gain_grad: float32 [2, 1024], P('pipe')
- ln1_bias_grad: float32 [2, 1024], P('pipe')
- w_qkv_grad: float32 [2, 1024, 3, 1024], P('pipe', None, None, 'tensor')
- qv_bias_grad: float32 [2, 2, 1024], P('pipe', None, 'tensor')
- w_out_grad: float32 [2, 1024, 1024], P('pipe', 'tensor')
- out_bias_grad: float32 [2, 1024], P('pipe')
- ln2_gain_grad: float32 [2, 1024], P('pipe')
- ln2_bias_grad: float32 [2, 1024], P('pipe')
- w_fc_grad: float32 [2, 1024, 4096], P('pipe', None, 'tensor')
- fc_bias_grad: float32 [2, 4096], P('pipe', 'tensor')
- w_proj_grad: float32 [2, 4096, 1024], P('pipe', 'tensor')
- proj_bias_grad: float32 [2, 1024], P('pipe')
The draws below stay inside these ranges and needn't reach their ends.
Inputs may be any that keep to these rules, and one draw needn't show every extreme that they name: `segment_ids`: along each sequence the document number never falls; each document has 1 to 384 tokens.
All inputs are finite; a program needn't handle non-finite values.
Results may differ from the reference program's by a relative error of at most 0.024.
Values may be sent and summed in bfloat16 or wider, within the bound.
No kernel may reach another device: no remote copies, remote signals or barrier semaphores. Data moves between devices by JAX's collectives and lax.ppermute only.
A program may use at most 128 MiB of HBM per device.

```python
import math
import jax
import jax.numpy as jnp
import numpy as np
from jax import lax

D = 1024
HEADS = 16
HEAD_DIM = 64
FF = 4096
LENGTH = 768
MICRO = 2
DOCS = 4
DOC_MOST = 384
SEQS = 8


def block_scale(own_key, dims, pieces, smallest, high):
    loudness = 1.0
    for position, parts in pieces:
        heights = jax.random.uniform(jax.random.fold_in(jax.random.fold_in(own_key, 6), position), (parts,), jnp.float32, smallest / len(pieces), high / len(pieces))
        loudness = loudness * jnp.repeat(jnp.exp(heights), dims[position] // parts).reshape((-1,) + (1,) * (len(dims) - 1 - position))
    return loudness


def split_up(number_of, total, reach, skew):
    portions = [(1 << 20) // math.isqrt(rank ** skew) + 1 for rank in range(2, number_of + 1)]
    rest, counts = total - reach - (number_of - 1), [1] * (number_of - 1)
    while rest > 0:
        movable = [i for i in range(number_of - 1) if counts[i] < reach]
        whole, left = sum([portions[i] for i in movable]), rest
        for i in movable:
            extra = min(reach - counts[i], max(1, left * portions[i] // whole), rest)
            counts[i] = counts[i] + extra
            rest = rest - extra
    return np.array([reach] + counts)


def ragged_sizes(rng, number_of, total, reach, slope):
    if number_of == 2:
        one = jax.random.randint(rng, (), max(1, total - reach), min(reach, total - 1) + 1)
        return jnp.stack([one, total - one])
    tallies = jnp.asarray(split_up(number_of, total, reach, slope), jnp.int32)
    pairs = (number_of - 1) // 2
    source_of, taker = tallies[1:1 + 2 * pairs:2], tallies[2:2 + 2 * pairs:2]
    slack = jnp.minimum(source_of - 1, reach - taker)
    moved = jax.random.randint(jax.random.fold_in(rng, 1), (pairs,), 0, 1 << 20) % (slack + 1)
    tallies = tallies.at[1:1 + 2 * pairs:2].set(source_of - moved).at[2:2 + 2 * pairs:2].set(taker + moved)
    return tallies[jax.random.permutation(jax.random.fold_in(rng, 2), number_of)]


def normal_values(stream_key, dims, scale, limit, split=(), kind=jnp.bfloat16):
    array = jax.random.normal(stream_key, dims, jnp.float32) * scale
    if len(split) > 0:
        array = block_scale(stream_key, dims, split, -0.22, 0.18) * array
    return jnp.clip(array, min=-limit, max=limit).astype(kind)


def setup_inputs(seed: int = 0) -> dict:
    key_list = jax.random.split(jax.random.key(seed), 16)
    inputs = normal_values(key_list[0], (MICRO, LENGTH, SEQS, D), 1.0, 6.0, ((1, 8), (2, 8)))
    segment_ids = jax.vmap(lambda own: jnp.searchsorted(jnp.cumsum(ragged_sizes(own, DOCS, LENGTH, DOC_MOST, 1)), jnp.arange(LENGTH), side="right"))(jax.random.split(key_list[1], MICRO * SEQS)).reshape((MICRO, SEQS, LENGTH)).astype(jnp.int32)
    cotangent = normal_values(key_list[2], (MICRO, LENGTH, SEQS, D), 1.0, 6.0, ((1, 8), (2, 8)))
    ln1_gain = jnp.clip(1.0 + 0.18 * jax.random.normal(key_list[3], (2, D), jnp.float32), 0.099609375, 1.8984375).astype(jnp.bfloat16)
    ln1_bias = normal_values(key_list[4], (2, D), 0.3, 1.5, ((0, 2),))
    w_qkv = normal_values(key_list[5], (2, D, 3, D), D ** -0.5, 0.1875, ((0, 2), (3, 8)))
    qv_bias = normal_values(key_list[6], (2, 2, D), 0.3, 1.5, ((0, 2), (2, 8)))
    w_out = normal_values(key_list[7], (2, D, D), (D // 32) ** -0.5, 1.0, ((0, 2), (1, 8)))
    out_bias = normal_values(key_list[8], (2, D), 0.3, 1.5, ((0, 2),))
    ln2_gain = jnp.clip(1.0 + 0.18 * jax.random.normal(key_list[9], (2, D), jnp.float32), 0.099609375, 1.8984375).astype(jnp.bfloat16)
    ln2_bias = normal_values(key_list[10], (2, D), 0.3, 1.5, ((0, 2),))
    w_fc = normal_values(key_list[11], (2, D, FF), D ** -0.5, 0.1875, ((0, 2), (2, 8)))
    fc_bias = normal_values(key_list[12], (2, FF), 0.3, 1.5, ((0, 2), (1, 8)))
    w_proj = normal_values(key_list[13], (2, FF, D), (FF // 2) ** -0.5, 0.125, ((0, 2), (1, 8)))
    proj_bias = normal_values(key_list[14], (2, D), 0.3, 1.5, ((0, 2),))
    return {"inputs": inputs, "segment_ids": segment_ids, "cotangent": cotangent, "ln1_gain": ln1_gain, "ln1_bias": ln1_bias, "w_qkv": w_qkv, "qv_bias": qv_bias, "w_out": w_out, "out_bias": out_bias, "ln2_gain": ln2_gain, "ln2_bias": ln2_bias, "w_fc": w_fc, "fc_bias": fc_bias, "w_proj": w_proj, "proj_bias": proj_bias}


@jax.custom_vjp
def low(v):
    return lax.optimization_barrier(v.astype(jnp.bfloat16)).astype(jnp.float32)

@jax.custom_vjp
def low_back(v):
    return v

def low_keep(v):
    return (low(v), None)

def low_pass(kept, grad):
    return (grad,)

def back_keep(v):
    return (v, None)

def back_low(kept, grad):
    return (low(grad),)
low.defvjp(low_keep, low_pass)
low_back.defvjp(back_keep, back_low)
epsilon = 1e-05
exact_mode = lax.Precision.HIGHEST

def norm_rows(stream, gain, shift):
    average = lax.optimization_barrier(jnp.mean(stream, axis=-1, keepdims=True))
    centred = stream - average
    variance = lax.optimization_barrier(jnp.mean(centred * centred, axis=-1, keepdims=True))
    return centred * lax.rsqrt(variance + epsilon) * gain + shift

def attend(query, key_rows, value_rows, segment):
    scores = jnp.einsum('qhe,khe->hqk', query, key_rows, precision=exact_mode) * HEAD_DIM ** (-0.5)
    scores = low_back(scores)
    positions = jnp.arange(segment.shape[0])
    allowed = (segment[:, None] == segment[None, :]) & (positions[None, :] <= positions[:, None])
    scores = jnp.where(allowed[None], scores, -1e+30)
    largest = lax.optimization_barrier(jnp.max(scores, axis=-1, keepdims=True))
    exponent_terms = jnp.exp(scores - largest)
    soft_weights = exponent_terms / lax.optimization_barrier(jnp.sum(exponent_terms, axis=-1, keepdims=True))
    return jnp.einsum('hqk,khe->qhe', low(soft_weights), value_rows, precision=exact_mode)

def per_sequence(element):
    stacked, segment = element
    return jax.checkpoint(attend)(stacked[:, 0], stacked[:, 1], stacked[:, 2], segment)

def block_layer(stream, params, segment_rows):
    gain_one, shift_one, w_qkv, qv_bias, w_out, out_bias, gain_two, shift_two, w_fc, fc_bias, w_proj, proj_bias = params
    length, count, width = stream.shape
    normed = low(norm_rows(stream, gain_one, shift_one))
    projected = jnp.einsum('lsd,dcw->lscw', normed, w_qkv, precision=exact_mode)
    biases = jnp.stack([qv_bias[0], jnp.zeros_like(qv_bias[0]), qv_bias[1]])
    projected = low(low_back(projected + biases))
    head_view = jnp.moveaxis(projected.reshape(length, count, 3, HEADS, HEAD_DIM), 1, 0)
    context = lax.map(per_sequence, (head_view, segment_rows))
    context = jnp.moveaxis(context, 0, 1).reshape(length, count, width)
    context = low(low_back(context))
    attention = jnp.einsum('lsw,wd->lsd', context, w_out, precision=exact_mode) + out_bias
    middle = stream + low_back(attention)
    normed_two = low(norm_rows(middle, gain_two, shift_two))
    gelu_input = jnp.einsum('lsd,dw->lsw', normed_two, w_fc, precision=exact_mode) + fc_bias
    gelu_input = low_back(gelu_input)
    hidden = low(jax.nn.gelu(gelu_input, approximate=True))
    feed = jnp.einsum('lsw,wd->lsd', hidden, w_proj, precision=exact_mode) + proj_bias
    return middle + low_back(feed)

def reference(inputs, segment_ids, cotangent, ln1_gain, ln1_bias, w_qkv, qv_bias, w_out, out_bias, ln2_gain, ln2_bias, w_fc, fc_bias, w_proj, proj_bias):
    stacked = tuple((item.astype(jnp.float32) for item in (ln1_gain, ln1_bias, w_qkv, qv_bias, w_out, out_bias, ln2_gain, ln2_bias, w_fc, fc_bias, w_proj, proj_bias)))

    def forward(stream_start, shift_terms, params):
        first_params = tuple((item[0] for item in params))
        second_params = tuple((item[1] for item in params))
        first_out = []
        second_out = []
        for micro_index in range(MICRO):
            segment_rows = segment_ids[micro_index]
            hidden_out = low(block_layer(stream_start[micro_index], first_params, segment_rows))
            first_out.append(hidden_out)
            second_in = low_back(hidden_out + shift_terms[micro_index])
            second_out.append(block_layer(second_in, second_params, segment_rows))
        return (jnp.stack(first_out), jnp.stack(second_out))
    stream_start = inputs.astype(jnp.float32)
    shift_terms = jnp.zeros_like(stream_start)
    (first_act, second_act), pullback = jax.vjp(forward, stream_start, shift_terms, stacked)
    input_grad, shift_grad, param_grads = pullback((jnp.zeros_like(first_act), cotangent.astype(jnp.float32)))
    activations = jnp.stack([first_act, second_act]).astype(jnp.bfloat16)
    in_grads = jnp.stack([input_grad, shift_grad]).astype(jnp.bfloat16)
    return (activations, in_grads, param_grads[0], param_grads[1], param_grads[2], param_grads[3], param_grads[4], param_grads[5], param_grads[6], param_grads[7], param_grads[8], param_grads[9], param_grads[10], param_grads[11])
```

```python
import jax
import jax.numpy as jnp
from jax import lax
from jax.sharding import PartitionSpec as P

HEAD_DIM = 64
BLOCK = 96
WIDTH = 1024
epsilon = 1e-05
AXES = ("pipe", "tensor", "dp")
bf16 = jnp.bfloat16
f32 = jnp.float32


def spot(axes, x, z, y, core):
    index = 0
    for axis in axes:
        if axis == "pipe":
            index = index * 2 + z % 2
        elif axis == "tensor":
            index = index * 8 + x * 2 + z // 2
        else:
            index = index * 8 + y * 2 + core
    return index


def move(array, axes, rule):
    pairs = {}
    for x in range(4):
        for z in range(4):
            for y in range(4):
                for core in range(2):
                    goal = rule(x, z, y, core)
                    if goal is not None:
                        pairs[spot(axes, x, z, y, core)] = spot(axes, *goal)
    return lax.ppermute(array, axes, sorted(pairs.items()))


def along_x(array, by):
    return move(array, ("tensor",), lambda x, z, y, core: ((x + by) % 4, z, y, core))


def along_y(array, by):
    return move(array, ("dp",), lambda x, z, y, core: (x, z, (y + by) % 4, core))


def along_z(array, by, only=None):
    def rule(x, z, y, core):
        return (x, (z + by) % 4, y, core) if only is None or z % 2 == only else None

    return move(array, ("pipe", "tensor"), rule)


def other_core(array):
    return move(array, ("dp",), lambda x, z, y, core: (x, z, y, 1 - core))


def turned(array):
    return move(
        array, ("tensor", "dp"), lambda x, z, y, core: (x, core * 2 + z % 2, y, z // 2)
    )


def pick(array, index, axis=0):
    return lax.dynamic_index_in_dim(array, index, axis, keepdims=False)


def place(buffer, piece, starts):
    return lax.dynamic_update_slice(buffer, piece, starts)


def gather_rows(rows):
    return jnp.concatenate([rows] + [along_x(rows, by) for by in (1, 2, 3)], axis=0)


def scatter_rows(partial):
    parts = partial.astype(bf16).reshape(4, BLOCK, WIDTH)
    total = parts[0].astype(f32)
    for by in (1, 2, 3):
        total = total + along_x(parts[by], -by).astype(f32)
    return total


def dot(left, right, left_dim, right_dim):
    return lax.dot_general(
        left, right, (((left_dim,), (right_dim,)), ((), ())), preferred_element_type=f32
    )


def norm_forward(stream, gain, shift):
    average = jnp.mean(stream, axis=-1, keepdims=True)
    centred = stream - average
    inverse_scale = lax.rsqrt(jnp.mean(centred * centred, axis=-1, keepdims=True) + epsilon)
    standard = centred * inverse_scale
    return (standard * gain + shift).astype(bf16), standard, inverse_scale


def norm_backward(incoming, standard, inverse_scale, gain):
    scaled = incoming * gain
    correction = (
        scaled
        - jnp.mean(scaled, axis=-1, keepdims=True)
        - standard * jnp.mean(scaled * standard, axis=-1, keepdims=True)
    )
    return (
        correction * inverse_scale,
        jnp.sum(incoming * standard, axis=0),
        jnp.sum(incoming, axis=0),
    )


def masked_scores(query, keys, allowed):
    scores = jnp.einsum("qhe,khe->hqk", query, keys, preferred_element_type=f32)
    return jnp.where(allowed[None], scores * HEAD_DIM ** (-0.5), -1e30)


def attend_forward(query, keys, values, allowed):
    scores = masked_scores(query, keys, allowed)
    largest = jnp.max(scores, axis=-1, keepdims=True)
    terms = jnp.exp(scores - largest)
    summed = jnp.sum(terms, axis=-1, keepdims=True)
    weights = (terms / summed).astype(bf16)
    context = jnp.einsum("hqk,khe->qhe", weights, values, preferred_element_type=f32)
    return context.astype(bf16), largest + jnp.log(summed)


def attend_backward(query, keys, values, allowed, log_total, context_grad):
    weights = jnp.exp(masked_scores(query, keys, allowed) - log_total)
    weight_grad = jnp.einsum("qhe,khe->hqk", context_grad, values, preferred_element_type=f32)
    value_grad = jnp.einsum(
        "hqk,qhe->khe", weights.astype(bf16), context_grad, preferred_element_type=f32
    )
    correction = jnp.sum(weights * weight_grad, axis=-1, keepdims=True)
    score_grad = (weights * (weight_grad - correction)).astype(bf16)
    query_grad = jnp.einsum("hqk,khe->qhe", score_grad, keys, preferred_element_type=f32)
    key_grad = jnp.einsum("hqk,qhe->khe", score_grad, query, preferred_element_type=f32)
    scale = HEAD_DIM ** (-0.5)
    return query_grad * scale, key_grad * scale, value_grad


def split_heads(projected):
    view = projected.reshape(4 * BLOCK, 2, 3, 2, HEAD_DIM)
    return tuple(view[:, :, part].reshape(4 * BLOCK, 4, HEAD_DIM) for part in range(3))


def layer_forward(stream, allowed, vectors, weights):
    gain_one, shift_one, out_bias, gain_two, shift_two, proj_bias, qkv_bias, fc_bias = vectors
    w_qkv, w_out, w_fc, w_proj = weights
    normed_one, standard_one, inverse_one = norm_forward(stream, gain_one, shift_one)
    rows_one = gather_rows(normed_one)
    projected = (dot(rows_one, w_qkv, 1, 0) + qkv_bias).astype(bf16)
    query, key, value = split_heads(projected)
    both = jnp.stack([key, value]).reshape(2, 4 * BLOCK, 256)
    keys, values = (
        part.reshape(8 * BLOCK, 4, HEAD_DIM)
        for part in jnp.concatenate([both, other_core(both)], axis=1)
    )
    context, log_total = attend_forward(query, keys, values, allowed)
    context = context.reshape(4 * BLOCK, 256)
    middle = stream + scatter_rows(dot(context, w_out, 1, 0)) + out_bias
    normed_two, standard_two, inverse_two = norm_forward(middle, gain_two, shift_two)
    rows_two = gather_rows(normed_two)
    gelu_input = dot(rows_two, w_fc, 1, 0) + fc_bias
    hidden = jax.nn.gelu(gelu_input, approximate=True).astype(bf16)
    result = middle + scatter_rows(dot(hidden, w_proj, 1, 0)) + proj_bias
    saved = (
        (standard_one, inverse_one, rows_one),
        (query, keys, values, log_total, context),
        (standard_two, inverse_two, rows_two, gelu_input, hidden),
    )
    return result.astype(bf16), saved


def halves(grad, rows):
    return grad.astype(bf16).reshape(2, 2, rows, WIDTH)


def layer_backward(incoming, allowed, vectors, weights, saved):
    gain_one, shift_one, out_bias, gain_two, shift_two, proj_bias, qkv_bias, fc_bias = vectors
    w_qkv, w_out, w_fc, w_proj = weights
    (
        (standard_one, inverse_one, rows_one),
        (query, keys, values, log_total, context),
        (standard_two, inverse_two, rows_two, gelu_input, hidden),
    ) = saved
    grad_feed = incoming.astype(bf16)
    proj_bias_grad = jnp.sum(grad_feed.astype(f32), axis=0)
    feed_rows = gather_rows(grad_feed)
    hidden_grad = dot(feed_rows, w_proj, 1, 1)
    gelu_pull = jax.vjp(lambda item: jax.nn.gelu(item, approximate=True), gelu_input)[1]
    gelu_grad = gelu_pull(hidden_grad)[0].astype(bf16)
    normed_two_grad = scatter_rows(dot(gelu_grad, w_fc, 1, 1))
    fc_bias_grad = jnp.sum(gelu_grad.astype(f32), axis=0)
    w_proj_grad = dot(hidden, feed_rows, 0, 0)
    w_fc_grad = dot(gelu_grad, rows_two, 0, 0)
    middle_norm, gain_two_grad, shift_two_grad = norm_backward(
        normed_two_grad, standard_two, inverse_two, gain_two
    )
    middle_grad = incoming + middle_norm
    grad_attention = middle_grad.astype(bf16)
    out_bias_grad = jnp.sum(grad_attention.astype(f32), axis=0)
    attention_rows = gather_rows(grad_attention)
    context_grad = dot(attention_rows, w_out, 1, 1).astype(bf16)
    w_out_grad = dot(context, attention_rows, 0, 0)
    query_grad, key_grad, value_grad = attend_backward(
        query,
        keys,
        values,
        allowed,
        log_total,
        context_grad.reshape(4 * BLOCK, 4, HEAD_DIM),
    )
    both = jnp.stack([key_grad, value_grad]).reshape(2, 8 * BLOCK, 256)
    arrived = other_core(both[:, 4 * BLOCK :].astype(bf16))
    summed = both[:, : 4 * BLOCK] + arrived.astype(f32)
    triple = jnp.stack([query_grad.reshape(4 * BLOCK, 256), summed[0], summed[1]], axis=1)
    triple = triple.astype(bf16).reshape(4 * BLOCK, 3, 2, 128)
    triple = jnp.moveaxis(triple, 2, 1).reshape(4 * BLOCK, 768)
    normed_one_grad = scatter_rows(dot(triple, w_qkv, 1, 1))
    qkv_bias_grad = jnp.sum(triple.astype(f32), axis=0)
    w_qkv_grad = dot(triple, rows_one, 0, 0)
    stream_norm, gain_one_grad, shift_one_grad = norm_backward(
        normed_one_grad, standard_one, inverse_one, gain_one
    )
    stream_grad = middle_grad + stream_norm
    feed_group = jnp.concatenate([halves(w_fc_grad, 256), halves(w_proj_grad, 256)], axis=2)
    attention_group = jnp.concatenate([halves(w_qkv_grad, 192), halves(w_out_grad, 64)], axis=2)
    early = (out_bias_grad, gain_two_grad, shift_two_grad, proj_bias_grad, fc_bias_grad)
    late = (gain_one_grad, shift_one_grad, qkv_bias_grad)
    return stream_grad, feed_group, attention_group, early, late


def to_owner(group, layer, here):
    pipe, high, core = here
    sent = other_core(pick(group, 1 - core, 1))
    mine = (pick(group, core, 1).astype(f32) + sent.astype(f32)).astype(bf16)
    near, far = pick(mine, high), pick(mine, 1 - high)
    step = 1 if layer == 1 else -1
    total = jnp.where(pipe == layer, near.astype(f32), 0.0)
    total = total + along_z(near, step, only=1 - layer).astype(f32)
    total = total + along_z(far, -step, only=1 - layer).astype(f32)
    total = total + along_z(far, 2, only=layer).astype(f32)
    return total.astype(bf16)


def over_y(total):
    rows = total.shape[0]
    y = lax.axis_index("dp") // 2
    chunks = total.reshape(4, rows // 4, WIDTH)
    own = pick(chunks, y).astype(f32)
    for by in (1, 2, 3):
        own = own + along_y(pick(chunks, (y + by) % 4), by).astype(f32)
    own = own.astype(bf16)
    whole = jnp.zeros((4, rows // 4, WIDTH), bf16)
    whole = place(whole, own[None], (y, 0, 0))
    for by in (1, 2, 3):
        whole = place(whole, along_y(own, by)[None], ((y - by) % 4, 0, 0))
    whole = whole.reshape(rows, WIDTH)
    core = lax.axis_index("dp") % 2
    both = jnp.zeros((2, rows, WIDTH), bf16)
    both = place(both, whole[None], (core, 0, 0))
    return place(both, other_core(whole)[None], (1 - core, 0, 0)).astype(f32)


def everywhere(array):
    array = array + other_core(array)
    for along in (along_x, along_y, along_z):
        array = array + along(array, 1) + along(array, 2) + along(array, 3)
    return array


def spread_weights(here, w_qkv, w_out, w_fc, w_proj, smalls):
    pipe, high, core = here
    z = high * 2 + pipe
    group_one = jnp.concatenate(
        [lax.dynamic_slice_in_dim(w_qkv, core * 512, 512, 0), smalls], axis=0
    )
    group_two = jnp.concatenate(
        [
            lax.dynamic_slice_in_dim(w_out, core * 64, 64, 0),
            lax.dynamic_slice_in_dim(w_proj, core * 256, 256, 0),
        ],
        axis=0,
    )
    group_three = lax.dynamic_slice_in_dim(w_fc, core * 512, 512, 0)
    all_qkv = jnp.zeros((2, 1024, 768), bf16)
    all_out = jnp.zeros((2, 256, 1024), bf16)
    all_fc = jnp.zeros((2, 1024, 1024), bf16)
    all_proj = jnp.zeros((2, 1024, 1024), bf16)
    all_small = jnp.zeros((2, 2, 32, 384), bf16)
    all_qkv = place(all_qkv, w_qkv[None], (pipe, 0, high * 384))
    all_out = place(all_out, w_out[None], (pipe, high * 128, 0))
    all_fc = place(all_fc, w_fc[None], (pipe, 0, high * 512))
    all_proj = place(all_proj, w_proj[None], (pipe, high * 512, 0))
    all_small = place(all_small, smalls[None, None], (pipe, high, 0, 0))
    order = (1, 3, 2)
    came = [along_z(group_one, by) for by in order]
    swapped = other_core(jnp.stack([item[:512] for item in came]))
    for i, by in enumerate(order):
        source = (z - by) % 4
        layer, slot = source % 2, source // 2
        all_small = place(all_small, came[i][None, None, 512:], (layer, slot, 0, 0))
        all_qkv = place(all_qkv, came[i][None, :512], (layer, core * 512, slot * 384))
        all_qkv = place(all_qkv, swapped[i][None], (layer, (1 - core) * 512, slot * 384))
    came = [along_z(group_two, by) for by in order]
    swapped = other_core(jnp.stack(came))
    for i, by in enumerate(order):
        source = (z - by) % 4
        layer, slot = source % 2, source // 2
        for half, item in ((core, came[i]), (1 - core, swapped[i])):
            all_out = place(all_out, item[None, :64], (layer, slot * 128 + half * 64, 0))
            all_proj = place(all_proj, item[None, 64:], (layer, slot * 512 + half * 256, 0))
    came = [along_z(group_three, by) for by in order]
    swapped = other_core(jnp.stack(came))
    for i, by in enumerate(order):
        source = (z - by) % 4
        layer, slot = source % 2, source // 2
        for half, item in ((core, came[i]), (1 - core, swapped[i])):
            all_fc = place(all_fc, item[None], (layer, half * 512, slot * 512))
    return all_qkv, all_out, all_fc, all_proj, all_small


def on_device(
    inputs,
    segment_ids,
    cotangent,
    ln1_gain,
    ln1_bias,
    w_qkv,
    qv_bias,
    w_out,
    out_bias,
    ln2_gain,
    ln2_bias,
    w_fc,
    fc_bias,
    w_proj,
    proj_bias,
):
    pipe = lax.axis_index("pipe")
    tensor = lax.axis_index("tensor")
    dp = lax.axis_index("dp")
    x, high, core = tensor // 2, tensor % 2, dp % 2
    here = (pipe, high, core)
    stream = turned(pick(inputs, pipe).reshape(BLOCK, WIDTH)).astype(f32)
    cotangent_rows = turned(pick(cotangent, pipe).reshape(BLOCK, WIDTH)).astype(f32)
    segments = pick(segment_ids, pipe).reshape(8, BLOCK)
    segments = jnp.where(high == core, segments, other_core(segments))
    slots = ((x - jnp.arange(4)) % 4) * 2
    blocks = jnp.concatenate([slots + core, slots + 1 - core])
    numbers = segments[blocks].reshape(-1)
    positions = (blocks[:, None] * BLOCK + jnp.arange(BLOCK)[None]).reshape(-1)
    allowed = (numbers[: 4 * BLOCK, None] == numbers[None]) & (
        positions[None] <= positions[: 4 * BLOCK, None]
    )

    smalls = jnp.concatenate(
        [
            ln1_gain[0],
            ln1_bias[0],
            out_bias[0],
            ln2_gain[0],
            ln2_bias[0],
            proj_bias[0],
            qv_bias[0].reshape(-1),
            fc_bias[0],
            jnp.zeros((32 * 384 - 6912,), bf16),
        ]
    ).reshape(32, 384)
    all_qkv, all_out, all_fc, all_proj, all_small = spread_weights(
        here, w_qkv[0].reshape(WIDTH, 384), w_out[0], w_fc[0], w_proj[0], smalls
    )
    weights, vectors = [], []
    for layer in range(2):
        weights.append((all_qkv[layer], all_out[layer], all_fc[layer], all_proj[layer]))
        flat = all_small[layer].reshape(2, -1).astype(f32)
        norms = tuple(flat[0, i * WIDTH : (i + 1) * WIDTH] for i in range(6))
        pairs = flat[:, 6144:6400].reshape(2, 2, 128)
        none = jnp.zeros((2, 128), f32)
        qkv_bias = jnp.stack([pairs[:, 0], none, pairs[:, 1]], axis=1).reshape(-1)
        vectors.append(norms + (qkv_bias, flat[:, 6400:6912].reshape(-1)))

    first, saved_first = layer_forward(stream, allowed, vectors[0], weights[0])
    second, saved_second = layer_forward(first.astype(f32), allowed, vectors[1], weights[1])
    middle_grad, feed_one, attention_one, early_one, late_one = layer_backward(
        cotangent_rows, allowed, vectors[1], weights[1], saved_second
    )
    middle_low = middle_grad.astype(bf16)
    feed_owned = to_owner(feed_one, 1, here)
    attention_owned = to_owner(attention_one, 1, here)
    last_grad, feed_zero, attention_zero, early_zero, late_zero = layer_backward(
        middle_low.astype(f32), allowed, vectors[0], weights[0], saved_first
    )
    last_low = last_grad.astype(bf16)
    feed_owned = jnp.where(pipe == 1, feed_owned, to_owner(feed_zero, 0, here))
    attention_owned = jnp.where(pipe == 1, attention_owned, to_owner(attention_zero, 0, here))
    feed_total = over_y(feed_owned)
    attention_total = over_y(attention_owned)

    def bias_rows(fc_bias_grad):
        return place(jnp.zeros((4, WIDTH), f32), fc_bias_grad[None], (x, 0))

    def late_rows(late):
        gain_grad, shift_grad, qkv_grad = late
        parts = qkv_grad.reshape(2, 3, 128)
        pairs = jnp.stack([parts[:, 0], parts[:, 2]]).reshape(2, 256)
        wide = place(jnp.zeros((2, WIDTH), f32), pairs, (0, x * 256))
        return jnp.concatenate([gain_grad[None], shift_grad[None], wide])

    early = jnp.stack(
        [
            jnp.concatenate([jnp.stack(item[:4]), bias_rows(item[4])])
            for item in (early_zero, early_one)
        ]
    )
    early = pick(lax.psum(early, AXES), pipe)
    late = pick(everywhere(jnp.stack([late_rows(late_zero), late_rows(late_one)])), pipe)

    w_fc_grad = feed_total[:, :256].reshape(512, WIDTH).T
    w_proj_grad = feed_total[:, 256:].reshape(512, WIDTH)
    w_qkv_grad = attention_total[:, :192].reshape(384, WIDTH).T.reshape(WIDTH, 3, 128)
    w_out_grad = attention_total[:, 192:].reshape(128, WIDTH)
    fc_bias_grad = lax.dynamic_slice(early[4:], (x, high * 512), (1, 512))[0]
    qv_bias_grad = lax.dynamic_slice(late[2:], (0, tensor * 128), (2, 128))

    def placed(own, other):
        def crossed(array):
            return move(
                array,
                AXES,
                lambda x, z, y, core: (x, core * 2 + 1 - z % 2, y, z // 2),
            )

        stays = turned(own)
        comes = crossed(other)
        return jnp.where(pipe == 0, jnp.stack([stays, comes]), jnp.stack([comes, stays]))

    activations = placed(
        jnp.where(pipe == 0, first, second), jnp.where(pipe == 0, second, first)
    )
    in_grads = placed(
        jnp.where(pipe == 0, last_low, middle_low), jnp.where(pipe == 0, middle_low, last_low)
    )
    return (
        activations[None, :, :, None],
        in_grads[None, :, :, None],
        late[0][None],
        late[1][None],
        w_qkv_grad[None],
        qv_bias_grad[None],
        w_out_grad[None],
        early[0][None],
        early[1][None],
        early[2][None],
        w_fc_grad[None],
        fc_bias_grad[None],
        w_proj_grad[None],
        early[3][None],
    )


def solution(mesh):
    return jax.shard_map(
        on_device,
        mesh=mesh,
        in_specs=(
            P(None, "tensor", "dp", None),
            P(None, "dp", None),
            P(None, "tensor", "dp", None),
            P("pipe", None),
            P("pipe", None),
            P("pipe", None, None, "tensor"),
            P("pipe", None, "tensor"),
            P("pipe", "tensor", None),
            P("pipe", None),
            P("pipe", None),
            P("pipe", None),
            P("pipe", None, "tensor"),
            P("pipe", "tensor"),
            P("pipe", "tensor", None),
            P("pipe", None),
        ),
        out_specs=(
            P("pipe", None, "tensor", "dp", None),
            P("pipe", None, "tensor", "dp", None),
            P("pipe", None),
            P("pipe", None),
            P("pipe", None, None, "tensor"),
            P("pipe", None, "tensor"),
            P("pipe", "tensor", None),
            P("pipe", None),
            P("pipe", None),
            P("pipe", None),
            P("pipe", None, "tensor"),
            P("pipe", "tensor"),
            P("pipe", "tensor", None),
            P("pipe", None),
        ),
        check_vma=False,
    )
```

```python
import jax
import jax.numpy as jnp
from jax import lax
from jax.experimental import pallas as pl
from jax.experimental.pallas import tpu as pltpu
from jax.sharding import PartitionSpec as P

HEAD_DIM = 64
BLOCK = 96
WIDTH = 1024
epsilon = 1e-05
AXES = ("pipe", "tensor", "dp")
bf16 = jnp.bfloat16
f32 = jnp.float32


def spot(axes, x, z, y, core):
    index = 0
    for axis in axes:
        if axis == "pipe":
            index = index * 2 + z % 2
        elif axis == "tensor":
            index = index * 8 + x * 2 + z // 2
        else:
            index = index * 8 + y * 2 + core
    return index


def move(array, axes, rule):
    pairs = {}
    for x in range(4):
        for z in range(4):
            for y in range(4):
                for core in range(2):
                    goal = rule(x, z, y, core)
                    if goal is not None:
                        pairs[spot(axes, x, z, y, core)] = spot(axes, *goal)
    return lax.ppermute(array, axes, sorted(pairs.items()))


def along_x(array, by):
    return move(array, ("tensor",), lambda x, z, y, core: ((x + by) % 4, z, y, core))


def along_y(array, by):
    return move(array, ("dp",), lambda x, z, y, core: (x, z, (y + by) % 4, core))


def along_z(array, by, only=None):
    def rule(x, z, y, core):
        return (x, (z + by) % 4, y, core) if only is None or z % 2 == only else None

    return move(array, ("pipe", "tensor"), rule)


def other_core(array):
    return move(array, ("dp",), lambda x, z, y, core: (x, z, y, 1 - core))


def turned(array):
    return move(
        array, ("tensor", "dp"), lambda x, z, y, core: (x, core * 2 + z % 2, y, z // 2)
    )


def pick(array, index, axis=0):
    return lax.dynamic_index_in_dim(array, index, axis, keepdims=False)


def place(buffer, piece, starts):
    return lax.dynamic_update_slice(buffer, piece, starts)


def gather_rows(rows):
    return jnp.concatenate([rows] + [along_x(rows, by) for by in (1, 2, 3)], axis=0)


def scatter_rows(partial):
    parts = partial.astype(bf16).reshape(4, BLOCK, WIDTH)
    total = parts[0].astype(f32)
    for by in (1, 2, 3):
        total = total + along_x(parts[by], -by).astype(f32)
    return total


def dot(left, right, left_dim, right_dim):
    return lax.dot_general(
        left, right, (((left_dim,), (right_dim,)), ((), ())), preferred_element_type=f32
    )


def norm_forward(stream, gain, shift):
    average = jnp.mean(stream, axis=-1, keepdims=True)
    centred = stream - average
    inverse_scale = lax.rsqrt(jnp.mean(centred * centred, axis=-1, keepdims=True) + epsilon)
    standard = centred * inverse_scale
    return (standard * gain + shift).astype(bf16), standard, inverse_scale


def norm_backward(incoming, standard, inverse_scale, gain):
    scaled = incoming * gain
    correction = (
        scaled
        - jnp.mean(scaled, axis=-1, keepdims=True)
        - standard * jnp.mean(scaled * standard, axis=-1, keepdims=True)
    )
    return (
        correction * inverse_scale,
        jnp.sum(incoming * standard, axis=0),
        jnp.sum(incoming, axis=0),
    )


def masked_scores(query, keys, allowed):
    scores = jnp.einsum("qhe,khe->hqk", query, keys, preferred_element_type=f32)
    return jnp.where(allowed[None], scores * HEAD_DIM ** (-0.5), -1e30)


def attend_forward(query, keys, values, allowed):
    scores = masked_scores(query, keys, allowed)
    largest = jnp.max(scores, axis=-1, keepdims=True)
    terms = jnp.exp(scores - largest)
    summed = jnp.sum(terms, axis=-1, keepdims=True)
    weights = (terms / summed).astype(bf16)
    context = jnp.einsum("hqk,khe->qhe", weights, values, preferred_element_type=f32)
    return context.astype(bf16), largest + jnp.log(summed)


def attend_backward(query, keys, values, allowed, log_total, context_grad):
    weights = jnp.exp(masked_scores(query, keys, allowed) - log_total)
    weight_grad = jnp.einsum("qhe,khe->hqk", context_grad, values, preferred_element_type=f32)
    value_grad = jnp.einsum(
        "hqk,qhe->khe", weights.astype(bf16), context_grad, preferred_element_type=f32
    )
    correction = jnp.sum(weights * weight_grad, axis=-1, keepdims=True)
    score_grad = (weights * (weight_grad - correction)).astype(bf16)
    query_grad = jnp.einsum("hqk,khe->qhe", score_grad, keys, preferred_element_type=f32)
    key_grad = jnp.einsum("hqk,qhe->khe", score_grad, query, preferred_element_type=f32)
    scale = HEAD_DIM ** (-0.5)
    return query_grad * scale, key_grad * scale, value_grad


def split_heads(projected):
    view = projected.reshape(4 * BLOCK, 2, 3, 2, HEAD_DIM)
    return tuple(view[:, :, part].reshape(4 * BLOCK, 4, HEAD_DIM) for part in range(3))


def layer_forward(stream, allowed, vectors, weights):
    gain_one, shift_one, out_bias, gain_two, shift_two, proj_bias, qkv_bias, fc_bias = vectors
    w_qkv, w_out, w_fc, w_proj = weights
    normed_one, standard_one, inverse_one = norm_forward(stream, gain_one, shift_one)
    rows_one = gather_rows(normed_one)
    projected = (dot(rows_one, w_qkv, 1, 0) + qkv_bias).astype(bf16)
    query, key, value = split_heads(projected)
    both = jnp.stack([key, value]).reshape(2, 4 * BLOCK, 256)
    keys, values = (
        part.reshape(8 * BLOCK, 4, HEAD_DIM)
        for part in jnp.concatenate([both, other_core(both)], axis=1)
    )
    context, log_total = attend_forward(query, keys, values, allowed)
    context = context.reshape(4 * BLOCK, 256)
    middle = stream + scatter_rows(dot(context, w_out, 1, 0)) + out_bias
    normed_two, standard_two, inverse_two = norm_forward(middle, gain_two, shift_two)
    rows_two = gather_rows(normed_two)
    gelu_input = dot(rows_two, w_fc, 1, 0) + fc_bias
    hidden = jax.nn.gelu(gelu_input, approximate=True).astype(bf16)
    result = middle + scatter_rows(dot(hidden, w_proj, 1, 0)) + proj_bias
    saved = (
        (standard_one, inverse_one, rows_one),
        (query, keys, values, log_total, context),
        (standard_two, inverse_two, rows_two, gelu_input, hidden),
    )
    return result.astype(bf16), saved


def halves(grad, rows):
    return grad.astype(bf16).reshape(2, 2, rows, WIDTH)


def layer_backward(incoming, allowed, vectors, weights, saved, hook):
    gain_one, shift_one, out_bias, gain_two, shift_two, proj_bias, qkv_bias, fc_bias = vectors
    w_qkv, w_out, w_fc, w_proj = weights
    (
        (standard_one, inverse_one, rows_one),
        (query, keys, values, log_total, context),
        (standard_two, inverse_two, rows_two, gelu_input, hidden),
    ) = saved
    grad_feed = incoming.astype(bf16)
    proj_bias_grad = jnp.sum(grad_feed.astype(f32), axis=0)
    feed_rows = hook(0, gather_rows(grad_feed))
    hidden_grad = dot(feed_rows, w_proj, 1, 1)
    gelu_pull = jax.vjp(lambda item: jax.nn.gelu(item, approximate=True), gelu_input)[1]
    gelu_grad = gelu_pull(hidden_grad)[0].astype(bf16)
    normed_two_grad = scatter_rows(dot(gelu_grad, w_fc, 1, 1))
    fc_bias_grad = jnp.sum(gelu_grad.astype(f32), axis=0)
    feed_group = jnp.concatenate(
        [halves(dot(gelu_grad, rows_two, 0, 0), 256), halves(dot(hidden, feed_rows, 0, 0), 256)],
        axis=2,
    )
    normed_two_grad = hook(1, normed_two_grad, feed_group)
    middle_norm, gain_two_grad, shift_two_grad = norm_backward(
        normed_two_grad, standard_two, inverse_two, gain_two
    )
    middle_grad = incoming + middle_norm
    grad_attention = middle_grad.astype(bf16)
    out_bias_grad = jnp.sum(grad_attention.astype(f32), axis=0)
    attention_rows = hook(2, gather_rows(grad_attention))
    context_grad = dot(attention_rows, w_out, 1, 1).astype(bf16)
    w_out_grad = dot(context, attention_rows, 0, 0)
    query_grad, key_grad, value_grad = attend_backward(
        query,
        keys,
        values,
        allowed,
        log_total,
        context_grad.reshape(4 * BLOCK, 4, HEAD_DIM),
    )
    both = jnp.stack([key_grad, value_grad]).reshape(2, 8 * BLOCK, 256)
    arrived = other_core(both[:, 4 * BLOCK :].astype(bf16))
    summed = both[:, : 4 * BLOCK] + arrived.astype(f32)
    triple = jnp.stack([query_grad.reshape(4 * BLOCK, 256), summed[0], summed[1]], axis=1)
    triple = triple.astype(bf16).reshape(4 * BLOCK, 3, 2, 128)
    triple = hook(3, jnp.moveaxis(triple, 2, 1).reshape(4 * BLOCK, 768))
    attention_group = jnp.concatenate(
        [halves(dot(triple, rows_one, 0, 0), 192), halves(w_out_grad, 64)], axis=2
    )
    normed_one_grad = hook(4, scatter_rows(dot(triple, w_qkv, 1, 1)), attention_group)
    qkv_bias_grad = jnp.sum(triple.astype(f32), axis=0)
    stream_norm, gain_one_grad, shift_one_grad = norm_backward(
        normed_one_grad, standard_one, inverse_one, gain_one
    )
    stream_grad = middle_grad + stream_norm
    early = (out_bias_grad, gain_two_grad, shift_two_grad, proj_bias_grad, fc_bias_grad)
    late = (gain_one_grad, shift_one_grad, qkv_bias_grad)
    return stream_grad, early, late


def over_cores(group, core):
    sent = other_core(pick(group, 1 - core, 1))
    mine = (pick(group, core, 1).astype(f32) + sent.astype(f32)).astype(bf16)
    return mine.reshape(2, 4, mine.shape[1] // 4, WIDTH)


def over_y(mine):
    y = lax.axis_index("dp") // 2
    own = pick(mine, y, 1).astype(f32)
    for by in (1, 2, 3):
        own = own + along_y(pick(mine, (y + by) % 4, 1), by).astype(f32)
    return own.astype(bf16)


def over_z(own, layer, pipe, high):
    near, far = pick(own, high), pick(own, 1 - high)
    step = 1 if layer == 1 else -1
    total = jnp.where(pipe == layer, near.astype(f32), 0.0)
    total = total + along_z(near, step, only=1 - layer).astype(f32)
    total = total + along_z(far, -step, only=1 - layer).astype(f32)
    total = total + along_z(far, 2, only=layer).astype(f32)
    return total.astype(bf16)


def back_over_y(own):
    rows = own.shape[0]
    y = lax.axis_index("dp") // 2
    whole = jnp.zeros((4, rows, WIDTH), bf16)
    whole = place(whole, own[None], (y, 0, 0))
    for by in (1, 2, 3):
        whole = place(whole, along_y(own, by)[None], ((y - by) % 4, 0, 0))
    whole = whole.reshape(4 * rows, WIDTH)
    core = lax.axis_index("dp") % 2
    both = jnp.zeros((2, 4 * rows, WIDTH), bf16)
    both = place(both, whole[None], (core, 0, 0))
    return place(both, other_core(whole)[None], (1 - core, 0, 0)).astype(f32)


def everywhere(array, pipe):
    mine, other = pick(array, pipe), pick(array, 1 - pipe)
    total = mine + along_z(other, 1) + along_z(other, 3) + along_z(mine, 2)
    total = total + other_core(total)
    for along in (along_x, along_y):
        total = total + along(total, 1) + along(total, 2) + along(total, 3)
    return total


def held(value, *others):
    return lax.optimization_barrier((value,) + others)[0]


def lay_out(here, copies, sources, shapes):
    def kernel(at_ref, *refs):
        inputs, outputs = refs[: len(sources)], refs[len(sources) : -1]
        semaphores = refs[-1]
        started = []
        for source, start, output, stop in copies(at_ref[0], at_ref[1], at_ref[2]):
            copy = pltpu.make_async_copy(
                inputs[source].at[start], outputs[output].at[stop], semaphores.at[len(started)]
            )
            copy.start()
            started.append(copy)
        for copy in started:
            copy.wait()

    count = len(copies(0, 0, 0))
    whole = pl.BlockSpec(memory_space=pl.ANY)
    return pl.pallas_call(
        kernel,
        out_shape=tuple(jax.ShapeDtypeStruct(shape, bf16) for shape in shapes),
        in_specs=[pl.BlockSpec(memory_space=pltpu.SMEM)] + [whole] * len(sources),
        out_specs=tuple(pl.BlockSpec(memory_space=pltpu.VMEM) for _ in shapes),
        scratch_shapes=[pltpu.SemaphoreType.DMA((count,))],
        compiler_params=pltpu.CompilerParams(vmem_limit_bytes=24 * 1024 * 1024),
    )(jnp.stack(here).astype(jnp.int32), *sources)


def span(start, size, unit=None):
    if unit is not None and not isinstance(start, int):
        start = pl.multiple_of(start, unit)
    return pl.ds(start, size)


ORDER = (1, 3, 2)


def sources_of(pipe, high):
    z = high * 2 + pipe
    return [((z + 4 - by) % 2, (z + 4 - by) % 4 // 2) for by in ORDER]


def spread_weights(here, w_qkv, w_out, w_fc, w_proj, smalls):
    pipe, high, core = here

    def exchanged(group, after):
        group = held(group, *after)
        came = [along_z(group, by) for by in ORDER]
        return came, other_core(jnp.stack(came))

    group = jnp.concatenate([lax.dynamic_slice_in_dim(w_qkv, core * 512, 512, 0), smalls], axis=0)
    came, swapped = exchanged(group, ())

    def copies(pipe, high, core):
        rows = span(0, 512)
        result = [(0, (span(0, 1024),), 0, (pipe, span(0, 1024), span(high * 384, 384, 128)))]
        result.append((1, (span(0, 32),), 1, (pipe, high)))
        for i, (layer, slot) in enumerate(sources_of(pipe, high)):
            columns = span(slot * 384, 384, 128)
            result.append((2 + i, (rows,), 0, (layer, span(core * 512, 512, 512), columns)))
            result.append(
                (5, (i, rows), 0, (layer, span((1 - core) * 512, 512, 512), columns))
            )
            result.append((2 + i, (span(512, 32),), 1, (layer, slot)))
        return result

    all_qkv, all_small = lay_out(
        here, copies, [w_qkv, smalls, *came, swapped], [(2, 1024, 768), (2, 2, 32, 384)]
    )

    half = lax.dynamic_slice_in_dim(w_fc, core * 512, 512, 0)
    group = jnp.concatenate(
        [
            jnp.concatenate([half[:256], half[256:]], axis=1),
            lax.dynamic_slice_in_dim(w_out, core * 64, 64, 0),
        ],
        axis=0,
    )
    came, swapped = exchanged(group, came)

    def copies(pipe, high, core):
        columns = span(0, 1024)
        result = [(0, (span(0, 1024),), 0, (pipe, span(0, 1024), span(high * 512, 512, 512)))]
        result.append((1, (span(0, 128),), 1, (pipe, span(high * 128, 128, 128))))
        for i, (layer, slot) in enumerate(sources_of(pipe, high)):
            for source, lead, number in ((2 + i, (), core), (5, (i,), 1 - core)):
                for part in range(2):
                    result.append(
                        (
                            source,
                            (*lead, span(0, 256), span(part * 512, 512)),
                            0,
                            (
                                layer,
                                span(number * 512 + part * 256, 256, 256),
                                span(slot * 512, 512, 512),
                            ),
                        )
                    )
                result.append(
                    (
                        source,
                        (*lead, span(256, 64)),
                        1,
                        (layer, span(slot * 128 + number * 64, 64, 64)),
                    )
                )
        return result

    all_fc, all_out = lay_out(
        here, copies, [w_fc, w_out, *came, swapped], [(2, 1024, 1024), (2, 256, 1024)]
    )

    group = lax.dynamic_slice_in_dim(w_proj, core * 256, 256, 0)
    came, swapped = exchanged(group, came)

    def copies(pipe, high, core):
        result = [(0, (span(0, 512),), 0, (pipe, span(high * 512, 512, 512)))]
        for i, (layer, slot) in enumerate(sources_of(pipe, high)):
            for source, lead, number in ((1 + i, (), core), (4, (i,), 1 - core)):
                result.append(
                    (
                        source,
                        (*lead, span(0, 256)),
                        0,
                        (layer, span(slot * 512 + number * 256, 256, 256)),
                    )
                )
        return result

    (all_proj,) = lay_out(here, copies, [w_proj, *came, swapped], [(2, 1024, 1024)])
    return all_qkv, all_out, all_fc, all_proj, all_small


def on_device(
    inputs,
    segment_ids,
    cotangent,
    ln1_gain,
    ln1_bias,
    w_qkv,
    qv_bias,
    w_out,
    out_bias,
    ln2_gain,
    ln2_bias,
    w_fc,
    fc_bias,
    w_proj,
    proj_bias,
):
    pipe = lax.axis_index("pipe")
    tensor = lax.axis_index("tensor")
    dp = lax.axis_index("dp")
    x, high, core = tensor // 2, tensor % 2, dp % 2
    here = (pipe, high, core)
    stream = turned(pick(inputs, pipe).reshape(BLOCK, WIDTH)).astype(f32)
    cotangent_rows = turned(pick(cotangent, pipe).reshape(BLOCK, WIDTH)).astype(f32)
    segments = pick(segment_ids, pipe).reshape(8, BLOCK)
    segments = jnp.where(high == core, segments, other_core(segments))
    slots = ((x - jnp.arange(4)) % 4) * 2
    blocks = jnp.concatenate([slots + core, slots + 1 - core])
    numbers = segments[blocks].reshape(-1)
    positions = (blocks[:, None] * BLOCK + jnp.arange(BLOCK)[None]).reshape(-1)
    allowed = (numbers[: 4 * BLOCK, None] == numbers[None]) & (
        positions[None] <= positions[: 4 * BLOCK, None]
    )

    smalls = jnp.concatenate(
        [
            ln1_gain,
            ln1_bias,
            out_bias,
            ln2_gain,
            ln2_bias,
            proj_bias,
            qv_bias.reshape(1, 256),
            fc_bias,
            jnp.zeros((1, 32 * 384 - 6912), bf16),
        ],
        axis=1,
    ).reshape(32, 384)
    all_qkv, all_out, all_fc, all_proj, all_small = spread_weights(
        here, w_qkv[0].reshape(WIDTH, 384), w_out[0], w_fc[0], w_proj[0], smalls
    )
    weights, vectors = [], []
    for layer in range(2):
        weights.append((all_qkv[layer], all_out[layer], all_fc[layer], all_proj[layer]))
        flat = all_small[layer].reshape(2, -1).astype(f32)
        norms = tuple(flat[0, i * WIDTH : (i + 1) * WIDTH] for i in range(6))
        pairs = flat[:, 6144:6400].reshape(2, 2, 128)
        none = jnp.zeros((2, 128), f32)
        qkv_bias = jnp.stack([pairs[:, 0], none, pairs[:, 1]], axis=1).reshape(-1)
        vectors.append(norms + (qkv_bias, flat[:, 6400:6912].reshape(-1)))

    first, saved_first = layer_forward(stream, allowed, vectors[0], weights[0])
    second, saved_second = layer_forward(first.astype(f32), allowed, vectors[1], weights[1])
    waiting = {}

    def keep(step, value, group=None):
        if group is not None:
            waiting[step] = group
        return value

    middle_grad, early_one, late_one = layer_backward(
        cotangent_rows, allowed, vectors[1], weights[1], saved_second, keep
    )
    middle_low = middle_grad.astype(bf16)
    groups_one = (waiting[1], waiting[4])
    kept = {}

    def reduce_along(step, value, group=None):
        if step == 0:
            halved = [over_cores(item, core) for item in groups_one]
            kept["one"] = jnp.concatenate(halved, axis=2)
            return held(value, kept["one"])
        if step == 1:
            kept["one"] = over_y(kept["one"])
            kept["feed"] = over_cores(group, core)
            return held(value, kept["one"])
        if step == 2:
            kept["one"] = over_z(kept["one"], 1, pipe, high)
            return held(value, kept["one"], kept["feed"])
        if step == 3:
            kept["feed"] = over_y(kept["feed"])
            return held(value, kept["feed"])
        kept["feed"] = over_z(kept["feed"], 0, pipe, high)
        kept["attention"] = over_cores(group, core)
        return held(value, kept["feed"], kept["attention"])

    last_grad, early_zero, late_zero = layer_backward(
        middle_low.astype(f32), allowed, vectors[0], weights[0], saved_first, reduce_along
    )
    last_low = last_grad.astype(bf16)
    feed_total = back_over_y(jnp.where(pipe == 1, kept["one"][:128], kept["feed"]))
    attention_owned = over_z(over_y(kept["attention"]), 0, pipe, high)
    attention_total = back_over_y(jnp.where(pipe == 1, kept["one"][128:], attention_owned))

    def bias_rows(fc_bias_grad):
        return place(jnp.zeros((4, WIDTH), f32), fc_bias_grad[None], (x, 0))

    def late_rows(late):
        gain_grad, shift_grad, qkv_grad = late
        parts = qkv_grad.reshape(2, 3, 128)
        pairs = jnp.stack([parts[:, 0], parts[:, 2]]).reshape(2, 256)
        wide = place(jnp.zeros((2, WIDTH), f32), pairs, (0, x * 256))
        return jnp.concatenate([gain_grad[None], shift_grad[None], wide])

    small = jnp.stack(
        [
            jnp.concatenate([jnp.stack(early[:4]), bias_rows(early[4]), late_rows(late)])
            for early, late in ((early_zero, late_zero), (early_one, late_one))
        ]
    )
    small = everywhere(small, pipe)
    early, late = small[:8], small[8:]

    w_fc_grad = feed_total[:, :256].reshape(512, WIDTH).T
    w_proj_grad = feed_total[:, 256:].reshape(512, WIDTH)
    w_qkv_grad = attention_total[:, :192].reshape(384, WIDTH).T.reshape(WIDTH, 3, 128)
    w_out_grad = attention_total[:, 192:].reshape(128, WIDTH)
    fc_bias_grad = lax.dynamic_slice(early[4:], (x, high * 512), (1, 512))[0]
    qv_bias_grad = lax.dynamic_slice(late[2:], (0, tensor * 128), (2, 128))

    def placed(own, other):
        def crossed(array):
            return move(
                array,
                AXES,
                lambda x, z, y, core: (x, core * 2 + 1 - z % 2, y, z // 2),
            )

        stays = turned(own)
        comes = crossed(other)
        return jnp.where(pipe == 0, jnp.stack([stays, comes]), jnp.stack([comes, stays]))

    activations = placed(
        jnp.where(pipe == 0, first, second), jnp.where(pipe == 0, second, first)
    )
    in_grads = placed(
        jnp.where(pipe == 0, last_low, middle_low), jnp.where(pipe == 0, middle_low, last_low)
    )
    return (
        activations[None, :, :, None],
        in_grads[None, :, :, None],
        late[0][None],
        late[1][None],
        w_qkv_grad[None],
        qv_bias_grad[None],
        w_out_grad[None],
        early[0][None],
        early[1][None],
        early[2][None],
        w_fc_grad[None],
        fc_bias_grad[None],
        w_proj_grad[None],
        early[3][None],
    )


def solution(mesh):
    return jax.shard_map(
        on_device,
        mesh=mesh,
        in_specs=(
            P(None, "tensor", "dp", None),
            P(None, "dp", None),
            P(None, "tensor", "dp", None),
            P("pipe", None),
            P("pipe", None),
            P("pipe", None, None, "tensor"),
            P("pipe", None, "tensor"),
            P("pipe", "tensor", None),
            P("pipe", None),
            P("pipe", None),
            P("pipe", None),
            P("pipe", None, "tensor"),
            P("pipe", "tensor"),
            P("pipe", "tensor", None),
            P("pipe", None),
        ),
        out_specs=(
            P("pipe", None, "tensor", "dp", None),
            P("pipe", None, "tensor", "dp", None),
            P("pipe", None),
            P("pipe", None),
            P("pipe", None, None, "tensor"),
            P("pipe", None, "tensor"),
            P("pipe", "tensor", None),
            P("pipe", None),
            P("pipe", None),
            P("pipe", None),
            P("pipe", None, "tensor"),
            P("pipe", "tensor"),
            P("pipe", "tensor", None),
            P("pipe", None),
        ),
        check_vma=False,
    )
```

```python
import jax
import jax.numpy as jnp
from jax import lax
from jax.experimental import pallas as pl
from jax.experimental.pallas import tpu as pltpu
from jax.sharding import PartitionSpec as P

HEAD_DIM = 64
BLOCK = 96
WIDTH = 1024
epsilon = 1e-05
AXES = ("pipe", "tensor", "dp")
bf16 = jnp.bfloat16
f32 = jnp.float32


def spot(axes, x, z, y, core):
    index = 0
    for axis in axes:
        if axis == "pipe":
            index = index * 2 + z % 2
        elif axis == "tensor":
            index = index * 8 + x * 2 + z // 2
        else:
            index = index * 8 + y * 2 + core
    return index


def move(array, axes, rule):
    pairs = {}
    for x in range(4):
        for z in range(4):
            for y in range(4):
                for core in range(2):
                    goal = rule(x, z, y, core)
                    if goal is not None:
                        pairs[spot(axes, x, z, y, core)] = spot(axes, *goal)
    return lax.ppermute(array, axes, sorted(pairs.items()))


def along_x(array, by):
    return move(array, ("tensor",), lambda x, z, y, core: ((x + by) % 4, z, y, core))


def along_y(array, by):
    return move(array, ("dp",), lambda x, z, y, core: (x, z, (y + by) % 4, core))


def along_z(array, by, only=None):
    def rule(x, z, y, core):
        return (x, (z + by) % 4, y, core) if only is None or z % 2 == only else None

    return move(array, ("pipe", "tensor"), rule)


def other_core(array):
    return move(array, ("dp",), lambda x, z, y, core: (x, z, y, 1 - core))


def turned(array):
    return move(
        array, ("tensor", "dp"), lambda x, z, y, core: (x, core * 2 + z % 2, y, z // 2)
    )


def pick(array, index, axis=0):
    return lax.dynamic_index_in_dim(array, index, axis, keepdims=False)


def place(buffer, piece, starts):
    return lax.dynamic_update_slice(buffer, piece, starts)


def gather_rows(rows):
    return jnp.concatenate([rows] + [along_x(rows, by) for by in (1, 2, 3)], axis=0)


def scatter_rows(partial):
    parts = partial.astype(bf16).reshape(4, BLOCK, WIDTH)
    total = parts[0].astype(f32)
    for by in (1, 2, 3):
        total = total + along_x(parts[by], -by).astype(f32)
    return total


def dot(left, right, left_dim, right_dim):
    return lax.dot_general(
        left, right, (((left_dim,), (right_dim,)), ((), ())), preferred_element_type=f32
    )


def norm_forward(stream, gain, shift):
    average = jnp.mean(stream, axis=-1, keepdims=True)
    centred = stream - average
    inverse_scale = lax.rsqrt(jnp.mean(centred * centred, axis=-1, keepdims=True) + epsilon)
    standard = centred * inverse_scale
    return (standard * gain + shift).astype(bf16), standard, inverse_scale


def norm_backward(incoming, standard, inverse_scale, gain):
    scaled = incoming * gain
    correction = (
        scaled
        - jnp.mean(scaled, axis=-1, keepdims=True)
        - standard * jnp.mean(scaled * standard, axis=-1, keepdims=True)
    )
    return (
        correction * inverse_scale,
        jnp.sum(incoming * standard, axis=0),
        jnp.sum(incoming, axis=0),
    )


def masked_scores(query, keys, allowed):
    scores = jnp.einsum("qhe,khe->hqk", query, keys, preferred_element_type=f32)
    return jnp.where(allowed[None], scores * HEAD_DIM ** (-0.5), -1e30)


def attend_forward(query, keys, values, allowed):
    scores = masked_scores(query, keys, allowed)
    largest = jnp.max(scores, axis=-1, keepdims=True)
    terms = jnp.exp(scores - largest)
    summed = jnp.sum(terms, axis=-1, keepdims=True)
    weights = (terms / summed).astype(bf16)
    context = jnp.einsum("hqk,khe->qhe", weights, values, preferred_element_type=f32)
    return context.astype(bf16), largest + jnp.log(summed)


def attend_backward(query, keys, values, allowed, log_total, context_grad):
    weights = jnp.exp(masked_scores(query, keys, allowed) - log_total)
    weight_grad = jnp.einsum("qhe,khe->hqk", context_grad, values, preferred_element_type=f32)
    value_grad = jnp.einsum(
        "hqk,qhe->khe", weights.astype(bf16), context_grad, preferred_element_type=f32
    )
    correction = jnp.sum(weights * weight_grad, axis=-1, keepdims=True)
    score_grad = (weights * (weight_grad - correction)).astype(bf16)
    query_grad = jnp.einsum("hqk,khe->qhe", score_grad, keys, preferred_element_type=f32)
    key_grad = jnp.einsum("hqk,qhe->khe", score_grad, query, preferred_element_type=f32)
    scale = HEAD_DIM ** (-0.5)
    return query_grad * scale, key_grad * scale, value_grad


def split_heads(projected):
    view = projected.reshape(4 * BLOCK, 2, 3, 2, HEAD_DIM)
    return tuple(view[:, :, part].reshape(4 * BLOCK, 4, HEAD_DIM) for part in range(3))


def layer_forward(stream, allowed, vectors, w_qkv, w_out, w_fc_after, w_proj_after):
    gain_one, shift_one, out_bias, gain_two, shift_two, proj_bias, qkv_bias, fc_bias = vectors
    normed_one, standard_one, inverse_one = norm_forward(stream, gain_one, shift_one)
    rows_one = gather_rows(normed_one)
    projected = (dot(rows_one, w_qkv, 1, 0) + qkv_bias).astype(bf16)
    w_fc = w_fc_after(projected)
    query, key, value = split_heads(projected)
    both = jnp.stack([key, value]).reshape(2, 4 * BLOCK, 256)
    keys, values = (
        part.reshape(8 * BLOCK, 4, HEAD_DIM)
        for part in jnp.concatenate([both, other_core(both)], axis=1)
    )
    context, log_total = attend_forward(query, keys, values, allowed)
    context = context.reshape(4 * BLOCK, 256)
    w_proj = w_proj_after(context)
    middle = stream + scatter_rows(dot(context, w_out, 1, 1)) + out_bias
    normed_two, standard_two, inverse_two = norm_forward(middle, gain_two, shift_two)
    rows_two = gather_rows(normed_two)
    gelu_input = dot(rows_two, w_fc, 1, 0) + fc_bias
    hidden = jax.nn.gelu(gelu_input, approximate=True).astype(bf16)
    result = middle + scatter_rows(dot(hidden, w_proj, 1, 0)) + proj_bias
    saved = (
        (standard_one, inverse_one, rows_one),
        (query, keys, values, log_total, context),
        (standard_two, inverse_two, rows_two, gelu_input, hidden),
    )
    return result.astype(bf16), (w_qkv, w_out, w_fc, w_proj), saved


def halves(grad, rows):
    return grad.astype(bf16).reshape(2, 2, rows, WIDTH)


def layer_backward(incoming, allowed, vectors, weights, saved, hook):
    gain_one, shift_one, out_bias, gain_two, shift_two, proj_bias, qkv_bias, fc_bias = vectors
    w_qkv, w_out, w_fc, w_proj = weights
    (
        (standard_one, inverse_one, rows_one),
        (query, keys, values, log_total, context),
        (standard_two, inverse_two, rows_two, gelu_input, hidden),
    ) = saved
    grad_feed = incoming.astype(bf16)
    proj_bias_grad = jnp.sum(grad_feed.astype(f32), axis=0)
    feed_rows = hook(0, gather_rows(grad_feed))
    hidden_grad = dot(feed_rows, w_proj, 1, 1)
    gelu_pull = jax.vjp(lambda item: jax.nn.gelu(item, approximate=True), gelu_input)[1]
    gelu_grad = gelu_pull(hidden_grad)[0].astype(bf16)
    normed_two_grad = scatter_rows(dot(gelu_grad, w_fc, 1, 1))
    fc_bias_grad = jnp.sum(gelu_grad.astype(f32), axis=0)
    feed_group = jnp.concatenate(
        [halves(dot(gelu_grad, rows_two, 0, 0), 256), halves(dot(hidden, feed_rows, 0, 0), 256)],
        axis=2,
    )
    normed_two_grad = hook(1, normed_two_grad, feed_group)
    middle_norm, gain_two_grad, shift_two_grad = norm_backward(
        normed_two_grad, standard_two, inverse_two, gain_two
    )
    middle_grad = incoming + middle_norm
    grad_attention = middle_grad.astype(bf16)
    out_bias_grad = jnp.sum(grad_attention.astype(f32), axis=0)
    attention_rows = hook(2, gather_rows(grad_attention))
    context_grad = dot(attention_rows, w_out, 1, 0).astype(bf16)
    w_out_grad = dot(context, attention_rows, 0, 0)
    query_grad, key_grad, value_grad = attend_backward(
        query,
        keys,
        values,
        allowed,
        log_total,
        context_grad.reshape(4 * BLOCK, 4, HEAD_DIM),
    )
    both = jnp.stack([key_grad, value_grad]).reshape(2, 8 * BLOCK, 256)
    arrived = other_core(both[:, 4 * BLOCK :].astype(bf16))
    summed = both[:, : 4 * BLOCK] + arrived.astype(f32)
    triple = jnp.stack([query_grad.reshape(4 * BLOCK, 256), summed[0], summed[1]], axis=1)
    triple = triple.astype(bf16).reshape(4 * BLOCK, 3, 2, 128)
    triple = hook(3, jnp.moveaxis(triple, 2, 1).reshape(4 * BLOCK, 768))
    attention_group = jnp.concatenate(
        [halves(dot(triple, rows_one, 0, 0), 192), halves(w_out_grad, 64)], axis=2
    )
    normed_one_grad = hook(4, scatter_rows(dot(triple, w_qkv, 1, 1)), attention_group)
    qkv_bias_grad = jnp.sum(triple.astype(f32), axis=0)
    stream_norm, gain_one_grad, shift_one_grad = norm_backward(
        normed_one_grad, standard_one, inverse_one, gain_one
    )
    stream_grad = middle_grad + stream_norm
    early = (out_bias_grad, gain_two_grad, shift_two_grad, proj_bias_grad, fc_bias_grad)
    late = (gain_one_grad, shift_one_grad, qkv_bias_grad)
    return stream_grad, early, late


def over_cores(group, core):
    sent = other_core(pick(group, 1 - core, 1))
    mine = (pick(group, core, 1).astype(f32) + sent.astype(f32)).astype(bf16)
    return mine.reshape(2, 4, mine.shape[1] // 4, WIDTH)


def over_y(mine):
    y = lax.axis_index("dp") // 2
    own = pick(mine, y, 1).astype(f32)
    for by in (1, 2, 3):
        own = own + along_y(pick(mine, (y + by) % 4, 1), by).astype(f32)
    return own.astype(bf16)


def over_z(own, layer, pipe, high):
    near, far = pick(own, high), pick(own, 1 - high)
    step = 1 if layer == 1 else -1
    total = jnp.where(pipe == layer, near.astype(f32), 0.0)
    total = total + along_z(near, step, only=1 - layer).astype(f32)
    total = total + along_z(far, -step, only=1 - layer).astype(f32)
    total = total + along_z(far, 2, only=layer).astype(f32)
    return total.astype(bf16)


def back_over_y(own):
    rows = own.shape[0]
    y = lax.axis_index("dp") // 2
    whole = jnp.zeros((4, rows, WIDTH), bf16)
    whole = place(whole, own[None], (y, 0, 0))
    for by in (1, 2, 3):
        whole = place(whole, along_y(own, by)[None], ((y - by) % 4, 0, 0))
    whole = whole.reshape(4 * rows, WIDTH)
    core = lax.axis_index("dp") % 2
    both = jnp.zeros((2, 4 * rows, WIDTH), bf16)
    both = place(both, whole[None], (core, 0, 0))
    both = place(both, other_core(whole)[None], (1 - core, 0, 0))
    return both.reshape(2, 4, rows, WIDTH)


def everywhere(array, pipe):
    mine, other = pick(array, pipe), pick(array, 1 - pipe)
    total = mine + along_z(other, 1) + along_z(other, 3) + along_z(mine, 2)
    total = total + other_core(total)
    for along in (along_x, along_y):
        total = total + along(total, 1) + along(total, 2) + along(total, 3)
    return total


def held(value, *others):
    return lax.optimization_barrier((value,) + others)[0]


def lay_out(here, copies, sources, shapes):
    def kernel(at_ref, *refs):
        inputs, outputs = refs[: len(sources)], refs[len(sources) : -1]
        semaphores = refs[-1]
        started = []
        for source, start, output, stop in copies(at_ref[0], at_ref[1], at_ref[2]):
            copy = pltpu.make_async_copy(
                inputs[source].at[start], outputs[output].at[stop], semaphores.at[len(started)]
            )
            copy.start()
            started.append(copy)
        for copy in started:
            copy.wait()

    count = len(copies(0, 0, 0))
    whole = pl.BlockSpec(memory_space=pl.ANY)
    return pl.pallas_call(
        kernel,
        out_shape=tuple(jax.ShapeDtypeStruct(shape, bf16) for shape in shapes),
        in_specs=[pl.BlockSpec(memory_space=pltpu.SMEM)] + [whole] * len(sources),
        out_specs=tuple(pl.BlockSpec(memory_space=pltpu.VMEM) for _ in shapes),
        scratch_shapes=[pltpu.SemaphoreType.DMA((count,))],
        compiler_params=pltpu.CompilerParams(vmem_limit_bytes=24 * 1024 * 1024),
    )(jnp.stack(here).astype(jnp.int32), *sources)


def span(start, size, unit=None):
    if unit is not None and not isinstance(start, int):
        start = pl.multiple_of(start, unit)
    return pl.ds(start, size)


ORDER = (1, 3, 2)


def sources_of(pipe, high):
    z = high * 2 + pipe
    return [((z + 4 - by) % 2, (z + 4 - by) % 4 // 2) for by in ORDER]


def exchanged(group, after):
    group = held(group, *after)
    return [along_z(group, by) for by in ORDER]


def spread_first(here, w_qkv, w_out, smalls):
    core = here[2]
    turned_out = w_out.T
    group = jnp.concatenate(
        [
            lax.dynamic_slice_in_dim(w_qkv, core * 512, 512, 0),
            lax.dynamic_slice_in_dim(turned_out, core * 512, 512, 0),
        ],
        axis=1,
    )
    came = exchanged(jnp.concatenate([group, smalls], axis=0), ())
    swapped = [other_core(item) for item in came]

    def copies(pipe, high, core):
        rows = span(0, 1024)
        result = [(0, (rows,), 0, (pipe, rows, span(high * 384, 384, 128)))]
        result.append((1, (rows,), 1, (pipe, rows, span(high * 128, 128, 128))))
        result.append((2, (span(0, 16),), 2, (pipe, high)))
        rows = span(0, 512)
        for i, (layer, slot) in enumerate(sources_of(pipe, high)):
            for source, half in ((3 + i, core), (6 + i, 1 - core)):
                goal = span(half * 512, 512, 512)
                result.append(
                    (source, (rows, span(0, 384)), 0, (layer, goal, span(slot * 384, 384, 128)))
                )
                result.append(
                    (source, (rows, span(384, 128)), 1, (layer, goal, span(slot * 128, 128, 128)))
                )
            result.append((3 + i, (span(512, 16),), 2, (layer, slot)))
        return result

    arrays = lay_out(
        here,
        copies,
        [w_qkv, turned_out, smalls, *came, *swapped],
        [(2, 1024, 768), (2, 1024, 256), (2, 2, 16, 512)],
    )
    return arrays, swapped


def spread_fc(here, w_fc, came, after):
    came = list(lax.optimization_barrier((*came, after)))[:3]
    swapped = [other_core(item) for item in came]

    def copies(pipe, high, core):
        rows = span(0, 1024)
        result = [(0, (rows,), 0, (pipe, rows, span(high * 512, 512, 512)))]
        for i, (layer, slot) in enumerate(sources_of(pipe, high)):
            for source, half in ((1 + i, core), (4 + i, 1 - core)):
                goal = (layer, span(half * 512, 512, 512), span(slot * 512, 512, 512))
                result.append((source, (span(0, 512),), 0, goal))
        return result

    (array,) = lay_out(here, copies, [w_fc, *came, *swapped], [(2, 1024, 1024)])
    return array


def spread_proj(here, w_proj, came):
    swapped = [other_core(item) for item in came]

    def copies(pipe, high, core):
        result = [(0, (span(0, 512),), 0, (pipe, span(high * 512, 512, 512)))]
        for i, (layer, slot) in enumerate(sources_of(pipe, high)):
            for source, half in ((1 + i, core), (4 + i, 1 - core)):
                goal = (layer, span(slot * 512 + half * 256, 256, 256))
                result.append((source, (span(0, 256),), 0, goal))
        return result

    (array,) = lay_out(here, copies, [w_proj, *came, *swapped], [(2, 1024, 1024)])
    return array


def on_device(
    inputs,
    segment_ids,
    cotangent,
    ln1_gain,
    ln1_bias,
    w_qkv,
    qv_bias,
    w_out,
    out_bias,
    ln2_gain,
    ln2_bias,
    w_fc,
    fc_bias,
    w_proj,
    proj_bias,
):
    pipe = lax.axis_index("pipe")
    tensor = lax.axis_index("tensor")
    dp = lax.axis_index("dp")
    x, high, core = tensor // 2, tensor % 2, dp % 2
    here = (pipe, high, core)
    stream = turned(pick(inputs, pipe).reshape(BLOCK, WIDTH)).astype(f32)
    cotangent_rows = turned(pick(cotangent, pipe).reshape(BLOCK, WIDTH)).astype(f32)
    segments = pick(segment_ids, pipe).reshape(8, BLOCK)
    segments = jnp.where(high == core, segments, other_core(segments))
    slots = ((x - jnp.arange(4)) % 4) * 2
    blocks = jnp.concatenate([slots + core, slots + 1 - core])
    numbers = segments[blocks].reshape(-1)
    positions = (blocks[:, None] * BLOCK + jnp.arange(BLOCK)[None]).reshape(-1)
    allowed = (numbers[: 4 * BLOCK, None] == numbers[None]) & (
        positions[None] <= positions[: 4 * BLOCK, None]
    )

    smalls = jnp.concatenate(
        [
            ln1_gain,
            ln1_bias,
            out_bias,
            ln2_gain,
            ln2_bias,
            proj_bias,
            qv_bias.reshape(1, 256),
            fc_bias,
            jnp.zeros((1, 16 * 512 - 6912), bf16),
        ],
        axis=1,
    ).reshape(16, 512)
    (all_qkv, all_out, all_small), swapped = spread_first(
        here, w_qkv[0].reshape(WIDTH, 384), w_out[0], smalls
    )
    half_fc = lax.dynamic_slice_in_dim(w_fc[0], core * 512, 512, 0)
    came_fc = exchanged(half_fc, swapped)
    laid = {}

    def fc_after(projected):
        laid["fc"] = spread_fc(here, w_fc[0], came_fc, projected)
        return laid["fc"][0]

    def proj_after(context):
        half = lax.dynamic_slice_in_dim(w_proj[0], core * 256, 256, 0)
        came = exchanged(half, (context, *came_fc))
        laid["proj"] = spread_proj(here, w_proj[0], came)
        return laid["proj"][0]

    vectors = []
    for layer in range(2):
        flat = all_small[layer].reshape(2, -1).astype(f32)
        norms = tuple(flat[0, i * WIDTH : (i + 1) * WIDTH] for i in range(6))
        pairs = flat[:, 6144:6400].reshape(2, 2, 128)
        none = jnp.zeros((2, 128), f32)
        qkv_bias = jnp.stack([pairs[:, 0], none, pairs[:, 1]], axis=1).reshape(-1)
        vectors.append(norms + (qkv_bias, flat[:, 6400:6912].reshape(-1)))

    first, weights_first, saved_first = layer_forward(
        stream, allowed, vectors[0], all_qkv[0], all_out[0], fc_after, proj_after
    )
    second, weights_second, saved_second = layer_forward(
        first.astype(f32),
        allowed,
        vectors[1],
        all_qkv[1],
        all_out[1],
        lambda after: laid["fc"][1],
        lambda after: laid["proj"][1],
    )
    waiting = {}

    def keep(step, value, group=None):
        if group is not None:
            waiting[step] = group
        return value

    middle_grad, early_one, late_one = layer_backward(
        cotangent_rows, allowed, vectors[1], weights_second, saved_second, keep
    )
    middle_low = middle_grad.astype(bf16)
    groups_one = (waiting[1], waiting[4])
    kept = {}

    def reduce_along(step, value, group=None):
        if step == 0:
            halved = [over_cores(item, core) for item in groups_one]
            kept["one"] = jnp.concatenate(halved, axis=2)
            return held(value, kept["one"])
        if step == 1:
            kept["one"] = over_y(kept["one"])
            kept["feed"] = over_cores(group, core)
            return held(value, kept["one"])
        if step == 2:
            kept["one"] = over_z(kept["one"], 1, pipe, high)
            return held(value, kept["one"], kept["feed"])
        if step == 3:
            return value
        kept["feed"] = over_y(kept["feed"])
        kept["attention"] = over_cores(group, core)
        return held(value, kept["feed"], kept["attention"])

    last_grad, early_zero, late_zero = layer_backward(
        middle_low.astype(f32), allowed, vectors[0], weights_first, saved_first, reduce_along
    )
    last_low = last_grad.astype(bf16)
    zero = jnp.concatenate([kept["feed"], over_y(kept["attention"])], axis=1)
    zero = over_z(zero, 0, pipe, high)
    total = back_over_y(jnp.where(pipe == 1, kept["one"], zero))

    def bias_rows(fc_bias_grad):
        return place(jnp.zeros((4, WIDTH), f32), fc_bias_grad[None], (x, 0))

    def late_rows(late):
        gain_grad, shift_grad, qkv_grad = late
        parts = qkv_grad.reshape(2, 3, 128)
        pairs = jnp.stack([parts[:, 0], parts[:, 2]]).reshape(2, 256)
        wide = place(jnp.zeros((2, WIDTH), f32), pairs, (0, x * 256))
        return jnp.concatenate([gain_grad[None], shift_grad[None], wide])

    small = jnp.stack(
        [
            jnp.concatenate([jnp.stack(early[:4]), bias_rows(early[4]), late_rows(late)])
            for early, late in ((early_zero, late_zero), (early_one, late_one))
        ]
    )
    small = everywhere(small, pipe)
    early, late = small[:8], small[8:]

    feed_total = total[:, :, :128].reshape(2, 512, WIDTH)
    attention_total = total[:, :, 128:].reshape(2, 256, WIDTH)
    w_fc_grad = feed_total[:, :256].reshape(512, WIDTH).T.astype(f32)
    w_proj_grad = feed_total[:, 256:].reshape(512, WIDTH).astype(f32)
    w_qkv_grad = attention_total[:, :192].reshape(384, WIDTH).T.reshape(WIDTH, 3, 128).astype(f32)
    w_out_grad = attention_total[:, 192:].reshape(128, WIDTH).astype(f32)
    fc_bias_grad = lax.dynamic_slice(early[4:], (x, high * 512), (1, 512))[0]
    qv_bias_grad = lax.dynamic_slice(late[2:], (0, tensor * 128), (2, 128))

    def placed(own, other):
        def crossed(array):
            return move(
                array,
                AXES,
                lambda x, z, y, core: (x, core * 2 + 1 - z % 2, y, z // 2),
            )

        stays = turned(own)
        comes = crossed(other)
        return jnp.where(pipe == 0, jnp.stack([stays, comes]), jnp.stack([comes, stays]))

    activations = placed(
        jnp.where(pipe == 0, first, second), jnp.where(pipe == 0, second, first)
    )
    in_grads = placed(
        jnp.where(pipe == 0, last_low, middle_low), jnp.where(pipe == 0, middle_low, last_low)
    )
    return (
        activations[None, :, :, None],
        in_grads[None, :, :, None],
        late[0][None],
        late[1][None],
        w_qkv_grad[None],
        qv_bias_grad[None],
        w_out_grad[None],
        early[0][None],
        early[1][None],
        early[2][None],
        w_fc_grad[None],
        fc_bias_grad[None],
        w_proj_grad[None],
        early[3][None],
    )


def solution(mesh):
    return jax.shard_map(
        on_device,
        mesh=mesh,
        in_specs=(
            P(None, "tensor", "dp", None),
            P(None, "dp", None),
            P(None, "tensor", "dp", None),
            P("pipe", None),
            P("pipe", None),
            P("pipe", None, None, "tensor"),
            P("pipe", None, "tensor"),
            P("pipe", "tensor", None),
            P("pipe", None),
            P("pipe", None),
            P("pipe", None),
            P("pipe", None, "tensor"),
            P("pipe", "tensor"),
            P("pipe", "tensor", None),
            P("pipe", None),
        ),
        out_specs=(
            P("pipe", None, "tensor", "dp", None),
            P("pipe", None, "tensor", "dp", None),
            P("pipe", None),
            P("pipe", None),
            P("pipe", None, None, "tensor"),
            P("pipe", None, "tensor"),
            P("pipe", "tensor", None),
            P("pipe", None),
            P("pipe", None),
            P("pipe", None),
            P("pipe", None, "tensor"),
            P("pipe", "tensor"),
            P("pipe", "tensor", None),
            P("pipe", None),
        ),
        check_vma=False,
    )
```

```python
import jax
import jax.numpy as jnp
from jax import lax
from jax.experimental import pallas as pl
from jax.experimental.pallas import tpu as pltpu
from jax.sharding import PartitionSpec as P

HEAD_DIM = 64
BLOCK = 96
WIDTH = 1024
epsilon = 1e-05
AXES = ("pipe", "tensor", "dp")
bf16 = jnp.bfloat16
f32 = jnp.float32


def spot(axes, x, z, y, core):
    index = 0
    for axis in axes:
        if axis == "pipe":
            index = index * 2 + z % 2
        elif axis == "tensor":
            index = index * 8 + x * 2 + z // 2
        else:
            index = index * 8 + y * 2 + core
    return index


def move(array, axes, rule):
    pairs = {}
    for x in range(4):
        for z in range(4):
            for y in range(4):
                for core in range(2):
                    goal = rule(x, z, y, core)
                    if goal is not None:
                        pairs[spot(axes, x, z, y, core)] = spot(axes, *goal)
    return lax.ppermute(array, axes, sorted(pairs.items()))


def along_x(array, by):
    return move(array, ("tensor",), lambda x, z, y, core: ((x + by) % 4, z, y, core))


def along_y(array, by):
    return move(array, ("dp",), lambda x, z, y, core: (x, z, (y + by) % 4, core))


def along_z(array, by, only=None):
    def rule(x, z, y, core):
        return (x, (z + by) % 4, y, core) if only is None or z % 2 == only else None

    return move(array, ("pipe", "tensor"), rule)


def other_core(array):
    return move(array, ("dp",), lambda x, z, y, core: (x, z, y, 1 - core))


def turned(array):
    return move(
        array, ("tensor", "dp"), lambda x, z, y, core: (x, core * 2 + z % 2, y, z // 2)
    )


def pick(array, index, axis=0):
    return lax.dynamic_index_in_dim(array, index, axis, keepdims=False)


def place(buffer, piece, starts):
    return lax.dynamic_update_slice(buffer, piece, starts)


def gather_rows(rows):
    return jnp.concatenate([rows] + [along_x(rows, by) for by in (1, 2, 3)], axis=0)


def scatter_rows(partial):
    parts = partial.astype(bf16).reshape(4, BLOCK, WIDTH)
    total = parts[0].astype(f32)
    for by in (1, 2, 3):
        total = total + along_x(parts[by], -by).astype(f32)
    return total


def dot(left, right, left_dim, right_dim):
    return lax.dot_general(
        left, right, (((left_dim,), (right_dim,)), ((), ())), preferred_element_type=f32
    )


def norm_forward(stream, gain, shift):
    average = jnp.mean(stream, axis=-1, keepdims=True)
    centred = stream - average
    inverse_scale = lax.rsqrt(jnp.mean(centred * centred, axis=-1, keepdims=True) + epsilon)
    standard = centred * inverse_scale
    return (standard * gain + shift).astype(bf16), standard, inverse_scale


def norm_backward(incoming, standard, inverse_scale, gain):
    scaled = incoming * gain
    correction = (
        scaled
        - jnp.mean(scaled, axis=-1, keepdims=True)
        - standard * jnp.mean(scaled * standard, axis=-1, keepdims=True)
    )
    return (
        correction * inverse_scale,
        jnp.sum(incoming * standard, axis=0),
        jnp.sum(incoming, axis=0),
    )


def masked_scores(query, keys, allowed):
    scores = jnp.einsum("qhe,khe->hqk", query, keys, preferred_element_type=f32)
    return jnp.where(allowed[None], scores * HEAD_DIM ** (-0.5), -1e30)


def attend_forward(query, keys, values, allowed):
    scores = masked_scores(query, keys, allowed)
    largest = jnp.max(scores, axis=-1, keepdims=True)
    terms = jnp.exp(scores - largest)
    summed = jnp.sum(terms, axis=-1, keepdims=True)
    weights = (terms / summed).astype(bf16)
    context = jnp.einsum("hqk,khe->qhe", weights, values, preferred_element_type=f32)
    return context.astype(bf16), largest + jnp.log(summed)


def attend_backward(query, keys, values, allowed, log_total, context_grad):
    weights = jnp.exp(masked_scores(query, keys, allowed) - log_total)
    weight_grad = jnp.einsum("qhe,khe->hqk", context_grad, values, preferred_element_type=f32)
    value_grad = jnp.einsum(
        "hqk,qhe->khe", weights.astype(bf16), context_grad, preferred_element_type=f32
    )
    correction = jnp.sum(weights * weight_grad, axis=-1, keepdims=True)
    score_grad = (weights * (weight_grad - correction)).astype(bf16)
    query_grad = jnp.einsum("hqk,khe->qhe", score_grad, keys, preferred_element_type=f32)
    key_grad = jnp.einsum("hqk,qhe->khe", score_grad, query, preferred_element_type=f32)
    scale = HEAD_DIM ** (-0.5)
    return query_grad * scale, key_grad * scale, value_grad


def split_heads(projected):
    view = projected.reshape(4 * BLOCK, 2, 3, 2, HEAD_DIM)
    return tuple(view[:, :, part].reshape(4 * BLOCK, 4, HEAD_DIM) for part in range(3))


def layer_forward(stream, allowed, vectors, w_qkv, w_out, hook):
    gain_one, shift_one, out_bias, gain_two, shift_two, proj_bias, qkv_bias, fc_bias = vectors
    normed_one, standard_one, inverse_one = norm_forward(stream, gain_one, shift_one)
    rows_one = gather_rows(normed_one)
    projected = (dot(rows_one, w_qkv, 1, 0) + qkv_bias).astype(bf16)
    query, key, value = split_heads(projected)
    both = jnp.stack([key, value]).reshape(2, 4 * BLOCK, 256)
    arrived = hook(0, other_core(both))
    keys, values = (
        part.reshape(8 * BLOCK, 4, HEAD_DIM)
        for part in jnp.concatenate([both, arrived], axis=1)
    )
    context, log_total = attend_forward(query, keys, values, allowed)
    context = context.reshape(4 * BLOCK, 256)
    context = hook(1, context)
    middle = stream + hook(2, scatter_rows(dot(context, w_out, 1, 1))) + out_bias
    normed_two, standard_two, inverse_two = norm_forward(middle, gain_two, shift_two)
    rows_two, w_fc, w_proj = hook(3, gather_rows(normed_two))
    gelu_input = dot(rows_two, w_fc, 1, 0) + fc_bias
    hidden = jax.nn.gelu(gelu_input, approximate=True).astype(bf16)
    result = middle + scatter_rows(dot(hidden, w_proj, 1, 0)) + proj_bias
    saved = (
        (standard_one, inverse_one, rows_one),
        (query, keys, values, log_total, context),
        (standard_two, inverse_two, rows_two, gelu_input, hidden),
    )
    return result.astype(bf16), (w_qkv, w_out, w_fc, w_proj), saved


def halves(grad, rows):
    return grad.astype(bf16).reshape(2, 2, rows, WIDTH)


def layer_backward(incoming, allowed, vectors, weights, saved, hook):
    gain_one, shift_one, out_bias, gain_two, shift_two, proj_bias, qkv_bias, fc_bias = vectors
    w_qkv, w_out, w_fc, w_proj = weights
    (
        (standard_one, inverse_one, rows_one),
        (query, keys, values, log_total, context),
        (standard_two, inverse_two, rows_two, gelu_input, hidden),
    ) = saved
    grad_feed = incoming.astype(bf16)
    proj_bias_grad = jnp.sum(grad_feed.astype(f32), axis=0)
    feed_rows = hook(0, gather_rows(grad_feed))
    hidden_grad = dot(feed_rows, w_proj, 1, 1)
    gelu_pull = jax.vjp(lambda item: jax.nn.gelu(item, approximate=True), gelu_input)[1]
    gelu_grad = gelu_pull(hidden_grad)[0].astype(bf16)
    normed_two_grad = scatter_rows(dot(gelu_grad, w_fc, 1, 1))
    fc_bias_grad = jnp.sum(gelu_grad.astype(f32), axis=0)
    feed_group = jnp.concatenate(
        [halves(dot(gelu_grad, rows_two, 0, 0), 256), halves(dot(hidden, feed_rows, 0, 0), 256)],
        axis=2,
    )
    normed_two_grad = hook(1, normed_two_grad, feed_group)
    middle_norm, gain_two_grad, shift_two_grad = norm_backward(
        normed_two_grad, standard_two, inverse_two, gain_two
    )
    middle_grad = incoming + middle_norm
    grad_attention = middle_grad.astype(bf16)
    out_bias_grad = jnp.sum(grad_attention.astype(f32), axis=0)
    attention_rows = hook(2, gather_rows(grad_attention))
    context_grad = dot(attention_rows, w_out, 1, 0).astype(bf16)
    w_out_grad = dot(context, attention_rows, 0, 0)
    query_grad, key_grad, value_grad = attend_backward(
        query,
        keys,
        values,
        allowed,
        log_total,
        context_grad.reshape(4 * BLOCK, 4, HEAD_DIM),
    )
    both = jnp.stack([key_grad, value_grad]).reshape(2, 8 * BLOCK, 256)
    arrived = other_core(both[:, 4 * BLOCK :].astype(bf16))
    summed = both[:, : 4 * BLOCK] + arrived.astype(f32)
    triple = jnp.stack([query_grad.reshape(4 * BLOCK, 256), summed[0], summed[1]], axis=1)
    triple = triple.astype(bf16).reshape(4 * BLOCK, 3, 2, 128)
    triple = hook(3, jnp.moveaxis(triple, 2, 1).reshape(4 * BLOCK, 768))
    attention_group = jnp.concatenate(
        [halves(dot(triple, rows_one, 0, 0), 192), halves(w_out_grad, 64)], axis=2
    )
    normed_one_grad = hook(4, scatter_rows(dot(triple, w_qkv, 1, 1)), attention_group)
    qkv_bias_grad = jnp.sum(triple.astype(f32), axis=0)
    stream_norm, gain_one_grad, shift_one_grad = norm_backward(
        normed_one_grad, standard_one, inverse_one, gain_one
    )
    stream_grad = middle_grad + stream_norm
    early = (out_bias_grad, gain_two_grad, shift_two_grad, proj_bias_grad, fc_bias_grad)
    late = (gain_one_grad, shift_one_grad, qkv_bias_grad)
    return stream_grad, early, late


def over_cores(group, core):
    sent = other_core(pick(group, 1 - core, 1))
    mine = (pick(group, core, 1).astype(f32) + sent.astype(f32)).astype(bf16)
    return mine.reshape(2, 4, mine.shape[1] // 4, WIDTH)


def near_y(mine):
    y = lax.axis_index("dp") // 2
    own = pick(mine, y, 1).astype(f32)
    for by in (1, 3):
        own = own + along_y(pick(mine, (y + by) % 4, 1), by).astype(f32)
    return own


def far_y(mine, own):
    y = lax.axis_index("dp") // 2
    sent = held(pick(mine, (y + 2) % 4, 1), own)
    return (own + along_y(sent, 2).astype(f32)).astype(bf16)


def over_z(own, layer, pipe, high):
    near, far = pick(own, high), pick(own, 1 - high)
    step = 1 if layer == 1 else -1
    total = jnp.where(pipe == layer, near.astype(f32), 0.0)
    total = total + along_z(near, step, only=1 - layer).astype(f32)
    total = total + along_z(far, -step, only=1 - layer).astype(f32)
    total = total + along_z(far, 2, only=layer).astype(f32)
    return total.astype(bf16)


def back_over_y(own):
    rows = own.shape[0]
    y = lax.axis_index("dp") // 2
    whole = jnp.zeros((4, rows, WIDTH), bf16)
    whole = place(whole, own[None], (y, 0, 0))
    for by in (1, 2, 3):
        whole = place(whole, along_y(own, by)[None], ((y - by) % 4, 0, 0))
    whole = whole.reshape(4 * rows, WIDTH)
    core = lax.axis_index("dp") % 2
    both = jnp.zeros((2, 4 * rows, WIDTH), bf16)
    both = place(both, whole[None], (core, 0, 0))
    both = place(both, other_core(whole)[None], (1 - core, 0, 0))
    return both.reshape(2, 4, rows, WIDTH)


def everywhere(array, pipe):
    mine, other = pick(array, pipe), pick(array, 1 - pipe)
    total = mine + along_z(other, 1) + along_z(other, 3) + along_z(mine, 2)
    total = total + other_core(total)
    for along in (along_x, along_y):
        total = total + along(total, 1) + along(total, 2) + along(total, 3)
    return total


def held(value, *others):
    return lax.optimization_barrier((value,) + others)[0]


def lay_out(here, copies, sources, shapes):
    def kernel(at_ref, *refs):
        inputs, outputs = refs[: len(sources)], refs[len(sources) : -1]
        semaphores = refs[-1]
        started = []
        for source, start, output, stop in copies(at_ref[0], at_ref[1], at_ref[2]):
            copy = pltpu.make_async_copy(
                inputs[source].at[start], outputs[output].at[stop], semaphores.at[len(started)]
            )
            copy.start()
            started.append(copy)
        for copy in started:
            copy.wait()

    count = len(copies(0, 0, 0))
    whole = pl.BlockSpec(memory_space=pl.ANY)
    return pl.pallas_call(
        kernel,
        out_shape=tuple(jax.ShapeDtypeStruct(shape, bf16) for shape in shapes),
        in_specs=[pl.BlockSpec(memory_space=pltpu.SMEM)] + [whole] * len(sources),
        out_specs=tuple(pl.BlockSpec(memory_space=pltpu.VMEM) for _ in shapes),
        scratch_shapes=[pltpu.SemaphoreType.DMA((count,))],
        compiler_params=pltpu.CompilerParams(vmem_limit_bytes=24 * 1024 * 1024),
    )(jnp.stack(here).astype(jnp.int32), *sources)


def span(start, size, unit=None):
    if unit is not None and not isinstance(start, int):
        start = pl.multiple_of(start, unit)
    return pl.ds(start, size)


ORDER = (1, 3, 2)


def sources_of(pipe, high):
    z = high * 2 + pipe
    return [((z + 4 - by) % 2, (z + 4 - by) % 4 // 2) for by in ORDER]


def spread_first(here, w_qkv, w_out, smalls):
    core = here[2]
    turned_out = w_out.T
    group = jnp.concatenate(
        [
            lax.dynamic_slice_in_dim(w_qkv, core * 512, 512, 0),
            lax.dynamic_slice_in_dim(turned_out, core * 512, 512, 0),
        ],
        axis=1,
    )
    group = jnp.concatenate([group, smalls], axis=0)
    came = [along_z(group, by) for by in ORDER]
    swapped = [other_core(item) for item in came]

    def copies(pipe, high, core):
        rows = span(0, 1024)
        result = [(0, (rows,), 0, (pipe, rows, span(high * 384, 384, 128)))]
        result.append((1, (rows,), 1, (pipe, rows, span(high * 128, 128, 128))))
        result.append((2, (span(0, 16),), 2, (pipe, high)))
        rows = span(0, 512)
        for i, (layer, slot) in enumerate(sources_of(pipe, high)):
            for source, half in ((3 + i, core), (6 + i, 1 - core)):
                goal = span(half * 512, 512, 512)
                result.append(
                    (source, (rows, span(0, 384)), 0, (layer, goal, span(slot * 384, 384, 128)))
                )
                result.append(
                    (source, (rows, span(384, 128)), 1, (layer, goal, span(slot * 128, 128, 128)))
                )
            result.append((3 + i, (span(512, 16),), 2, (layer, slot)))
        return result

    arrays = lay_out(
        here,
        copies,
        [w_qkv, turned_out, smalls, *came, *swapped],
        [(2, 1024, 768), (2, 1024, 256), (2, 2, 16, 512)],
    )
    return arrays, swapped


def lay_fc(here, w_fc, came):
    swapped = other_core(jnp.stack(came))

    def copies(pipe, high, core):
        rows = span(0, 1024)
        result = [(0, (rows,), 0, (pipe, rows, span(high * 512, 512, 512)))]
        for i, (layer, slot) in enumerate(sources_of(pipe, high)):
            for source, lead, half in ((1 + i, (), core), (4, (i,), 1 - core)):
                goal = (layer, span(half * 512, 512, 512), span(slot * 512, 512, 512))
                result.append((source, (*lead, span(0, 512)), 0, goal))
        return result

    (array,) = lay_out(here, copies, [w_fc, *came, swapped], [(2, 1024, 1024)])
    return array


def lay_proj(here, w_proj, came):
    swapped = other_core(jnp.stack(came))

    def copies(pipe, high, core):
        result = [(0, (span(0, 512),), 0, (pipe, span(high * 512, 512, 512)))]
        for i, (layer, slot) in enumerate(sources_of(pipe, high)):
            for source, lead, half in ((1 + i, (), core), (4, (i,), 1 - core)):
                goal = (layer, span(slot * 512 + half * 256, 256, 256))
                result.append((source, (*lead, span(0, 256)), 0, goal))
        return result

    (array,) = lay_out(here, copies, [w_proj, *came, swapped], [(2, 1024, 1024)])
    return array


def on_device(
    inputs,
    segment_ids,
    cotangent,
    ln1_gain,
    ln1_bias,
    w_qkv,
    qv_bias,
    w_out,
    out_bias,
    ln2_gain,
    ln2_bias,
    w_fc,
    fc_bias,
    w_proj,
    proj_bias,
):
    pipe = lax.axis_index("pipe")
    tensor = lax.axis_index("tensor")
    dp = lax.axis_index("dp")
    x, high, core = tensor // 2, tensor % 2, dp % 2
    here = (pipe, high, core)
    stream = turned(pick(inputs, pipe).reshape(BLOCK, WIDTH)).astype(f32)
    cotangent_rows = turned(pick(cotangent, pipe).reshape(BLOCK, WIDTH)).astype(f32)
    segments = pick(segment_ids, pipe).reshape(8, BLOCK)
    segments = jnp.where(high == core, segments, other_core(segments))
    slots = ((x - jnp.arange(4)) % 4) * 2
    blocks = jnp.concatenate([slots + core, slots + 1 - core])
    numbers = segments[blocks].reshape(-1)
    positions = (blocks[:, None] * BLOCK + jnp.arange(BLOCK)[None]).reshape(-1)
    allowed = (numbers[: 4 * BLOCK, None] == numbers[None]) & (
        positions[None] <= positions[: 4 * BLOCK, None]
    )

    smalls = jnp.concatenate(
        [
            ln1_gain,
            ln1_bias,
            out_bias,
            ln2_gain,
            ln2_bias,
            proj_bias,
            qv_bias.reshape(1, 256),
            fc_bias,
            jnp.zeros((1, 16 * 512 - 6912), bf16),
        ],
        axis=1,
    ).reshape(16, 512)
    (all_qkv, all_out, all_small), swapped = spread_first(
        here, w_qkv[0].reshape(WIDTH, 384), w_out[0], smalls
    )
    half_fc = lax.dynamic_slice_in_dim(w_fc[0], core * 512, 512, 0)
    half_proj = lax.dynamic_slice_in_dim(w_proj[0], core * 256, 256, 0)
    coming, laid = {}, {}

    def first_hook(step, value):
        if step == 0:
            sent = held(half_fc, *swapped)
            coming["fc"] = [along_z(sent, by) for by in ORDER[:2]]
            return held(value, *coming["fc"])
        if step == 1:
            coming["fc"].append(along_z(held(half_fc, *coming["fc"]), ORDER[2]))
            return held(value, *coming["fc"])
        if step == 2:
            laid["fc"] = lay_fc(here, w_fc[0], coming["fc"])
            sent = held(half_proj, *coming["fc"])
            coming["proj"] = [along_z(sent, by) for by in ORDER[:2]]
            return held(value, *coming["proj"])
        coming["proj"].append(along_z(held(half_proj, *coming["proj"]), ORDER[2]))
        laid["proj"] = lay_proj(here, w_proj[0], coming["proj"])
        return held(value, coming["proj"][2]), laid["fc"][0], laid["proj"][0]

    def second_hook(step, value):
        return value if step < 3 else (value, laid["fc"][1], laid["proj"][1])

    vectors = []
    for layer in range(2):
        flat = all_small[layer].reshape(2, -1).astype(f32)
        norms = tuple(flat[0, i * WIDTH : (i + 1) * WIDTH] for i in range(6))
        pairs = flat[:, 6144:6400].reshape(2, 2, 128)
        none = jnp.zeros((2, 128), f32)
        qkv_bias = jnp.stack([pairs[:, 0], none, pairs[:, 1]], axis=1).reshape(-1)
        vectors.append(norms + (qkv_bias, flat[:, 6400:6912].reshape(-1)))

    first, weights_first, saved_first = layer_forward(
        stream, allowed, vectors[0], all_qkv[0], all_out[0], first_hook
    )
    second, weights_second, saved_second = layer_forward(
        first.astype(f32),
        allowed,
        vectors[1],
        all_qkv[1],
        all_out[1],
        second_hook,
    )
    waiting = {}

    def keep(step, value, group=None):
        if group is not None:
            waiting[step] = group
        return value

    middle_grad, early_one, late_one = layer_backward(
        cotangent_rows, allowed, vectors[1], weights_second, saved_second, keep
    )
    middle_low = middle_grad.astype(bf16)
    groups_one = (waiting[1], waiting[4])
    kept = {}

    def reduce_along(step, value, group=None):
        if step == 0:
            halved = [over_cores(item, core) for item in groups_one]
            kept["one"] = jnp.concatenate(halved, axis=2)
            return held(value, kept["one"])
        if step == 1:
            kept["near"] = near_y(kept["one"])
            kept["feed"] = group
            return value
        if step == 2:
            return held(value, kept["near"])
        if step == 3:
            kept["one"] = far_y(kept["one"], kept["near"])
            kept["feed"] = over_cores(kept["feed"], core)
            return held(value, kept["one"], kept["feed"])
        kept["near"] = near_y(kept["feed"])
        kept["attention"] = over_cores(group, core)
        return held(value, kept["near"], kept["attention"])

    last_grad, early_zero, late_zero = layer_backward(
        middle_low.astype(f32), allowed, vectors[0], weights_first, saved_first, reduce_along
    )
    last_low = last_grad.astype(bf16)
    one = over_z(kept["one"], 1, pipe, high)
    feed = far_y(kept["feed"], kept["near"])
    attention = far_y(kept["attention"], near_y(kept["attention"]))
    zero = over_z(jnp.concatenate([feed, attention], axis=1), 0, pipe, high)
    total = back_over_y(jnp.where(pipe == 1, one, zero))

    def bias_rows(fc_bias_grad):
        return place(jnp.zeros((4, WIDTH), f32), fc_bias_grad[None], (x, 0))

    def late_rows(late):
        gain_grad, shift_grad, qkv_grad = late
        parts = qkv_grad.reshape(2, 3, 128)
        pairs = jnp.stack([parts[:, 0], parts[:, 2]]).reshape(2, 256)
        wide = place(jnp.zeros((2, WIDTH), f32), pairs, (0, x * 256))
        return jnp.concatenate([gain_grad[None], shift_grad[None], wide])

    small = jnp.stack(
        [
            jnp.concatenate([jnp.stack(early[:4]), bias_rows(early[4]), late_rows(late)])
            for early, late in ((early_zero, late_zero), (early_one, late_one))
        ]
    )
    small = everywhere(small, pipe)
    early, late = small[:8], small[8:]

    feed_total = total[:, :, :128].reshape(2, 512, WIDTH)
    attention_total = total[:, :, 128:].reshape(2, 256, WIDTH)
    w_fc_grad = feed_total[:, :256].reshape(512, WIDTH).T.astype(f32)
    w_proj_grad = feed_total[:, 256:].reshape(512, WIDTH).astype(f32)
    w_qkv_grad = attention_total[:, :192].reshape(384, WIDTH).T.reshape(WIDTH, 3, 128).astype(f32)
    w_out_grad = attention_total[:, 192:].reshape(128, WIDTH).astype(f32)
    fc_bias_grad = lax.dynamic_slice(early[4:], (x, high * 512), (1, 512))[0]
    qv_bias_grad = lax.dynamic_slice(late[2:], (0, tensor * 128), (2, 128))

    def placed(own, other):
        def crossed(array):
            return move(
                array,
                AXES,
                lambda x, z, y, core: (x, core * 2 + 1 - z % 2, y, z // 2),
            )

        stays = turned(own)
        comes = crossed(other)
        return jnp.where(pipe == 0, jnp.stack([stays, comes]), jnp.stack([comes, stays]))

    activations = placed(
        jnp.where(pipe == 0, first, second), jnp.where(pipe == 0, second, first)
    )
    in_grads = placed(
        jnp.where(pipe == 0, last_low, middle_low), jnp.where(pipe == 0, middle_low, last_low)
    )
    return (
        activations[None, :, :, None],
        in_grads[None, :, :, None],
        late[0][None],
        late[1][None],
        w_qkv_grad[None],
        qv_bias_grad[None],
        w_out_grad[None],
        early[0][None],
        early[1][None],
        early[2][None],
        w_fc_grad[None],
        fc_bias_grad[None],
        w_proj_grad[None],
        early[3][None],
    )


def solution(mesh):
    return jax.shard_map(
        on_device,
        mesh=mesh,
        in_specs=(
            P(None, "tensor", "dp", None),
            P(None, "dp", None),
            P(None, "tensor", "dp", None),
            P("pipe", None),
            P("pipe", None),
            P("pipe", None, None, "tensor"),
            P("pipe", None, "tensor"),
            P("pipe", "tensor", None),
            P("pipe", None),
            P("pipe", None),
            P("pipe", None),
            P("pipe", None, "tensor"),
            P("pipe", "tensor"),
            P("pipe", "tensor", None),
            P("pipe", None),
        ),
        out_specs=(
            P("pipe", None, "tensor", "dp", None),
            P("pipe", None, "tensor", "dp", None),
            P("pipe", None),
            P("pipe", None),
            P("pipe", None, None, "tensor"),
            P("pipe", None, "tensor"),
            P("pipe", "tensor", None),
            P("pipe", None),
            P("pipe", None),
            P("pipe", None),
            P("pipe", None, "tensor"),
            P("pipe", "tensor"),
            P("pipe", "tensor", None),
            P("pipe", None),
        ),
        check_vma=False,
    )
```

```python
import jax
import jax.numpy as jnp
from jax import lax
from jax.experimental import pallas as pl
from jax.experimental.pallas import tpu as pltpu
from jax.sharding import PartitionSpec as P

HEAD_DIM = 64
BLOCK = 96
WIDTH = 1024
epsilon = 1e-05
AXES = ("pipe", "tensor", "dp")
bf16 = jnp.bfloat16
f32 = jnp.float32


def spot(axes, x, z, y, core):
    index = 0
    for axis in axes:
        if axis == "pipe":
            index = index * 2 + z % 2
        elif axis == "tensor":
            index = index * 8 + x * 2 + z // 2
        else:
            index = index * 8 + y * 2 + core
    return index


def move(array, axes, rule):
    pairs = {}
    for x in range(4):
        for z in range(4):
            for y in range(4):
                for core in range(2):
                    goal = rule(x, z, y, core)
                    if goal is not None:
                        pairs[spot(axes, x, z, y, core)] = spot(axes, *goal)
    return lax.ppermute(array, axes, sorted(pairs.items()))


def along_x(array, by):
    return move(array, ("tensor",), lambda x, z, y, core: ((x + by) % 4, z, y, core))


def along_y(array, by):
    return move(array, ("dp",), lambda x, z, y, core: (x, z, (y + by) % 4, core))


def along_z(array, by, only=None):
    def rule(x, z, y, core):
        return (x, (z + by) % 4, y, core) if only is None or z % 2 == only else None

    return move(array, ("pipe", "tensor"), rule)


def other_core(array):
    return move(array, ("dp",), lambda x, z, y, core: (x, z, y, 1 - core))


def turned(array):
    return move(
        array, ("tensor", "dp"), lambda x, z, y, core: (x, core * 2 + z % 2, y, z // 2)
    )


def pick(array, index, axis=0):
    return lax.dynamic_index_in_dim(array, index, axis, keepdims=False)


def place(buffer, piece, starts):
    return lax.dynamic_update_slice(buffer, piece, starts)


def gather_rows(rows):
    return jnp.concatenate([rows] + [along_x(rows, by) for by in (1, 2, 3)], axis=0)


def scatter_rows(partial):
    parts = partial.astype(bf16).reshape(4, BLOCK, WIDTH)
    total = parts[0].astype(f32)
    for by in (1, 2, 3):
        total = total + along_x(parts[by], -by).astype(f32)
    return total


def dot(left, right, left_dim, right_dim):
    return lax.dot_general(
        left, right, (((left_dim,), (right_dim,)), ((), ())), preferred_element_type=f32
    )


def norm_forward(stream, gain, shift):
    average = jnp.mean(stream, axis=-1, keepdims=True)
    centred = stream - average
    inverse_scale = lax.rsqrt(jnp.mean(centred * centred, axis=-1, keepdims=True) + epsilon)
    standard = centred * inverse_scale
    return (standard * gain + shift).astype(bf16), standard, inverse_scale


def norm_backward(incoming, standard, inverse_scale, gain):
    scaled = incoming * gain
    correction = (
        scaled
        - jnp.mean(scaled, axis=-1, keepdims=True)
        - standard * jnp.mean(scaled * standard, axis=-1, keepdims=True)
    )
    return (
        correction * inverse_scale,
        jnp.sum(incoming * standard, axis=0),
        jnp.sum(incoming, axis=0),
    )


def masked_scores(query, keys, allowed):
    scores = jnp.einsum("qhe,khe->hqk", query, keys, preferred_element_type=f32)
    return jnp.where(allowed[None], scores * HEAD_DIM ** (-0.5), -1e30)


def attend_forward(query, keys, values, allowed):
    scores = masked_scores(query, keys, allowed)
    largest = jnp.max(scores, axis=-1, keepdims=True)
    terms = jnp.exp(scores - largest)
    summed = jnp.sum(terms, axis=-1, keepdims=True)
    weights = (terms / summed).astype(bf16)
    context = jnp.einsum("hqk,khe->qhe", weights, values, preferred_element_type=f32)
    return context.astype(bf16), largest + jnp.log(summed)


def attend_backward(query, keys, values, allowed, log_total, context_grad):
    weights = jnp.exp(masked_scores(query, keys, allowed) - log_total)
    weight_grad = jnp.einsum("qhe,khe->hqk", context_grad, values, preferred_element_type=f32)
    value_grad = jnp.einsum(
        "hqk,qhe->khe", weights.astype(bf16), context_grad, preferred_element_type=f32
    )
    correction = jnp.sum(weights * weight_grad, axis=-1, keepdims=True)
    score_grad = (weights * (weight_grad - correction)).astype(bf16)
    query_grad = jnp.einsum("hqk,khe->qhe", score_grad, keys, preferred_element_type=f32)
    key_grad = jnp.einsum("hqk,qhe->khe", score_grad, query, preferred_element_type=f32)
    scale = HEAD_DIM ** (-0.5)
    return query_grad * scale, key_grad * scale, value_grad


def split_heads(projected):
    view = projected.reshape(4 * BLOCK, 2, 3, 2, HEAD_DIM)
    return tuple(view[:, :, part].reshape(4 * BLOCK, 4, HEAD_DIM) for part in range(3))


def layer_forward(stream, allowed, vectors, hook):
    gain_one, shift_one, out_bias, gain_two, shift_two, proj_bias = vectors
    normed_one, standard_one, inverse_one = norm_forward(stream, gain_one, shift_one)
    rows_one, w_qkv, w_out, qkv_bias, fc_bias = hook(-1, gather_rows(normed_one))
    projected = (dot(rows_one, w_qkv, 1, 0) + qkv_bias).astype(bf16)
    query, key, value = split_heads(projected)
    both = jnp.stack([key, value]).reshape(2, 4 * BLOCK, 256)
    arrived = hook(0, other_core(both))
    keys, values = (
        part.reshape(8 * BLOCK, 4, HEAD_DIM)
        for part in jnp.concatenate([both, arrived], axis=1)
    )
    context, log_total = attend_forward(query, keys, values, allowed)
    context = context.reshape(4 * BLOCK, 256)
    context = hook(1, context)
    middle = stream + hook(2, scatter_rows(dot(context, w_out, 1, 1))) + out_bias
    normed_two, standard_two, inverse_two = norm_forward(middle, gain_two, shift_two)
    rows_two, w_fc, w_proj = hook(3, gather_rows(normed_two))
    gelu_input = dot(rows_two, w_fc, 1, 0) + fc_bias
    hidden = jax.nn.gelu(gelu_input, approximate=True).astype(bf16)
    result = middle + scatter_rows(dot(hidden, w_proj, 1, 0)) + proj_bias
    saved = (
        (standard_one, inverse_one, rows_one),
        (query, keys, values, log_total, context),
        (standard_two, inverse_two, rows_two, gelu_input, hidden),
    )
    return result.astype(bf16), (w_qkv, w_out, w_fc, w_proj), saved


def halves(grad, rows):
    return grad.astype(bf16).reshape(2, 2, rows, WIDTH)


def layer_backward(incoming, allowed, vectors, weights, saved, hook):
    gain_one, shift_one, out_bias, gain_two, shift_two, proj_bias = vectors
    w_qkv, w_out, w_fc, w_proj = weights
    (
        (standard_one, inverse_one, rows_one),
        (query, keys, values, log_total, context),
        (standard_two, inverse_two, rows_two, gelu_input, hidden),
    ) = saved
    grad_feed = incoming.astype(bf16)
    proj_bias_grad = jnp.sum(grad_feed.astype(f32), axis=0)
    feed_rows = hook(0, gather_rows(grad_feed))
    hidden_grad = dot(feed_rows, w_proj, 1, 1)
    gelu_pull = jax.vjp(lambda item: jax.nn.gelu(item, approximate=True), gelu_input)[1]
    gelu_grad = gelu_pull(hidden_grad)[0].astype(bf16)
    normed_two_grad = scatter_rows(dot(gelu_grad, w_fc, 1, 1))
    fc_bias_grad = jnp.sum(gelu_grad.astype(f32), axis=0)
    feed_group = jnp.concatenate(
        [halves(dot(gelu_grad, rows_two, 0, 0), 256), halves(dot(hidden, feed_rows, 0, 0), 256)],
        axis=2,
    )
    normed_two_grad = hook(1, normed_two_grad, feed_group)
    middle_norm, gain_two_grad, shift_two_grad = norm_backward(
        normed_two_grad, standard_two, inverse_two, gain_two
    )
    middle_grad = incoming + middle_norm
    grad_attention = middle_grad.astype(bf16)
    out_bias_grad = jnp.sum(grad_attention.astype(f32), axis=0)
    attention_rows = hook(2, gather_rows(grad_attention))
    context_grad = dot(attention_rows, w_out, 1, 0).astype(bf16)
    w_out_grad = dot(context, attention_rows, 0, 0)
    query_grad, key_grad, value_grad = attend_backward(
        query,
        keys,
        values,
        allowed,
        log_total,
        context_grad.reshape(4 * BLOCK, 4, HEAD_DIM),
    )
    both = jnp.stack([key_grad, value_grad]).reshape(2, 8 * BLOCK, 256)
    arrived = other_core(both[:, 4 * BLOCK :].astype(bf16))
    summed = both[:, : 4 * BLOCK] + arrived.astype(f32)
    triple = jnp.stack([query_grad.reshape(4 * BLOCK, 256), summed[0], summed[1]], axis=1)
    triple = triple.astype(bf16).reshape(4 * BLOCK, 3, 2, 128)
    triple = hook(3, jnp.moveaxis(triple, 2, 1).reshape(4 * BLOCK, 768))
    attention_group = jnp.concatenate(
        [halves(dot(triple, rows_one, 0, 0), 192), halves(w_out_grad, 64)], axis=2
    )
    normed_one_grad = hook(4, scatter_rows(dot(triple, w_qkv, 1, 1)), attention_group)
    qkv_bias_grad = jnp.sum(triple.astype(f32), axis=0)
    stream_norm, gain_one_grad, shift_one_grad = norm_backward(
        normed_one_grad, standard_one, inverse_one, gain_one
    )
    stream_grad = middle_grad + stream_norm
    early = (out_bias_grad, gain_two_grad, shift_two_grad, proj_bias_grad, fc_bias_grad)
    late = (gain_one_grad, shift_one_grad, qkv_bias_grad)
    return stream_grad, early, late


def over_cores(group, core):
    sent = other_core(pick(group, 1 - core, 1))
    mine = (pick(group, core, 1).astype(f32) + sent.astype(f32)).astype(bf16)
    return mine.reshape(2, 4, mine.shape[1] // 4, WIDTH)


def near_y(mine):
    y = lax.axis_index("dp") // 2
    own = pick(mine, y, 1).astype(f32)
    for by in (1, 3):
        own = own + along_y(pick(mine, (y + by) % 4, 1), by).astype(f32)
    return own


def far_y(mine, own):
    y = lax.axis_index("dp") // 2
    sent, own = tied(pick(mine, (y + 2) % 4, 1), own)
    return (own + along_y(sent, 2).astype(f32)).astype(bf16)


def over_z(zero, one, pipe, high):
    zero_near, zero_far = pick(zero, high), pick(zero, 1 - high)
    one_near, one_far = pick(one, high), pick(one, 1 - high)
    even = pipe == 0
    total = jnp.where(even, zero_near, one_near).astype(f32)
    total = total + along_z(jnp.where(even, one_near, zero_far), 1).astype(f32)
    total = total + along_z(jnp.where(even, one_far, zero_near), -1).astype(f32)
    total = total + along_z(jnp.where(even, zero_far, one_far), 2).astype(f32)
    return total.astype(bf16)


def back_over_y(own):
    rows = own.shape[0]
    y = lax.axis_index("dp") // 2
    whole = jnp.zeros((4, rows, WIDTH), bf16)
    whole = place(whole, own[None], (y, 0, 0))
    for by in (1, 2, 3):
        whole = place(whole, along_y(own, by)[None], ((y - by) % 4, 0, 0))
    whole = whole.reshape(4 * rows, WIDTH)
    core = lax.axis_index("dp") % 2
    both = jnp.zeros((2, 4 * rows, WIDTH), bf16)
    both = place(both, whole[None], (core, 0, 0))
    both = place(both, other_core(whole)[None], (1 - core, 0, 0))
    return both.reshape(2, 4, rows, WIDTH)


def everywhere(array, pipe):
    mine, other = pick(array, pipe), pick(array, 1 - pipe)
    total = mine + along_z(other, 1) + along_z(other, 3) + along_z(mine, 2)
    total = total + other_core(total)
    for along in (along_x, along_y):
        total = total + along(total, 1) + along(total, 2) + along(total, 3)
    return total


def tied(*arrays):
    return lax.optimization_barrier(arrays)


def lay_out(here, copies, sources, shapes):
    def kernel(at_ref, *refs):
        inputs, outputs = refs[: len(sources)], refs[len(sources) : -1]
        semaphores = refs[-1]
        started = []
        for source, start, output, stop in copies(at_ref[0], at_ref[1], at_ref[2]):
            copy = pltpu.make_async_copy(
                inputs[source].at[start], outputs[output].at[stop], semaphores.at[len(started)]
            )
            copy.start()
            started.append(copy)
        for copy in started:
            copy.wait()

    count = len(copies(0, 0, 0))
    whole = pl.BlockSpec(memory_space=pl.ANY)
    return pl.pallas_call(
        kernel,
        out_shape=tuple(jax.ShapeDtypeStruct(shape, bf16) for shape in shapes),
        in_specs=[pl.BlockSpec(memory_space=pltpu.SMEM)] + [whole] * len(sources),
        out_specs=tuple(pl.BlockSpec(memory_space=pltpu.VMEM) for _ in shapes),
        scratch_shapes=[pltpu.SemaphoreType.DMA((count,))],
        compiler_params=pltpu.CompilerParams(vmem_limit_bytes=24 * 1024 * 1024),
    )(jnp.stack(here).astype(jnp.int32), *sources)


def span(start, size, unit=None):
    if unit is not None and not isinstance(start, int):
        start = pl.multiple_of(start, unit)
    return pl.ds(start, size)


ORDER = (1, 3, 2)


def sources_of(pipe, high):
    z = high * 2 + pipe
    return [((z + 4 - by) % 2, (z + 4 - by) % 4 // 2) for by in ORDER]


def send_first(core, w_qkv, turned_out, smalls):
    group = jnp.concatenate(
        [
            lax.dynamic_slice_in_dim(w_qkv, core * 512, 512, 0),
            lax.dynamic_slice_in_dim(turned_out, core * 512, 512, 0),
        ],
        axis=1,
    )
    group = jnp.concatenate([group, smalls], axis=0)
    came = [along_z(group, by) for by in ORDER[:2]]
    group, *came = tied(group, *came)
    return came + [along_z(group, ORDER[2])]


def lay_first(here, w_qkv, turned_out, smalls, came, after):
    swapped = [other_core(item) for item in came[:2]]
    last, after = tied(came[2], after)
    came = came[:2] + [last]
    swapped.append(other_core(last))

    def copies(pipe, high, core):
        rows = span(0, 1024)
        result = [(0, (rows,), 0, (pipe, rows, span(high * 384, 384, 128)))]
        result.append((1, (rows,), 1, (pipe, rows, span(high * 128, 128, 128))))
        result.append((2, (span(0, 16),), 2, (pipe, high)))
        rows = span(0, 512)
        for i, (layer, slot) in enumerate(sources_of(pipe, high)):
            for source, half in ((3 + i, core), (6 + i, 1 - core)):
                goal = span(half * 512, 512, 512)
                result.append(
                    (source, (rows, span(0, 384)), 0, (layer, goal, span(slot * 384, 384, 128)))
                )
                result.append(
                    (source, (rows, span(384, 128)), 1, (layer, goal, span(slot * 128, 128, 128)))
                )
            result.append((3 + i, (span(512, 16),), 2, (layer, slot)))
        return result

    arrays = lay_out(
        here,
        copies,
        [w_qkv, turned_out, smalls, *came, *swapped],
        [(2, 1024, 768), (2, 1024, 256), (2, 2, 16, 512)],
    )
    return arrays, after


def lay_fc(here, w_fc, came):
    swapped = other_core(jnp.stack(came))

    def copies(pipe, high, core):
        rows = span(0, 1024)
        result = [(0, (rows,), 0, (pipe, rows, span(high * 512, 512, 512)))]
        for i, (layer, slot) in enumerate(sources_of(pipe, high)):
            for source, lead, half in ((1 + i, (), core), (4, (i,), 1 - core)):
                goal = (layer, span(half * 512, 512, 512), span(slot * 512, 512, 512))
                result.append((source, (*lead, span(0, 512)), 0, goal))
        return result

    (array,) = lay_out(here, copies, [w_fc, *came, swapped], [(2, 1024, 1024)])
    return array


def lay_proj(here, w_proj, came):
    swapped = other_core(jnp.stack(came))

    def copies(pipe, high, core):
        result = [(0, (span(0, 512),), 0, (pipe, span(high * 512, 512, 512)))]
        for i, (layer, slot) in enumerate(sources_of(pipe, high)):
            for source, lead, half in ((1 + i, (), core), (4, (i,), 1 - core)):
                goal = (layer, span(slot * 512 + half * 256, 256, 256))
                result.append((source, (*lead, span(0, 256)), 0, goal))
        return result

    (array,) = lay_out(here, copies, [w_proj, *came, swapped], [(2, 1024, 1024)])
    return array


def on_device(
    inputs,
    segment_ids,
    cotangent,
    ln1_gain,
    ln1_bias,
    w_qkv,
    qv_bias,
    w_out,
    out_bias,
    ln2_gain,
    ln2_bias,
    w_fc,
    fc_bias,
    w_proj,
    proj_bias,
):
    pipe = lax.axis_index("pipe")
    tensor = lax.axis_index("tensor")
    dp = lax.axis_index("dp")
    x, high, core = tensor // 2, tensor % 2, dp % 2
    here = (pipe, high, core)
    stream = turned(pick(inputs, pipe).reshape(BLOCK, WIDTH)).astype(f32)
    cotangent_rows = turned(pick(cotangent, pipe).reshape(BLOCK, WIDTH)).astype(f32)
    segments = pick(segment_ids, pipe).reshape(8, BLOCK)
    segments = jnp.where(high == core, segments, other_core(segments))
    slots = ((x - jnp.arange(4)) % 4) * 2
    blocks = jnp.concatenate([slots + core, slots + 1 - core])
    numbers = segments[blocks].reshape(-1)
    positions = (blocks[:, None] * BLOCK + jnp.arange(BLOCK)[None]).reshape(-1)
    allowed = (numbers[: 4 * BLOCK, None] == numbers[None]) & (
        positions[None] <= positions[: 4 * BLOCK, None]
    )

    smalls = jnp.concatenate(
        [
            ln1_gain,
            ln1_bias,
            out_bias,
            ln2_gain,
            ln2_bias,
            proj_bias,
            qv_bias.reshape(1, 256),
            fc_bias,
            jnp.zeros((1, 16 * 512 - 6912), bf16),
        ],
        axis=1,
    ).reshape(16, 512)
    before = along_z(smalls, 1)
    flat_w_qkv, turned_out = w_qkv[0].reshape(WIDTH, 384), w_out[0].T
    came_first = send_first(core, flat_w_qkv, turned_out, smalls)
    half_fc = lax.dynamic_slice_in_dim(w_fc[0], core * 512, 512, 0)
    half_proj = lax.dynamic_slice_in_dim(w_proj[0], core * 256, 256, 0)
    coming, laid = {}, {}

    def biases(all_small, layer):
        flat = all_small[layer].reshape(2, -1).astype(f32)
        pairs = flat[:, 6144:6400].reshape(2, 2, 128)
        none = jnp.zeros((2, 128), f32)
        qkv_bias = jnp.stack([pairs[:, 0], none, pairs[:, 1]], axis=1).reshape(-1)
        return qkv_bias, flat[:, 6400:6912].reshape(-1)

    def first_hook(step, value):
        if step == -1:
            laid["first"], value = lay_first(
                here, flat_w_qkv, turned_out, smalls, came_first, value
            )
            return second_hook(step, value, 0)
        if step == 0:
            sent, *laid["first"] = tied(half_fc, *laid["first"])
            value, *coming["fc"] = tied(value, *[along_z(sent, by) for by in ORDER[:2]])
            return value
        if step == 1:
            sent, *came = tied(half_fc, *coming["fc"])
            value, *coming["fc"] = tied(value, *came, along_z(sent, ORDER[2]))
            return value
        if step == 2:
            sent, *coming["fc"] = tied(half_proj, *coming["fc"])
            laid["fc"] = lay_fc(here, w_fc[0], coming["fc"])
            value, *coming["proj"] = tied(value, *[along_z(sent, by) for by in ORDER[:2]])
            return value
        sent, *came = tied(half_proj, *coming["proj"])
        value, last = tied(value, along_z(sent, ORDER[2]))
        laid["proj"] = lay_proj(here, w_proj[0], came + [last])
        return value, laid["fc"][0], laid["proj"][0]

    def second_hook(step, value, layer=1):
        if step == -1:
            all_qkv, all_out, all_small = laid["first"]
            return (value, all_qkv[layer], all_out[layer]) + biases(all_small, layer)
        return value if step < 3 else (value, laid["fc"][1], laid["proj"][1])

    vectors = []
    for layer in range(2):
        flat = jnp.where(pipe == layer, smalls, before).astype(f32).reshape(-1)
        vectors.append(tuple(flat[i * WIDTH : (i + 1) * WIDTH] for i in range(6)))

    first, weights_first, saved_first = layer_forward(
        stream, allowed, vectors[0], first_hook
    )
    second, weights_second, saved_second = layer_forward(
        first.astype(f32),
        allowed,
        vectors[1],
        second_hook,
    )
    waiting = {}

    def keep(step, value, group=None):
        if group is not None:
            waiting[step] = group
        return value

    middle_grad, early_one, late_one = layer_backward(
        cotangent_rows, allowed, vectors[1], weights_second, saved_second, keep
    )
    middle_low = middle_grad.astype(bf16)
    groups_one = (waiting[1], waiting[4])
    kept = {}

    def reduce_along(step, value, group=None):
        if step == 0:
            halved = [over_cores(item, core) for item in groups_one]
            value, kept["one"] = tied(value, jnp.concatenate(halved, axis=2))
            return value
        if step == 1:
            kept["near"] = near_y(kept["one"])
            kept["feed"] = group
            return value
        if step == 2:
            value, kept["near"] = tied(value, kept["near"])
            return value
        if step == 3:
            kept["one"] = far_y(kept["one"], kept["near"])
            value, kept["feed"] = tied(value, over_cores(kept["feed"], core))
            return value
        near, attention = near_y(kept["feed"]), over_cores(group, core)
        value, *rest = tied(value, kept["one"], near, attention)
        kept["one"], kept["near"], kept["attention"] = rest
        return value

    last_grad, early_zero, late_zero = layer_backward(
        middle_low.astype(f32), allowed, vectors[0], weights_first, saved_first, reduce_along
    )
    last_low = last_grad.astype(bf16)
    y = dp // 2
    near = jnp.concatenate([kept["near"], near_y(kept["attention"])], axis=1)
    far = [pick(kept[name], (y + 2) % 4, 1) for name in ("feed", "attention")]
    zero = near + along_y(jnp.concatenate(far, axis=1), 2).astype(f32)
    total = back_over_y(over_z(zero.astype(bf16), kept["one"], pipe, high))

    def bias_rows(fc_bias_grad):
        return place(jnp.zeros((4, WIDTH), f32), fc_bias_grad[None], (x, 0))

    def late_rows(late):
        gain_grad, shift_grad, qkv_grad = late
        parts = qkv_grad.reshape(2, 3, 128)
        pairs = jnp.stack([parts[:, 0], parts[:, 2]]).reshape(2, 256)
        wide = place(jnp.zeros((2, WIDTH), f32), pairs, (0, x * 256))
        return jnp.concatenate([gain_grad[None], shift_grad[None], wide])

    small = jnp.stack(
        [
            jnp.concatenate([jnp.stack(early[:4]), bias_rows(early[4]), late_rows(late)])
            for early, late in ((early_zero, late_zero), (early_one, late_one))
        ]
    )
    small = everywhere(small, pipe)
    early, late = small[:8], small[8:]

    feed_total = total[:, :, :128].reshape(2, 512, WIDTH)
    attention_total = total[:, :, 128:].reshape(2, 256, WIDTH)
    w_fc_grad = feed_total[:, :256].reshape(512, WIDTH).T.astype(f32)
    w_proj_grad = feed_total[:, 256:].reshape(512, WIDTH).astype(f32)
    w_qkv_grad = attention_total[:, :192].reshape(384, WIDTH).T.reshape(WIDTH, 3, 128).astype(f32)
    w_out_grad = attention_total[:, 192:].reshape(128, WIDTH).astype(f32)
    fc_bias_grad = lax.dynamic_slice(early[4:], (x, high * 512), (1, 512))[0]
    qv_bias_grad = lax.dynamic_slice(late[2:], (0, tensor * 128), (2, 128))

    def placed(own, other):
        def crossed(array):
            return move(
                array,
                AXES,
                lambda x, z, y, core: (x, core * 2 + 1 - z % 2, y, z // 2),
            )

        stays = turned(own)
        comes = crossed(other)
        return jnp.where(pipe == 0, jnp.stack([stays, comes]), jnp.stack([comes, stays]))

    activations = placed(
        jnp.where(pipe == 0, first, second), jnp.where(pipe == 0, second, first)
    )
    in_grads = placed(
        jnp.where(pipe == 0, last_low, middle_low), jnp.where(pipe == 0, middle_low, last_low)
    )
    return (
        activations[None, :, :, None],
        in_grads[None, :, :, None],
        late[0][None],
        late[1][None],
        w_qkv_grad[None],
        qv_bias_grad[None],
        w_out_grad[None],
        early[0][None],
        early[1][None],
        early[2][None],
        w_fc_grad[None],
        fc_bias_grad[None],
        w_proj_grad[None],
        early[3][None],
    )


def solution(mesh):
    return jax.shard_map(
        on_device,
        mesh=mesh,
        in_specs=(
            P(None, "tensor", "dp", None),
            P(None, "dp", None),
            P(None, "tensor", "dp", None),
            P("pipe", None),
            P("pipe", None),
            P("pipe", None, None, "tensor"),
            P("pipe", None, "tensor"),
            P("pipe", "tensor", None),
            P("pipe", None),
            P("pipe", None),
            P("pipe", None),
            P("pipe", None, "tensor"),
            P("pipe", "tensor"),
            P("pipe", "tensor", None),
            P("pipe", None),
        ),
        out_specs=(
            P("pipe", None, "tensor", "dp", None),
            P("pipe", None, "tensor", "dp", None),
            P("pipe", None),
            P("pipe", None),
            P("pipe", None, None, "tensor"),
            P("pipe", None, "tensor"),
            P("pipe", "tensor", None),
            P("pipe", None),
            P("pipe", None),
            P("pipe", None),
            P("pipe", None, "tensor"),
            P("pipe", "tensor"),
            P("pipe", "tensor", None),
            P("pipe", None),
        ),
        check_vma=False,
    )
```

```python
import jax
import jax.numpy as jnp
from jax import lax
from jax.experimental import pallas as pl
from jax.experimental.pallas import tpu as pltpu
from jax.sharding import PartitionSpec as P

HEAD_DIM = 64
BLOCK = 96
WIDTH = 1024
epsilon = 1e-05
AXES = ("pipe", "tensor", "dp")
bf16 = jnp.bfloat16
f32 = jnp.float32


def spot(axes, x, z, y, core):
    index = 0
    for axis in axes:
        if axis == "pipe":
            index = index * 2 + z % 2
        elif axis == "tensor":
            index = index * 8 + x * 2 + z // 2
        else:
            index = index * 8 + y * 2 + core
    return index


def move(array, axes, rule):
    pairs = {}
    for x in range(4):
        for z in range(4):
            for y in range(4):
                for core in range(2):
                    goal = rule(x, z, y, core)
                    if goal is not None:
                        pairs[spot(axes, x, z, y, core)] = spot(axes, *goal)
    return lax.ppermute(array, axes, sorted(pairs.items()))


def along_x(array, by):
    return move(array, ("tensor",), lambda x, z, y, core: ((x + by) % 4, z, y, core))


def along_y(array, by):
    return move(array, ("dp",), lambda x, z, y, core: (x, z, (y + by) % 4, core))


def along_z(array, by, only=None):
    def rule(x, z, y, core):
        return (x, (z + by) % 4, y, core) if only is None or z % 2 == only else None

    return move(array, ("pipe", "tensor"), rule)


def other_core(array):
    return move(array, ("dp",), lambda x, z, y, core: (x, z, y, 1 - core))


def turned(array):
    return move(
        array, ("tensor", "dp"), lambda x, z, y, core: (x, core * 2 + z % 2, y, z // 2)
    )


def pick(array, index, axis=0):
    return lax.dynamic_index_in_dim(array, index, axis, keepdims=False)


def place(buffer, piece, starts):
    return lax.dynamic_update_slice(buffer, piece, starts)


def gather_rows(rows):
    return jnp.concatenate([rows] + [along_x(rows, by) for by in (1, 2, 3)], axis=0)


def scatter_rows(partial):
    parts = partial.astype(bf16).reshape(4, BLOCK, WIDTH)
    total = parts[0].astype(f32)
    for by in (1, 2, 3):
        total = total + along_x(parts[by], -by).astype(f32)
    return total


def dot(left, right, left_dim, right_dim):
    return lax.dot_general(
        left, right, (((left_dim,), (right_dim,)), ((), ())), preferred_element_type=f32
    )


def norm_forward(stream, gain, shift):
    average = jnp.mean(stream, axis=-1, keepdims=True)
    centred = stream - average
    inverse_scale = lax.rsqrt(jnp.mean(centred * centred, axis=-1, keepdims=True) + epsilon)
    standard = centred * inverse_scale
    return (standard * gain + shift).astype(bf16), standard, inverse_scale


def norm_backward(incoming, standard, inverse_scale, gain):
    scaled = incoming * gain
    correction = (
        scaled
        - jnp.mean(scaled, axis=-1, keepdims=True)
        - standard * jnp.mean(scaled * standard, axis=-1, keepdims=True)
    )
    return (
        correction * inverse_scale,
        jnp.sum(incoming * standard, axis=0),
        jnp.sum(incoming, axis=0),
    )


def masked_scores(query, keys, allowed):
    scores = jnp.einsum("qhe,khe->hqk", query, keys, preferred_element_type=f32)
    return jnp.where(allowed[None], scores * HEAD_DIM ** (-0.5), -1e30)


def attend_forward(query, keys, values, allowed):
    scores = masked_scores(query, keys, allowed)
    largest = jnp.max(scores, axis=-1, keepdims=True)
    terms = jnp.exp(scores - largest)
    summed = jnp.sum(terms, axis=-1, keepdims=True)
    weights = (terms / summed).astype(bf16)
    context = jnp.einsum("hqk,khe->qhe", weights, values, preferred_element_type=f32)
    return context.astype(bf16), largest + jnp.log(summed)


def attend_backward(query, keys, values, allowed, log_total, context_grad):
    weights = jnp.exp(masked_scores(query, keys, allowed) - log_total)
    weight_grad = jnp.einsum("qhe,khe->hqk", context_grad, values, preferred_element_type=f32)
    value_grad = jnp.einsum(
        "hqk,qhe->khe", weights.astype(bf16), context_grad, preferred_element_type=f32
    )
    correction = jnp.sum(weights * weight_grad, axis=-1, keepdims=True)
    score_grad = (weights * (weight_grad - correction)).astype(bf16)
    query_grad = jnp.einsum("hqk,khe->qhe", score_grad, keys, preferred_element_type=f32)
    key_grad = jnp.einsum("hqk,qhe->khe", score_grad, query, preferred_element_type=f32)
    scale = HEAD_DIM ** (-0.5)
    return query_grad * scale, key_grad * scale, value_grad


def split_heads(projected):
    view = projected.reshape(4 * BLOCK, 2, 3, 2, HEAD_DIM)
    return tuple(view[:, :, part].reshape(4 * BLOCK, 4, HEAD_DIM) for part in range(3))


def layer_forward(stream, allowed, vectors, hook):
    gain_one, shift_one, out_bias, gain_two, shift_two, proj_bias = vectors
    normed_one, standard_one, inverse_one = norm_forward(stream, gain_one, shift_one)
    rows_one, w_qkv, w_out, qkv_bias, fc_bias = hook(-1, gather_rows(normed_one))
    projected = (dot(rows_one, w_qkv, 1, 0) + qkv_bias).astype(bf16)
    query, key, value = split_heads(projected)
    both = jnp.stack([key, value]).reshape(2, 4 * BLOCK, 256)
    arrived = hook(0, other_core(both))
    keys, values = (
        part.reshape(8 * BLOCK, 4, HEAD_DIM)
        for part in jnp.concatenate([both, arrived], axis=1)
    )
    context, log_total = attend_forward(query, keys, values, allowed)
    context = context.reshape(4 * BLOCK, 256)
    context = hook(1, context)
    middle = stream + hook(2, scatter_rows(dot(context, w_out, 1, 1))) + out_bias
    normed_two, standard_two, inverse_two = norm_forward(middle, gain_two, shift_two)
    rows_two, w_fc, w_proj = hook(3, gather_rows(normed_two))
    gelu_input = dot(rows_two, w_fc, 1, 0) + fc_bias
    hidden = jax.nn.gelu(gelu_input, approximate=True).astype(bf16)
    result = middle + scatter_rows(dot(hidden, w_proj, 1, 0)) + proj_bias
    saved = (
        (standard_one, inverse_one, rows_one),
        (query, keys, values, log_total, context),
        (standard_two, inverse_two, rows_two, gelu_input, hidden),
    )
    return result.astype(bf16), (w_qkv, w_out, w_fc, w_proj), saved


def halves(grad, rows):
    return grad.astype(bf16).reshape(2, 2, rows, WIDTH)


def layer_backward(incoming, allowed, vectors, weights, saved, hook):
    gain_one, shift_one, out_bias, gain_two, shift_two, proj_bias = vectors
    w_qkv, w_out, w_fc, w_proj = weights
    (
        (standard_one, inverse_one, rows_one),
        (query, keys, values, log_total, context),
        (standard_two, inverse_two, rows_two, gelu_input, hidden),
    ) = saved
    grad_feed = incoming.astype(bf16)
    proj_bias_grad = jnp.sum(grad_feed.astype(f32), axis=0)
    feed_rows = hook(0, gather_rows(grad_feed))
    hidden_grad = dot(feed_rows, w_proj, 1, 1)
    gelu_pull = jax.vjp(lambda item: jax.nn.gelu(item, approximate=True), gelu_input)[1]
    gelu_grad = gelu_pull(hidden_grad)[0].astype(bf16)
    normed_two_grad = scatter_rows(dot(gelu_grad, w_fc, 1, 1))
    fc_bias_grad = jnp.sum(gelu_grad.astype(f32), axis=0)
    feed_group = jnp.concatenate(
        [halves(dot(gelu_grad, rows_two, 0, 0), 256), halves(dot(hidden, feed_rows, 0, 0), 256)],
        axis=2,
    )
    normed_two_grad = hook(1, normed_two_grad, feed_group)
    middle_norm, gain_two_grad, shift_two_grad = norm_backward(
        normed_two_grad, standard_two, inverse_two, gain_two
    )
    middle_grad = incoming + middle_norm
    grad_attention = middle_grad.astype(bf16)
    out_bias_grad = jnp.sum(grad_attention.astype(f32), axis=0)
    attention_rows = hook(2, gather_rows(grad_attention))
    context_grad = dot(attention_rows, w_out, 1, 0).astype(bf16)
    w_out_grad = dot(context, attention_rows, 0, 0)
    query_grad, key_grad, value_grad = attend_backward(
        query,
        keys,
        values,
        allowed,
        log_total,
        context_grad.reshape(4 * BLOCK, 4, HEAD_DIM),
    )
    both = jnp.stack([key_grad, value_grad]).reshape(2, 8 * BLOCK, 256)
    arrived = other_core(both[:, 4 * BLOCK :].astype(bf16))
    summed = both[:, : 4 * BLOCK] + arrived.astype(f32)
    triple = jnp.stack([query_grad.reshape(4 * BLOCK, 256), summed[0], summed[1]], axis=1)
    triple = triple.astype(bf16).reshape(4 * BLOCK, 3, 2, 128)
    triple = hook(3, jnp.moveaxis(triple, 2, 1).reshape(4 * BLOCK, 768))
    attention_group = jnp.concatenate(
        [halves(dot(triple, rows_one, 0, 0), 192), halves(w_out_grad, 64)], axis=2
    )
    normed_one_grad = hook(4, scatter_rows(dot(triple, w_qkv, 1, 1)), attention_group)
    qkv_bias_grad = jnp.sum(triple.astype(f32), axis=0)
    stream_norm, gain_one_grad, shift_one_grad = norm_backward(
        normed_one_grad, standard_one, inverse_one, gain_one
    )
    stream_grad = middle_grad + stream_norm
    early = (out_bias_grad, gain_two_grad, shift_two_grad, proj_bias_grad, fc_bias_grad)
    late = (gain_one_grad, shift_one_grad, qkv_bias_grad)
    return stream_grad, early, late


def over_cores(group, core):
    sent = other_core(pick(group, 1 - core, 1))
    mine = (pick(group, core, 1).astype(f32) + sent.astype(f32)).astype(bf16)
    return mine.reshape(2, 4, mine.shape[1] // 4, WIDTH)


def near_y(mine):
    y = lax.axis_index("dp") // 2
    own = pick(mine, y, 1).astype(f32)
    for by in (1, 3):
        own = own + along_y(pick(mine, (y + by) % 4, 1), by).astype(f32)
    return own


def far_y(mine, own):
    y = lax.axis_index("dp") // 2
    sent, own = tied(pick(mine, (y + 2) % 4, 1), own)
    return (own + along_y(sent, 2).astype(f32)).astype(bf16)


def over_z(zero, one, pipe, high):
    zero_near, zero_far = pick(zero, high), pick(zero, 1 - high)
    one_near, one_far = pick(one, high), pick(one, 1 - high)
    even = pipe == 0
    total = jnp.where(even, zero_near, one_near).astype(f32)
    total = total + along_z(jnp.where(even, one_near, zero_far), 1).astype(f32)
    total = total + along_z(jnp.where(even, one_far, zero_near), -1).astype(f32)
    total = total + along_z(jnp.where(even, zero_far, one_far), 2).astype(f32)
    return total.astype(bf16)


def back_over_y(own):
    rows = own.shape[0]
    y = lax.axis_index("dp") // 2
    whole = jnp.zeros((4, rows, WIDTH), bf16)
    whole = place(whole, own[None], (y, 0, 0))
    for by in (1, 2, 3):
        whole = place(whole, along_y(own, by)[None], ((y - by) % 4, 0, 0))
    whole = whole.reshape(4 * rows, WIDTH)
    core = lax.axis_index("dp") % 2
    both = jnp.zeros((2, 4 * rows, WIDTH), bf16)
    both = place(both, whole[None], (core, 0, 0))
    both = place(both, other_core(whole)[None], (1 - core, 0, 0))
    return both.reshape(2, 4, rows, WIDTH)


def everywhere(array, pipe):
    mine, other = pick(array, pipe), pick(array, 1 - pipe)
    total = mine + along_z(other, 1) + along_z(other, 3) + along_z(mine, 2)
    total = total + other_core(total)
    for along in (along_x, along_y):
        total = total + along(total, 1) + along(total, 2) + along(total, 3)
    return total


def tied(*arrays):
    return lax.optimization_barrier(arrays)


def lay_out(here, copies, sources, shapes):
    def kernel(at_ref, *refs):
        inputs, outputs = refs[: len(sources)], refs[len(sources) : -1]
        semaphores = refs[-1]
        started = []
        for source, start, output, stop in copies(at_ref[0], at_ref[1], at_ref[2]):
            copy = pltpu.make_async_copy(
                inputs[source].at[start], outputs[output].at[stop], semaphores.at[len(started)]
            )
            copy.start()
            started.append(copy)
        for copy in started:
            copy.wait()

    count = len(copies(0, 0, 0))
    whole = pl.BlockSpec(memory_space=pl.ANY)
    return pl.pallas_call(
        kernel,
        out_shape=tuple(jax.ShapeDtypeStruct(shape, bf16) for shape in shapes),
        in_specs=[pl.BlockSpec(memory_space=pltpu.SMEM)] + [whole] * len(sources),
        out_specs=tuple(pl.BlockSpec(memory_space=pltpu.VMEM) for _ in shapes),
        scratch_shapes=[pltpu.SemaphoreType.DMA((count,))],
        compiler_params=pltpu.CompilerParams(vmem_limit_bytes=24 * 1024 * 1024),
    )(jnp.stack(here).astype(jnp.int32), *sources)


def span(start, size, unit=None):
    if unit is not None and not isinstance(start, int):
        start = pl.multiple_of(start, unit)
    return pl.ds(start, size)


ORDER = (1, 3, 2)


def sources_of(pipe, high):
    z = high * 2 + pipe
    return [((z + 4 - by) % 2, (z + 4 - by) % 4 // 2) for by in ORDER]


def send_first(core, w_qkv, turned_out, smalls):
    group = jnp.concatenate(
        [
            lax.dynamic_slice_in_dim(w_qkv, core * 512, 512, 0),
            lax.dynamic_slice_in_dim(turned_out, core * 512, 512, 0),
        ],
        axis=1,
    )
    group = jnp.concatenate([group, smalls], axis=0)
    came = [along_z(group, by) for by in ORDER[:2]]
    group, *came = tied(group, *came)
    return came + [along_z(group, ORDER[2])]


def lay_first(here, w_qkv, turned_out, smalls, came, after):
    swapped = [other_core(item) for item in came[:2]]
    last, after = tied(came[2], after)
    came = came[:2] + [last]
    swapped.append(other_core(last))

    def copies(pipe, high, core):
        rows = span(0, 1024)
        result = [(0, (rows,), 0, (pipe, rows, span(high * 384, 384, 128)))]
        result.append((1, (rows,), 1, (pipe, rows, span(high * 128, 128, 128))))
        result.append((2, (span(0, 16),), 2, (pipe, high)))
        rows = span(0, 512)
        for i, (layer, slot) in enumerate(sources_of(pipe, high)):
            for source, half in ((3 + i, core), (6 + i, 1 - core)):
                goal = span(half * 512, 512, 512)
                result.append(
                    (source, (rows, span(0, 384)), 0, (layer, goal, span(slot * 384, 384, 128)))
                )
                result.append(
                    (source, (rows, span(384, 128)), 1, (layer, goal, span(slot * 128, 128, 128)))
                )
            result.append((3 + i, (span(512, 16),), 2, (layer, slot)))
        return result

    arrays = lay_out(
        here,
        copies,
        [w_qkv, turned_out, smalls, *came, *swapped],
        [(2, 1024, 768), (2, 1024, 256), (2, 2, 16, 512)],
    )
    return arrays, after


def lay_fc(here, w_fc, came):
    swapped = other_core(jnp.stack(came))

    def copies(pipe, high, core):
        rows = span(0, 1024)
        result = [(0, (rows,), 0, (pipe, rows, span(high * 512, 512, 512)))]
        for i, (layer, slot) in enumerate(sources_of(pipe, high)):
            for source, lead, half in ((1 + i, (), core), (4, (i,), 1 - core)):
                goal = (layer, span(half * 512, 512, 512), span(slot * 512, 512, 512))
                result.append((source, (*lead, span(0, 512)), 0, goal))
        return result

    (array,) = lay_out(here, copies, [w_fc, *came, swapped], [(2, 1024, 1024)])
    return array


def lay_proj(here, w_proj, came):
    swapped = other_core(jnp.stack(came))

    def copies(pipe, high, core):
        result = [(0, (span(0, 512),), 0, (pipe, span(high * 512, 512, 512)))]
        for i, (layer, slot) in enumerate(sources_of(pipe, high)):
            for source, lead, half in ((1 + i, (), core), (4, (i,), 1 - core)):
                goal = (layer, span(slot * 512 + half * 256, 256, 256))
                result.append((source, (*lead, span(0, 256)), 0, goal))
        return result

    (array,) = lay_out(here, copies, [w_proj, *came, swapped], [(2, 1024, 1024)])
    return array


def on_device(
    inputs,
    segment_ids,
    cotangent,
    ln1_gain,
    ln1_bias,
    w_qkv,
    qv_bias,
    w_out,
    out_bias,
    ln2_gain,
    ln2_bias,
    w_fc,
    fc_bias,
    w_proj,
    proj_bias,
):
    pipe = lax.axis_index("pipe")
    tensor = lax.axis_index("tensor")
    dp = lax.axis_index("dp")
    x, high, core = tensor // 2, tensor % 2, dp % 2
    here = (pipe, high, core)
    stream = turned(pick(inputs, pipe).reshape(BLOCK, WIDTH)).astype(f32)
    cotangent_rows = turned(pick(cotangent, pipe).reshape(BLOCK, WIDTH)).astype(f32)
    segments = pick(segment_ids, pipe).reshape(8, BLOCK)
    segments = jnp.where(high == core, segments, other_core(segments))
    slots = ((x - jnp.arange(4)) % 4) * 2
    blocks = jnp.concatenate([slots + core, slots + 1 - core])
    numbers = segments[blocks].reshape(-1)
    positions = (blocks[:, None] * BLOCK + jnp.arange(BLOCK)[None]).reshape(-1)
    allowed = (numbers[: 4 * BLOCK, None] == numbers[None]) & (
        positions[None] <= positions[: 4 * BLOCK, None]
    )

    smalls = jnp.concatenate(
        [
            ln1_gain,
            ln1_bias,
            out_bias,
            ln2_gain,
            ln2_bias,
            proj_bias,
            qv_bias.reshape(1, 256),
            fc_bias,
            jnp.zeros((1, 16 * 512 - 6912), bf16),
        ],
        axis=1,
    ).reshape(16, 512)
    before = along_z(smalls, 1)
    flat_w_qkv, turned_out = w_qkv[0].reshape(WIDTH, 384), w_out[0].T
    came_first = send_first(core, flat_w_qkv, turned_out, smalls)
    half_fc = lax.dynamic_slice_in_dim(w_fc[0], core * 512, 512, 0)
    half_proj = lax.dynamic_slice_in_dim(w_proj[0], core * 256, 256, 0)
    coming, laid = {}, {}

    def biases(all_small, layer):
        flat = all_small[layer].reshape(2, -1).astype(f32)
        pairs = flat[:, 6144:6400].reshape(2, 2, 128)
        none = jnp.zeros((2, 128), f32)
        qkv_bias = jnp.stack([pairs[:, 0], none, pairs[:, 1]], axis=1).reshape(-1)
        return qkv_bias, flat[:, 6400:6912].reshape(-1)

    def first_hook(step, value):
        if step == -1:
            laid["first"], value = lay_first(
                here, flat_w_qkv, turned_out, smalls, came_first, value
            )
            return second_hook(step, value, 0)
        if step == 0:
            sent, *laid["first"] = tied(half_fc, *laid["first"])
            value, *coming["fc"] = tied(value, *[along_z(sent, by) for by in ORDER[:2]])
            return value
        if step == 1:
            sent, *came = tied(half_fc, *coming["fc"])
            value, *coming["fc"] = tied(value, *came, along_z(sent, ORDER[2]))
            return value
        if step == 2:
            sent, *coming["fc"] = tied(half_proj, *coming["fc"])
            laid["fc"] = lay_fc(here, w_fc[0], coming["fc"])
            value, *coming["proj"] = tied(value, *[along_z(sent, by) for by in ORDER[:2]])
            return value
        sent, *came = tied(half_proj, *coming["proj"])
        value, last = tied(value, along_z(sent, ORDER[2]))
        laid["proj"] = lay_proj(here, w_proj[0], came + [last])
        return value, laid["fc"][0], laid["proj"][0]

    def second_hook(step, value, layer=1):
        if step == -1:
            all_qkv, all_out, all_small = laid["first"]
            return (value, all_qkv[layer], all_out[layer]) + biases(all_small, layer)
        return value if step < 3 else (value, laid["fc"][1], laid["proj"][1])

    vectors = []
    for layer in range(2):
        flat = jnp.where(pipe == layer, smalls, before).astype(f32).reshape(-1)
        vectors.append(tuple(flat[i * WIDTH : (i + 1) * WIDTH] for i in range(6)))

    first, weights_first, saved_first = layer_forward(
        stream, allowed, vectors[0], first_hook
    )
    second, weights_second, saved_second = layer_forward(
        first.astype(f32),
        allowed,
        vectors[1],
        second_hook,
    )
    waiting = {}

    def keep(step, value, group=None):
        if group is not None:
            waiting[step] = group
        return value

    middle_grad, early_one, late_one = layer_backward(
        cotangent_rows, allowed, vectors[1], weights_second, saved_second, keep
    )
    middle_low = middle_grad.astype(bf16)
    groups_one = (waiting[1], waiting[4])
    kept = {}

    def reduce_along(step, value, group=None):
        if step == 0:
            halved = [over_cores(item, core) for item in groups_one]
            value, kept["one"] = tied(value, jnp.concatenate(halved, axis=2))
            return value
        if step == 1:
            value, kept["near"] = tied(value, near_y(kept["one"]))
            kept["feed"] = group
            return value
        if step == 2:
            value, kept["feed"] = tied(value, over_cores(kept["feed"], core))
            return value
        if step == 3:
            value, kept["one"] = tied(value, far_y(kept["one"], kept["near"]))
            return value
        feed = far_y(kept["feed"], near_y(kept["feed"]))
        value, kept["feed"], kept["attention"] = tied(value, feed, over_cores(group, core))
        return value

    last_grad, early_zero, late_zero = layer_backward(
        middle_low.astype(f32), allowed, vectors[0], weights_first, saved_first, reduce_along
    )
    last_low = last_grad.astype(bf16)
    attention = near_y(kept["attention"])
    far = along_y(pick(kept["attention"], (dp // 2 + 2) % 4, 1), 2)
    attention = (attention + far.astype(f32)).astype(bf16)
    zero = jnp.concatenate([kept["feed"], attention], axis=1)
    total = back_over_y(over_z(zero, kept["one"], pipe, high))

    def bias_rows(fc_bias_grad):
        return place(jnp.zeros((4, WIDTH), f32), fc_bias_grad[None], (x, 0))

    def late_rows(late):
        gain_grad, shift_grad, qkv_grad = late
        parts = qkv_grad.reshape(2, 3, 128)
        pairs = jnp.stack([parts[:, 0], parts[:, 2]]).reshape(2, 256)
        wide = place(jnp.zeros((2, WIDTH), f32), pairs, (0, x * 256))
        return jnp.concatenate([gain_grad[None], shift_grad[None], wide])

    small = jnp.stack(
        [
            jnp.concatenate([jnp.stack(early[:4]), bias_rows(early[4]), late_rows(late)])
            for early, late in ((early_zero, late_zero), (early_one, late_one))
        ]
    )
    small = everywhere(small, pipe)
    early, late = small[:8], small[8:]

    feed_total = total[:, :, :128].reshape(2, 512, WIDTH)
    attention_total = total[:, :, 128:].reshape(2, 256, WIDTH)
    w_fc_grad = feed_total[:, :256].reshape(512, WIDTH).T.astype(f32)
    w_proj_grad = feed_total[:, 256:].reshape(512, WIDTH).astype(f32)
    w_qkv_grad = attention_total[:, :192].reshape(384, WIDTH).T.reshape(WIDTH, 3, 128).astype(f32)
    w_out_grad = attention_total[:, 192:].reshape(128, WIDTH).astype(f32)
    fc_bias_grad = lax.dynamic_slice(early[4:], (x, high * 512), (1, 512))[0]
    qv_bias_grad = lax.dynamic_slice(late[2:], (0, tensor * 128), (2, 128))

    def placed(own, other):
        def crossed(array):
            return move(
                array,
                AXES,
                lambda x, z, y, core: (x, core * 2 + 1 - z % 2, y, z // 2),
            )

        stays = turned(own)
        comes = crossed(other)
        return jnp.where(pipe == 0, jnp.stack([stays, comes]), jnp.stack([comes, stays]))

    activations = placed(
        jnp.where(pipe == 0, first, second), jnp.where(pipe == 0, second, first)
    )
    in_grads = placed(
        jnp.where(pipe == 0, last_low, middle_low), jnp.where(pipe == 0, middle_low, last_low)
    )
    return (
        activations[None, :, :, None],
        in_grads[None, :, :, None],
        late[0][None],
        late[1][None],
        w_qkv_grad[None],
        qv_bias_grad[None],
        w_out_grad[None],
        early[0][None],
        early[1][None],
        early[2][None],
        w_fc_grad[None],
        fc_bias_grad[None],
        w_proj_grad[None],
        early[3][None],
    )


def solution(mesh):
    return jax.shard_map(
        on_device,
        mesh=mesh,
        in_specs=(
            P(None, "tensor", "dp", None),
            P(None, "dp", None),
            P(None, "tensor", "dp", None),
            P("pipe", None),
            P("pipe", None),
            P("pipe", None, None, "tensor"),
            P("pipe", None, "tensor"),
            P("pipe", "tensor", None),
            P("pipe", None),
            P("pipe", None),
            P("pipe", None),
            P("pipe", None, "tensor"),
            P("pipe", "tensor"),
            P("pipe", "tensor", None),
            P("pipe", None),
        ),
        out_specs=(
            P("pipe", None, "tensor", "dp", None),
            P("pipe", None, "tensor", "dp", None),
            P("pipe", None),
            P("pipe", None),
            P("pipe", None, None, "tensor"),
            P("pipe", None, "tensor"),
            P("pipe", "tensor", None),
            P("pipe", None),
            P("pipe", None),
            P("pipe", None),
            P("pipe", None, "tensor"),
            P("pipe", "tensor"),
            P("pipe", "tensor", None),
            P("pipe", None),
        ),
        check_vma=False,
    )
```

```python
import jax
import jax.numpy as jnp
from jax import lax
from jax.experimental import pallas as pl
from jax.experimental.pallas import tpu as pltpu
from jax.sharding import PartitionSpec as P

HEAD_DIM = 64
BLOCK = 96
WIDTH = 1024
epsilon = 1e-05
AXES = ("pipe", "tensor", "dp")
bf16 = jnp.bfloat16
f32 = jnp.float32


def spot(axes, x, z, y, core):
    index = 0
    for axis in axes:
        if axis == "pipe":
            index = index * 2 + z % 2
        elif axis == "tensor":
            index = index * 8 + x * 2 + z // 2
        else:
            index = index * 8 + y * 2 + core
    return index


def move(array, axes, rule):
    pairs = {}
    for x in range(4):
        for z in range(4):
            for y in range(4):
                for core in range(2):
                    goal = rule(x, z, y, core)
                    if goal is not None:
                        pairs[spot(axes, x, z, y, core)] = spot(axes, *goal)
    return lax.ppermute(array, axes, sorted(pairs.items()))


def along_x(array, by):
    return move(array, ("tensor",), lambda x, z, y, core: ((x + by) % 4, z, y, core))


def along_y(array, by):
    return move(array, ("dp",), lambda x, z, y, core: (x, z, (y + by) % 4, core))


def along_z(array, by, only=None):
    def rule(x, z, y, core):
        return (x, (z + by) % 4, y, core) if only is None or z % 2 == only else None

    return move(array, ("pipe", "tensor"), rule)


def other_core(array):
    return move(array, ("dp",), lambda x, z, y, core: (x, z, y, 1 - core))


def turned(array):
    return move(
        array, ("tensor", "dp"), lambda x, z, y, core: (x, core * 2 + z % 2, y, z // 2)
    )


def pick(array, index, axis=0):
    return lax.dynamic_index_in_dim(array, index, axis, keepdims=False)


def place(buffer, piece, starts):
    return lax.dynamic_update_slice(buffer, piece, starts)


def gather_rows(rows):
    return jnp.concatenate([rows] + [along_x(rows, by) for by in (1, 2, 3)], axis=0)


def scatter_rows(partial):
    parts = partial.astype(bf16).reshape(4, BLOCK, WIDTH)
    total = parts[0].astype(f32)
    for by in (1, 2, 3):
        total = total + along_x(parts[by], -by).astype(f32)
    return total


def dot(left, right, left_dim, right_dim):
    return lax.dot_general(
        left, right, (((left_dim,), (right_dim,)), ((), ())), preferred_element_type=f32
    )


def norm_forward(stream, gain, shift):
    average = jnp.mean(stream, axis=-1, keepdims=True)
    centred = stream - average
    inverse_scale = lax.rsqrt(jnp.mean(centred * centred, axis=-1, keepdims=True) + epsilon)
    standard = centred * inverse_scale
    return (standard * gain + shift).astype(bf16), standard, inverse_scale


def norm_backward(incoming, standard, inverse_scale, gain):
    scaled = incoming * gain
    correction = (
        scaled
        - jnp.mean(scaled, axis=-1, keepdims=True)
        - standard * jnp.mean(scaled * standard, axis=-1, keepdims=True)
    )
    return (
        correction * inverse_scale,
        jnp.sum(incoming * standard, axis=0),
        jnp.sum(incoming, axis=0),
    )


def masked_scores(query, keys, allowed):
    scores = jnp.einsum("qhe,khe->hqk", query, keys, preferred_element_type=f32)
    return jnp.where(allowed[None], scores * HEAD_DIM ** (-0.5), -1e30)


def attend_forward(query, keys, values, allowed):
    scores = masked_scores(query, keys, allowed)
    largest = jnp.max(scores, axis=-1, keepdims=True)
    terms = jnp.exp(scores - largest)
    summed = jnp.sum(terms, axis=-1, keepdims=True)
    weights = (terms / summed).astype(bf16)
    context = jnp.einsum("hqk,khe->qhe", weights, values, preferred_element_type=f32)
    return context.astype(bf16), largest + jnp.log(summed)


def attend_backward(query, keys, values, allowed, log_total, context_grad):
    weights = jnp.exp(masked_scores(query, keys, allowed) - log_total)
    weight_grad = jnp.einsum("qhe,khe->hqk", context_grad, values, preferred_element_type=f32)
    value_grad = jnp.einsum(
        "hqk,qhe->khe", weights.astype(bf16), context_grad, preferred_element_type=f32
    )
    correction = jnp.sum(weights * weight_grad, axis=-1, keepdims=True)
    score_grad = (weights * (weight_grad - correction)).astype(bf16)
    query_grad = jnp.einsum("hqk,khe->qhe", score_grad, keys, preferred_element_type=f32)
    key_grad = jnp.einsum("hqk,qhe->khe", score_grad, query, preferred_element_type=f32)
    scale = HEAD_DIM ** (-0.5)
    return query_grad * scale, key_grad * scale, value_grad


def split_heads(projected):
    view = projected.reshape(4 * BLOCK, 2, 3, 2, HEAD_DIM)
    return tuple(view[:, :, part].reshape(4 * BLOCK, 4, HEAD_DIM) for part in range(3))


def layer_forward(stream, allowed, vectors, hook):
    gain_one, shift_one, out_bias, gain_two, shift_two, proj_bias = vectors
    normed_one, standard_one, inverse_one = norm_forward(stream, gain_one, shift_one)
    rows_one, w_qkv, w_out, qkv_bias, fc_bias = hook(-1, gather_rows(normed_one))
    projected = (dot(rows_one, w_qkv, 1, 0) + qkv_bias).astype(bf16)
    query, key, value = split_heads(projected)
    both = jnp.stack([key, value]).reshape(2, 4 * BLOCK, 256)
    arrived = hook(0, other_core(both))
    keys, values = (
        part.reshape(8 * BLOCK, 4, HEAD_DIM)
        for part in jnp.concatenate([both, arrived], axis=1)
    )
    context, log_total = attend_forward(query, keys, values, allowed)
    context = context.reshape(4 * BLOCK, 256)
    context = hook(1, context)
    middle = stream + hook(2, scatter_rows(dot(context, w_out, 1, 1))) + out_bias
    normed_two, standard_two, inverse_two = norm_forward(middle, gain_two, shift_two)
    rows_two, w_fc, w_proj = hook(3, gather_rows(normed_two))
    gelu_input = dot(rows_two, w_fc, 1, 0) + fc_bias
    hidden = jax.nn.gelu(gelu_input, approximate=True).astype(bf16)
    result = middle + scatter_rows(dot(hidden, w_proj, 1, 0)) + proj_bias
    saved = (
        (standard_one, inverse_one, rows_one),
        (query, keys, values, log_total, context),
        (standard_two, inverse_two, rows_two, gelu_input, hidden),
    )
    return result.astype(bf16), (w_qkv, w_out, w_fc, w_proj), saved


def halves(grad, rows):
    return grad.astype(bf16).reshape(2, 2, rows, WIDTH)


def layer_backward(incoming, allowed, vectors, weights, saved, hook):
    gain_one, shift_one, out_bias, gain_two, shift_two, proj_bias = vectors
    w_qkv, w_out, w_fc, w_proj = weights
    (
        (standard_one, inverse_one, rows_one),
        (query, keys, values, log_total, context),
        (standard_two, inverse_two, rows_two, gelu_input, hidden),
    ) = saved
    grad_feed = incoming.astype(bf16)
    proj_bias_grad = jnp.sum(grad_feed.astype(f32), axis=0)
    feed_rows = hook(0, gather_rows(grad_feed))
    hidden_grad = dot(feed_rows, w_proj, 1, 1)
    gelu_pull = jax.vjp(lambda item: jax.nn.gelu(item, approximate=True), gelu_input)[1]
    gelu_grad = gelu_pull(hidden_grad)[0].astype(bf16)
    normed_two_grad = scatter_rows(dot(gelu_grad, w_fc, 1, 1))
    fc_bias_grad = jnp.sum(gelu_grad.astype(f32), axis=0)
    feed_group = jnp.concatenate(
        [halves(dot(gelu_grad, rows_two, 0, 0), 256), halves(dot(hidden, feed_rows, 0, 0), 256)],
        axis=2,
    )
    normed_two_grad = hook(1, normed_two_grad, feed_group)
    middle_norm, gain_two_grad, shift_two_grad = norm_backward(
        normed_two_grad, standard_two, inverse_two, gain_two
    )
    middle_grad = incoming + middle_norm
    grad_attention = middle_grad.astype(bf16)
    out_bias_grad = jnp.sum(grad_attention.astype(f32), axis=0)
    attention_rows = hook(2, gather_rows(grad_attention))
    context_grad = dot(attention_rows, w_out, 1, 0).astype(bf16)
    w_out_grad = dot(context, attention_rows, 0, 0)
    query_grad, key_grad, value_grad = attend_backward(
        query,
        keys,
        values,
        allowed,
        log_total,
        context_grad.reshape(4 * BLOCK, 4, HEAD_DIM),
    )
    both = jnp.stack([key_grad, value_grad]).reshape(2, 8 * BLOCK, 256)
    arrived = other_core(both[:, 4 * BLOCK :].astype(bf16))
    summed = both[:, : 4 * BLOCK] + arrived.astype(f32)
    triple = jnp.stack([query_grad.reshape(4 * BLOCK, 256), summed[0], summed[1]], axis=1)
    triple = triple.astype(bf16).reshape(4 * BLOCK, 3, 2, 128)
    triple = hook(3, jnp.moveaxis(triple, 2, 1).reshape(4 * BLOCK, 768))
    attention_group = jnp.concatenate(
        [halves(dot(triple, rows_one, 0, 0), 192), halves(w_out_grad, 64)], axis=2
    )
    normed_one_grad = hook(4, scatter_rows(dot(triple, w_qkv, 1, 1)), attention_group)
    qkv_bias_grad = jnp.sum(triple.astype(f32), axis=0)
    stream_norm, gain_one_grad, shift_one_grad = norm_backward(
        normed_one_grad, standard_one, inverse_one, gain_one
    )
    stream_grad = middle_grad + stream_norm
    early = (out_bias_grad, gain_two_grad, shift_two_grad, proj_bias_grad, fc_bias_grad)
    late = (gain_one_grad, shift_one_grad, qkv_bias_grad)
    return stream_grad, early, late


def over_cores(group, core):
    sent = other_core(pick(group, 1 - core, 1))
    mine = (pick(group, core, 1).astype(f32) + sent.astype(f32)).astype(bf16)
    return mine.reshape(2, 4, mine.shape[1] // 4, WIDTH)


def near_y(mine):
    y = lax.axis_index("dp") // 2
    own = pick(mine, y, 1).astype(f32)
    for by in (1, 3):
        own = own + along_y(pick(mine, (y + by) % 4, 1), by).astype(f32)
    return own


def far_y(mine, own):
    y = lax.axis_index("dp") // 2
    sent, own = tied(pick(mine, (y + 2) % 4, 1), own)
    return (own + along_y(sent, 2).astype(f32)).astype(bf16)


def over_z(zero, one, pipe, high):
    zero_near, zero_far = pick(zero, high), pick(zero, 1 - high)
    one_near, one_far = pick(one, high), pick(one, 1 - high)
    even = pipe == 0
    total = jnp.where(even, zero_near, one_near).astype(f32)
    total = total + along_z(jnp.where(even, one_near, zero_far), 1).astype(f32)
    total = total + along_z(jnp.where(even, one_far, zero_near), -1).astype(f32)
    total = total + along_z(jnp.where(even, zero_far, one_far), 2).astype(f32)
    return total.astype(bf16)


def back_over_y(own):
    rows = own.shape[0]
    y = lax.axis_index("dp") // 2
    whole = jnp.zeros((4, rows, WIDTH), bf16)
    whole = place(whole, own[None], (y, 0, 0))
    for by in (1, 2, 3):
        whole = place(whole, along_y(own, by)[None], ((y - by) % 4, 0, 0))
    return whole


def both_halves(whole):
    core = lax.axis_index("dp") % 2
    both = jnp.zeros((2,) + whole.shape, bf16)
    both = place(both, whole[None], (core, 0, 0, 0))
    return place(both, other_core(whole)[None], (1 - core, 0, 0, 0))


def over_line(small):
    small = small + other_core(small)
    return small + along_x(small, 1) + along_x(small, 2) + along_x(small, 3)


def small_over_z(small, pipe):
    mine, other = pick(small, pipe), pick(small, 1 - pipe)
    return mine + along_z(other, 1) + along_z(other, 3) + along_z(mine, 2)


def tied(*arrays):
    return lax.optimization_barrier(arrays)


def lay_out(here, copies, sources, shapes):
    def kernel(at_ref, *refs):
        inputs, outputs = refs[: len(sources)], refs[len(sources) : -1]
        semaphores = refs[-1]
        started = []
        for source, start, output, stop in copies(at_ref[0], at_ref[1], at_ref[2]):
            copy = pltpu.make_async_copy(
                inputs[source].at[start], outputs[output].at[stop], semaphores.at[len(started)]
            )
            copy.start()
            started.append(copy)
        for copy in started:
            copy.wait()

    count = len(copies(0, 0, 0))
    whole = pl.BlockSpec(memory_space=pl.ANY)
    return pl.pallas_call(
        kernel,
        out_shape=tuple(jax.ShapeDtypeStruct(shape, bf16) for shape in shapes),
        in_specs=[pl.BlockSpec(memory_space=pltpu.SMEM)] + [whole] * len(sources),
        out_specs=tuple(pl.BlockSpec(memory_space=pltpu.VMEM) for _ in shapes),
        scratch_shapes=[pltpu.SemaphoreType.DMA((count,))],
        compiler_params=pltpu.CompilerParams(vmem_limit_bytes=24 * 1024 * 1024),
    )(jnp.stack(here).astype(jnp.int32), *sources)


def span(start, size, unit=None):
    if unit is not None and not isinstance(start, int):
        start = pl.multiple_of(start, unit)
    return pl.ds(start, size)


ORDER = (1, 3, 2)


def sources_of(pipe, high):
    z = high * 2 + pipe
    return [((z + 4 - by) % 2, (z + 4 - by) % 4 // 2) for by in ORDER]


def send_first(core, w_qkv, turned_out, smalls):
    group = jnp.concatenate(
        [
            lax.dynamic_slice_in_dim(w_qkv, core * 512, 512, 0),
            lax.dynamic_slice_in_dim(turned_out, core * 512, 512, 0),
        ],
        axis=1,
    )
    group = jnp.concatenate([group, smalls], axis=0)
    came = [along_z(group, by) for by in ORDER[:2]]
    group, *came = tied(group, *came)
    return came + [along_z(group, ORDER[2])]


def lay_first(here, w_qkv, turned_out, smalls, came, after):
    swapped = [other_core(item) for item in came[:2]]
    last, after = tied(came[2], after)
    came = came[:2] + [last]
    swapped.append(other_core(last))

    def copies(pipe, high, core):
        rows = span(0, 1024)
        result = [(0, (rows,), 0, (pipe, rows, span(high * 384, 384, 128)))]
        result.append((1, (rows,), 1, (pipe, rows, span(high * 128, 128, 128))))
        result.append((2, (span(0, 16),), 2, (pipe, high)))
        rows = span(0, 512)
        for i, (layer, slot) in enumerate(sources_of(pipe, high)):
            for source, half in ((3 + i, core), (6 + i, 1 - core)):
                goal = span(half * 512, 512, 512)
                result.append(
                    (source, (rows, span(0, 384)), 0, (layer, goal, span(slot * 384, 384, 128)))
                )
                result.append(
                    (source, (rows, span(384, 128)), 1, (layer, goal, span(slot * 128, 128, 128)))
                )
            result.append((3 + i, (span(512, 16),), 2, (layer, slot)))
        return result

    arrays = lay_out(
        here,
        copies,
        [w_qkv, turned_out, smalls, *came, *swapped],
        [(2, 1024, 768), (2, 1024, 256), (2, 2, 16, 512)],
    )
    return arrays, after


def lay_fc(here, w_fc, came):
    swapped = other_core(jnp.stack(came))

    def copies(pipe, high, core):
        rows = span(0, 1024)
        result = [(0, (rows,), 0, (pipe, rows, span(high * 512, 512, 512)))]
        for i, (layer, slot) in enumerate(sources_of(pipe, high)):
            for source, lead, half in ((1 + i, (), core), (4, (i,), 1 - core)):
                goal = (layer, span(half * 512, 512, 512), span(slot * 512, 512, 512))
                result.append((source, (*lead, span(0, 512)), 0, goal))
        return result

    (array,) = lay_out(here, copies, [w_fc, *came, swapped], [(2, 1024, 1024)])
    return array


def lay_proj(here, w_proj, came):
    swapped = other_core(jnp.stack(came))

    def copies(pipe, high, core):
        result = [(0, (span(0, 512),), 0, (pipe, span(high * 512, 512, 512)))]
        for i, (layer, slot) in enumerate(sources_of(pipe, high)):
            for source, lead, half in ((1 + i, (), core), (4, (i,), 1 - core)):
                goal = (layer, span(slot * 512 + half * 256, 256, 256))
                result.append((source, (*lead, span(0, 256)), 0, goal))
        return result

    (array,) = lay_out(here, copies, [w_proj, *came, swapped], [(2, 1024, 1024)])
    return array


def on_device(
    inputs,
    segment_ids,
    cotangent,
    ln1_gain,
    ln1_bias,
    w_qkv,
    qv_bias,
    w_out,
    out_bias,
    ln2_gain,
    ln2_bias,
    w_fc,
    fc_bias,
    w_proj,
    proj_bias,
):
    pipe = lax.axis_index("pipe")
    tensor = lax.axis_index("tensor")
    dp = lax.axis_index("dp")
    x, high, core = tensor // 2, tensor % 2, dp % 2
    here = (pipe, high, core)
    stream = turned(pick(inputs, pipe).reshape(BLOCK, WIDTH)).astype(f32)
    cotangent_rows = turned(pick(cotangent, pipe).reshape(BLOCK, WIDTH)).astype(f32)
    segments = pick(segment_ids, pipe).reshape(8, BLOCK)
    segments = jnp.where(high == core, segments, other_core(segments))
    slots = ((x - jnp.arange(4)) % 4) * 2
    blocks = jnp.concatenate([slots + core, slots + 1 - core])
    numbers = segments[blocks].reshape(-1)
    positions = (blocks[:, None] * BLOCK + jnp.arange(BLOCK)[None]).reshape(-1)
    allowed = (numbers[: 4 * BLOCK, None] == numbers[None]) & (
        positions[None] <= positions[: 4 * BLOCK, None]
    )

    smalls = jnp.concatenate(
        [
            ln1_gain,
            ln1_bias,
            out_bias,
            ln2_gain,
            ln2_bias,
            proj_bias,
            qv_bias.reshape(1, 256),
            fc_bias,
            jnp.zeros((1, 16 * 512 - 6912), bf16),
        ],
        axis=1,
    ).reshape(16, 512)
    before = along_z(smalls, 1)
    flat_w_qkv, turned_out = w_qkv[0].reshape(WIDTH, 384), w_out[0].T
    came_first = send_first(core, flat_w_qkv, turned_out, smalls)
    half_fc = lax.dynamic_slice_in_dim(w_fc[0], core * 512, 512, 0)
    half_proj = lax.dynamic_slice_in_dim(w_proj[0], core * 256, 256, 0)
    coming, laid = {}, {}

    def biases(all_small, layer):
        flat = all_small[layer].reshape(2, -1).astype(f32)
        pairs = flat[:, 6144:6400].reshape(2, 2, 128)
        none = jnp.zeros((2, 128), f32)
        qkv_bias = jnp.stack([pairs[:, 0], none, pairs[:, 1]], axis=1).reshape(-1)
        return qkv_bias, flat[:, 6400:6912].reshape(-1)

    def first_hook(step, value):
        if step == -1:
            laid["first"], value = lay_first(
                here, flat_w_qkv, turned_out, smalls, came_first, value
            )
            return second_hook(step, value, 0)
        if step == 0:
            sent, *laid["first"] = tied(half_fc, *laid["first"])
            value, *coming["fc"] = tied(value, *[along_z(sent, by) for by in ORDER[:2]])
            return value
        if step == 1:
            sent, *came = tied(half_fc, *coming["fc"])
            value, *coming["fc"] = tied(value, *came, along_z(sent, ORDER[2]))
            return value
        if step == 2:
            sent, *coming["fc"] = tied(half_proj, *coming["fc"])
            laid["fc"] = lay_fc(here, w_fc[0], coming["fc"])
            value, *coming["proj"] = tied(value, *[along_z(sent, by) for by in ORDER[:2]])
            return value
        sent, *came = tied(half_proj, *coming["proj"])
        value, last = tied(value, along_z(sent, ORDER[2]))
        laid["proj"] = lay_proj(here, w_proj[0], came + [last])
        return value, laid["fc"][0], laid["proj"][0]

    def second_hook(step, value, layer=1):
        if step == -1:
            all_qkv, all_out, all_small = laid["first"]
            return (value, all_qkv[layer], all_out[layer]) + biases(all_small, layer)
        return value if step < 3 else (value, laid["fc"][1], laid["proj"][1])

    vectors = []
    for layer in range(2):
        flat = jnp.where(pipe == layer, smalls, before).astype(f32).reshape(-1)
        vectors.append(tuple(flat[i * WIDTH : (i + 1) * WIDTH] for i in range(6)))

    first, weights_first, saved_first = layer_forward(
        stream, allowed, vectors[0], first_hook
    )
    second, weights_second, saved_second = layer_forward(
        first.astype(f32),
        allowed,
        vectors[1],
        second_hook,
    )
    waiting = {}

    def keep(step, value, group=None):
        if group is not None:
            waiting[step] = group
        return value

    middle_grad, early_one, late_one = layer_backward(
        cotangent_rows, allowed, vectors[1], weights_second, saved_second, keep
    )
    middle_low = middle_grad.astype(bf16)
    groups_one = (waiting[1], waiting[4])
    kept = {}

    def reduce_along(step, value, group=None):
        if step == 0:
            halved = [over_cores(item, core) for item in groups_one]
            value, kept["one"] = tied(value, jnp.concatenate(halved, axis=2))
            return value
        if step == 1:
            kept["near"] = near_y(kept["one"])
            kept["feed"] = group
            return value
        if step == 2:
            value, kept["near"] = tied(value, kept["near"])
            return value
        if step == 3:
            kept["one"] = far_y(kept["one"], kept["near"])
            value, kept["feed"] = tied(value, over_cores(kept["feed"], core))
            return value
        near, attention = near_y(kept["feed"]), over_cores(group, core)
        value, *rest = tied(value, kept["one"], near, attention)
        kept["one"], kept["near"], kept["attention"] = rest
        return value

    last_grad, early_zero, late_zero = layer_backward(
        middle_low.astype(f32), allowed, vectors[0], weights_first, saved_first, reduce_along
    )
    last_low = last_grad.astype(bf16)
    y = dp // 2
    near = jnp.concatenate([kept["near"], near_y(kept["attention"])], axis=1)
    far = [pick(kept[name], (y + 2) % 4, 1) for name in ("feed", "attention")]
    zero = near + along_y(jnp.concatenate(far, axis=1), 2).astype(f32)
    def bias_rows(fc_bias_grad):
        return place(jnp.zeros((4, WIDTH), f32), fc_bias_grad[None], (x, 0))

    def late_rows(late):
        gain_grad, shift_grad, qkv_grad = late
        parts = qkv_grad.reshape(2, 3, 128)
        pairs = jnp.stack([parts[:, 0], parts[:, 2]]).reshape(2, 256)
        wide = place(jnp.zeros((2, WIDTH), f32), pairs, (0, x * 256))
        return jnp.concatenate([gain_grad[None], shift_grad[None], wide])

    small = jnp.stack(
        [
            jnp.concatenate([jnp.stack(early[:4]), bias_rows(early[4]), late_rows(late)])
            for early, late in ((early_zero, late_zero), (early_one, late_one))
        ]
    )
    zero, small = tied(zero.astype(bf16), over_line(small))
    owned, small = tied(over_z(zero, kept["one"], pipe, high), small_over_z(small, pipe))
    small = small + along_y(small, 1) + along_y(small, 2) + along_y(small, 3)
    whole, small = tied(back_over_y(owned), small)
    total = both_halves(whole)
    early, late = small[:8], small[8:]

    feed_total = total[:, :, :128].reshape(2, 512, WIDTH)
    attention_total = total[:, :, 128:].reshape(2, 256, WIDTH)
    w_fc_grad = feed_total[:, :256].reshape(512, WIDTH).T.astype(f32)
    w_proj_grad = feed_total[:, 256:].reshape(512, WIDTH).astype(f32)
    w_qkv_grad = attention_total[:, :192].reshape(384, WIDTH).T.reshape(WIDTH, 3, 128).astype(f32)
    w_out_grad = attention_total[:, 192:].reshape(128, WIDTH).astype(f32)
    fc_bias_grad = lax.dynamic_slice(early[4:], (x, high * 512), (1, 512))[0]
    qv_bias_grad = lax.dynamic_slice(late[2:], (0, tensor * 128), (2, 128))

    def placed(own, other):
        def crossed(array):
            return move(
                array,
                AXES,
                lambda x, z, y, core: (x, core * 2 + 1 - z % 2, y, z // 2),
            )

        stays = turned(own)
        comes = crossed(other)
        return jnp.where(pipe == 0, jnp.stack([stays, comes]), jnp.stack([comes, stays]))

    activations = placed(
        jnp.where(pipe == 0, first, second), jnp.where(pipe == 0, second, first)
    )
    in_grads = placed(
        jnp.where(pipe == 0, last_low, middle_low), jnp.where(pipe == 0, middle_low, last_low)
    )
    return (
        activations[None, :, :, None],
        in_grads[None, :, :, None],
        late[0][None],
        late[1][None],
        w_qkv_grad[None],
        qv_bias_grad[None],
        w_out_grad[None],
        early[0][None],
        early[1][None],
        early[2][None],
        w_fc_grad[None],
        fc_bias_grad[None],
        w_proj_grad[None],
        early[3][None],
    )


def solution(mesh):
    return jax.shard_map(
        on_device,
        mesh=mesh,
        in_specs=(
            P(None, "tensor", "dp", None),
            P(None, "dp", None),
            P(None, "tensor", "dp", None),
            P("pipe", None),
            P("pipe", None),
            P("pipe", None, None, "tensor"),
            P("pipe", None, "tensor"),
            P("pipe", "tensor", None),
            P("pipe", None),
            P("pipe", None),
            P("pipe", None),
            P("pipe", None, "tensor"),
            P("pipe", "tensor"),
            P("pipe", "tensor", None),
            P("pipe", None),
        ),
        out_specs=(
            P("pipe", None, "tensor", "dp", None),
            P("pipe", None, "tensor", "dp", None),
            P("pipe", None),
            P("pipe", None),
            P("pipe", None, None, "tensor"),
            P("pipe", None, "tensor"),
            P("pipe", "tensor", None),
            P("pipe", None),
            P("pipe", None),
            P("pipe", None),
            P("pipe", None, "tensor"),
            P("pipe", "tensor"),
            P("pipe", "tensor", None),
            P("pipe", None),
        ),
        check_vma=False,
    )
```

```python
import jax
import jax.numpy as jnp
from jax import lax
from jax.experimental import pallas as pl
from jax.experimental.pallas import tpu as pltpu
from jax.sharding import PartitionSpec as P

HEAD_DIM = 64
BLOCK = 96
WIDTH = 1024
epsilon = 1e-05
AXES = ("pipe", "tensor", "dp")
bf16 = jnp.bfloat16
f32 = jnp.float32


def spot(axes, x, z, y, core):
    index = 0
    for axis in axes:
        if axis == "pipe":
            index = index * 2 + z % 2
        elif axis == "tensor":
            index = index * 8 + x * 2 + z // 2
        else:
            index = index * 8 + y * 2 + core
    return index


def move(array, axes, rule):
    pairs = {}
    for x in range(4):
        for z in range(4):
            for y in range(4):
                for core in range(2):
                    goal = rule(x, z, y, core)
                    if goal is not None:
                        pairs[spot(axes, x, z, y, core)] = spot(axes, *goal)
    return lax.ppermute(array, axes, sorted(pairs.items()))


def along_x(array, by):
    return move(array, ("tensor",), lambda x, z, y, core: ((x + by) % 4, z, y, core))


def along_y(array, by):
    return move(array, ("dp",), lambda x, z, y, core: (x, z, (y + by) % 4, core))


def along_z(array, by, only=None):
    def rule(x, z, y, core):
        return (x, (z + by) % 4, y, core) if only is None or z % 2 == only else None

    return move(array, ("pipe", "tensor"), rule)


def other_core(array):
    return move(array, ("dp",), lambda x, z, y, core: (x, z, y, 1 - core))


def turned(array):
    return move(
        array, ("tensor", "dp"), lambda x, z, y, core: (x, core * 2 + z % 2, y, z // 2)
    )


def pick(array, index, axis=0):
    return lax.dynamic_index_in_dim(array, index, axis, keepdims=False)


def place(buffer, piece, starts):
    return lax.dynamic_update_slice(buffer, piece, starts)


def gather_rows(rows):
    return jnp.concatenate([rows] + [along_x(rows, by) for by in (1, 2, 3)], axis=0)


def scatter_rows(partial):
    parts = partial.astype(bf16).reshape(4, BLOCK, WIDTH)
    total = parts[0].astype(f32)
    for by in (1, 2, 3):
        total = total + along_x(parts[by], -by).astype(f32)
    return total


def dot(left, right, left_dim, right_dim):
    return lax.dot_general(
        left, right, (((left_dim,), (right_dim,)), ((), ())), preferred_element_type=f32
    )


def norm_forward(stream, gain, shift):
    average = jnp.mean(stream, axis=-1, keepdims=True)
    centred = stream - average
    inverse_scale = lax.rsqrt(jnp.mean(centred * centred, axis=-1, keepdims=True) + epsilon)
    standard = centred * inverse_scale
    return (standard * gain + shift).astype(bf16), standard, inverse_scale


def norm_backward(incoming, standard, inverse_scale, gain):
    scaled = incoming * gain
    correction = (
        scaled
        - jnp.mean(scaled, axis=-1, keepdims=True)
        - standard * jnp.mean(scaled * standard, axis=-1, keepdims=True)
    )
    return (
        correction * inverse_scale,
        jnp.sum(incoming * standard, axis=0),
        jnp.sum(incoming, axis=0),
    )


def masked_scores(query, keys, allowed):
    scores = jnp.einsum("qhe,khe->hqk", query, keys, preferred_element_type=f32)
    return jnp.where(allowed[None], scores * HEAD_DIM ** (-0.5), -1e30)


def attend_forward(query, keys, values, allowed):
    scores = masked_scores(query, keys, allowed)
    largest = jnp.max(scores, axis=-1, keepdims=True)
    terms = jnp.exp(scores - largest)
    summed = jnp.sum(terms, axis=-1, keepdims=True)
    weights = (terms / summed).astype(bf16)
    context = jnp.einsum("hqk,khe->qhe", weights, values, preferred_element_type=f32)
    return context.astype(bf16), largest + jnp.log(summed)


def attend_backward(query, keys, values, allowed, log_total, context_grad):
    weights = jnp.exp(masked_scores(query, keys, allowed) - log_total)
    weight_grad = jnp.einsum("qhe,khe->hqk", context_grad, values, preferred_element_type=f32)
    value_grad = jnp.einsum(
        "hqk,qhe->khe", weights.astype(bf16), context_grad, preferred_element_type=f32
    )
    correction = jnp.sum(weights * weight_grad, axis=-1, keepdims=True)
    score_grad = (weights * (weight_grad - correction)).astype(bf16)
    query_grad = jnp.einsum("hqk,khe->qhe", score_grad, keys, preferred_element_type=f32)
    key_grad = jnp.einsum("hqk,qhe->khe", score_grad, query, preferred_element_type=f32)
    scale = HEAD_DIM ** (-0.5)
    return query_grad * scale, key_grad * scale, value_grad


def split_heads(projected):
    view = projected.reshape(4 * BLOCK, 2, 3, 2, HEAD_DIM)
    return tuple(view[:, :, part].reshape(4 * BLOCK, 4, HEAD_DIM) for part in range(3))


def layer_forward(stream, allowed, vectors, hook):
    gain_one, shift_one, out_bias, gain_two, shift_two, proj_bias = vectors
    normed_one, standard_one, inverse_one = norm_forward(stream, gain_one, shift_one)
    rows_one, w_qkv, w_out, qkv_bias, fc_bias = hook(-1, gather_rows(normed_one))
    projected = (dot(rows_one, w_qkv, 1, 0) + qkv_bias).astype(bf16)
    query, key, value = split_heads(projected)
    both = jnp.stack([key, value]).reshape(2, 4 * BLOCK, 256)
    arrived = hook(0, other_core(both))
    keys, values = (
        part.reshape(8 * BLOCK, 4, HEAD_DIM)
        for part in jnp.concatenate([both, arrived], axis=1)
    )
    context, log_total = attend_forward(query, keys, values, allowed)
    context = context.reshape(4 * BLOCK, 256)
    context = hook(1, context)
    middle = stream + hook(2, scatter_rows(dot(context, w_out, 1, 1))) + out_bias
    normed_two, standard_two, inverse_two = norm_forward(middle, gain_two, shift_two)
    rows_two, w_fc, w_proj = hook(3, gather_rows(normed_two))
    gelu_input = dot(rows_two, w_fc, 1, 0) + fc_bias
    hidden = jax.nn.gelu(gelu_input, approximate=True).astype(bf16)
    result = middle + scatter_rows(dot(hidden, w_proj, 1, 0)) + proj_bias
    saved = (
        (standard_one, inverse_one, rows_one),
        (query, keys, values, log_total, context),
        (standard_two, inverse_two, rows_two, gelu_input, hidden),
    )
    return result.astype(bf16), (w_qkv, w_out, w_fc, w_proj), saved


def halves(grad, rows):
    return grad.astype(bf16).reshape(2, 2, rows, WIDTH)


def layer_backward(incoming, allowed, vectors, weights, saved, hook):
    gain_one, shift_one, out_bias, gain_two, shift_two, proj_bias = vectors
    w_qkv, w_out, w_fc, w_proj = weights
    (
        (standard_one, inverse_one, rows_one),
        (query, keys, values, log_total, context),
        (standard_two, inverse_two, rows_two, gelu_input, hidden),
    ) = saved
    grad_feed = incoming.astype(bf16)
    proj_bias_grad = jnp.sum(grad_feed.astype(f32), axis=0)
    feed_rows = hook(0, gather_rows(grad_feed))
    hidden_grad = dot(feed_rows, w_proj, 1, 1)
    gelu_pull = jax.vjp(lambda item: jax.nn.gelu(item, approximate=True), gelu_input)[1]
    gelu_grad = gelu_pull(hidden_grad)[0].astype(bf16)
    normed_two_grad = scatter_rows(dot(gelu_grad, w_fc, 1, 1))
    fc_bias_grad = jnp.sum(gelu_grad.astype(f32), axis=0)
    feed_group = jnp.concatenate(
        [halves(dot(gelu_grad, rows_two, 0, 0), 256), halves(dot(hidden, feed_rows, 0, 0), 256)],
        axis=2,
    )
    normed_two_grad = hook(1, normed_two_grad, feed_group)
    middle_norm, gain_two_grad, shift_two_grad = norm_backward(
        normed_two_grad, standard_two, inverse_two, gain_two
    )
    middle_grad = incoming + middle_norm
    grad_attention = middle_grad.astype(bf16)
    out_bias_grad = jnp.sum(grad_attention.astype(f32), axis=0)
    attention_rows = hook(2, gather_rows(grad_attention))
    context_grad = dot(attention_rows, w_out, 1, 0).astype(bf16)
    w_out_grad = dot(context, attention_rows, 0, 0)
    query_grad, key_grad, value_grad = attend_backward(
        query,
        keys,
        values,
        allowed,
        log_total,
        context_grad.reshape(4 * BLOCK, 4, HEAD_DIM),
    )
    both = jnp.stack([key_grad, value_grad]).reshape(2, 8 * BLOCK, 256)
    arrived = other_core(both[:, 4 * BLOCK :].astype(bf16))
    summed = both[:, : 4 * BLOCK] + arrived.astype(f32)
    triple = jnp.stack([query_grad.reshape(4 * BLOCK, 256), summed[0], summed[1]], axis=1)
    triple = triple.astype(bf16).reshape(4 * BLOCK, 3, 2, 128)
    triple = hook(3, jnp.moveaxis(triple, 2, 1).reshape(4 * BLOCK, 768))
    attention_group = jnp.concatenate(
        [halves(dot(triple, rows_one, 0, 0), 192), halves(w_out_grad, 64)], axis=2
    )
    normed_one_grad = hook(4, scatter_rows(dot(triple, w_qkv, 1, 1)), attention_group)
    qkv_bias_grad = jnp.sum(triple.astype(f32), axis=0)
    stream_norm, gain_one_grad, shift_one_grad = norm_backward(
        normed_one_grad, standard_one, inverse_one, gain_one
    )
    stream_grad = middle_grad + stream_norm
    early = (out_bias_grad, gain_two_grad, shift_two_grad, proj_bias_grad, fc_bias_grad)
    late = (gain_one_grad, shift_one_grad, qkv_bias_grad)
    return stream_grad, early, late


def over_cores(group, core):
    sent = other_core(pick(group, 1 - core, 1))
    mine = (pick(group, core, 1).astype(f32) + sent.astype(f32)).astype(bf16)
    return mine.reshape(2, 4, mine.shape[1] // 4, WIDTH)


def near_y(mine):
    y = lax.axis_index("dp") // 2
    own = pick(mine, y, 1).astype(f32)
    for by in (1, 3):
        own = own + along_y(pick(mine, (y + by) % 4, 1), by).astype(f32)
    return own


def far_y(mine, own):
    y = lax.axis_index("dp") // 2
    sent, own = tied(pick(mine, (y + 2) % 4, 1), own)
    return (own + along_y(sent, 2).astype(f32)).astype(bf16)


def over_z(zero, one, pipe, high):
    zero_near, zero_far = pick(zero, high), pick(zero, 1 - high)
    one_near, one_far = pick(one, high), pick(one, 1 - high)
    even = pipe == 0
    total = jnp.where(even, zero_near, one_near).astype(f32)
    total = total + along_z(jnp.where(even, one_near, zero_far), 1).astype(f32)
    total = total + along_z(jnp.where(even, one_far, zero_near), -1).astype(f32)
    total = total + along_z(jnp.where(even, zero_far, one_far), 2).astype(f32)
    return total.astype(bf16)


def back_over_y(own):
    rows = own.shape[0]
    y = lax.axis_index("dp") // 2
    whole = jnp.zeros((4, rows, WIDTH), bf16)
    whole = place(whole, own[None], (y, 0, 0))
    for by in (1, 2, 3):
        whole = place(whole, along_y(own, by)[None], ((y - by) % 4, 0, 0))
    whole = whole.reshape(4 * rows, WIDTH)
    core = lax.axis_index("dp") % 2
    both = jnp.zeros((2, 4 * rows, WIDTH), bf16)
    both = place(both, whole[None], (core, 0, 0))
    both = place(both, other_core(whole)[None], (1 - core, 0, 0))
    return both.reshape(2, 4, rows, WIDTH)


def everywhere(array, pipe):
    mine, other = pick(array, pipe), pick(array, 1 - pipe)
    total = mine + along_z(other, 1) + along_z(other, 3) + along_z(mine, 2)
    total = total + other_core(total)
    for along in (along_x, along_y):
        total = total + along(total, 1) + along(total, 2) + along(total, 3)
    return total


def tied(*arrays):
    return lax.optimization_barrier(arrays)


def lay_out(here, copies, sources, shapes):
    def kernel(at_ref, *refs):
        inputs, outputs = refs[: len(sources)], refs[len(sources) : -1]
        semaphores = refs[-1]
        started = []
        for source, start, output, stop in copies(at_ref[0], at_ref[1], at_ref[2]):
            copy = pltpu.make_async_copy(
                inputs[source].at[start], outputs[output].at[stop], semaphores.at[len(started)]
            )
            copy.start()
            started.append(copy)
        for copy in started:
            copy.wait()

    count = len(copies(0, 0, 0))
    whole = pl.BlockSpec(memory_space=pl.ANY)
    return pl.pallas_call(
        kernel,
        out_shape=tuple(jax.ShapeDtypeStruct(shape, bf16) for shape in shapes),
        in_specs=[pl.BlockSpec(memory_space=pltpu.SMEM)] + [whole] * len(sources),
        out_specs=tuple(pl.BlockSpec(memory_space=pltpu.VMEM) for _ in shapes),
        scratch_shapes=[pltpu.SemaphoreType.DMA((count,))],
        compiler_params=pltpu.CompilerParams(vmem_limit_bytes=24 * 1024 * 1024),
    )(jnp.stack(here).astype(jnp.int32), *sources)


def span(start, size, unit=None):
    if unit is not None and not isinstance(start, int):
        start = pl.multiple_of(start, unit)
    return pl.ds(start, size)


ORDER = (1, 3, 2)


def sources_of(pipe, high):
    z = high * 2 + pipe
    return [((z + 4 - by) % 2, (z + 4 - by) % 4 // 2) for by in ORDER]


def send_first(core, w_qkv, turned_out, smalls):
    group = jnp.concatenate(
        [
            lax.dynamic_slice_in_dim(w_qkv, core * 512, 512, 0),
            lax.dynamic_slice_in_dim(turned_out, core * 512, 512, 0),
        ],
        axis=1,
    )
    group = jnp.concatenate([group, smalls], axis=0)
    came = [along_z(group, by) for by in ORDER[:2]]
    group, *came = tied(group, *came)
    return came + [along_z(group, ORDER[2])]


def lay_first(here, w_qkv, turned_out, smalls, came, after):
    swapped = [other_core(item) for item in came[:2]]
    last, after = tied(came[2], after)
    came = came[:2] + [last]
    swapped.append(other_core(last))

    def copies(pipe, high, core):
        rows = span(0, 1024)
        result = [(0, (rows,), 0, (pipe, rows, span(high * 384, 384, 128)))]
        result.append((1, (rows,), 1, (pipe, rows, span(high * 128, 128, 128))))
        result.append((2, (span(0, 16),), 2, (pipe, high)))
        rows = span(0, 512)
        for i, (layer, slot) in enumerate(sources_of(pipe, high)):
            for source, half in ((3 + i, core), (6 + i, 1 - core)):
                goal = span(half * 512, 512, 512)
                result.append(
                    (source, (rows, span(0, 384)), 0, (layer, goal, span(slot * 384, 384, 128)))
                )
                result.append(
                    (source, (rows, span(384, 128)), 1, (layer, goal, span(slot * 128, 128, 128)))
                )
            result.append((3 + i, (span(512, 16),), 2, (layer, slot)))
        return result

    arrays = lay_out(
        here,
        copies,
        [w_qkv, turned_out, smalls, *came, *swapped],
        [(2, 1024, 768), (2, 1024, 256), (2, 2, 16, 512)],
    )
    return arrays, after


def lay_fc(here, w_fc, came):
    swapped = other_core(jnp.stack(came))

    def copies(pipe, high, core):
        rows = span(0, 1024)
        result = [(0, (rows,), 0, (pipe, rows, span(high * 512, 512, 512)))]
        for i, (layer, slot) in enumerate(sources_of(pipe, high)):
            for source, lead, half in ((1 + i, (), core), (4, (i,), 1 - core)):
                goal = (layer, span(half * 512, 512, 512), span(slot * 512, 512, 512))
                result.append((source, (*lead, span(0, 512)), 0, goal))
        return result

    (array,) = lay_out(here, copies, [w_fc, *came, swapped], [(2, 1024, 1024)])
    return array


def lay_proj(here, w_proj, came):
    swapped = other_core(jnp.stack(came))

    def copies(pipe, high, core):
        result = [(0, (span(0, 512),), 0, (pipe, span(high * 512, 512, 512)))]
        for i, (layer, slot) in enumerate(sources_of(pipe, high)):
            for source, lead, half in ((1 + i, (), core), (4, (i,), 1 - core)):
                goal = (layer, span(slot * 512 + half * 256, 256, 256))
                result.append((source, (*lead, span(0, 256)), 0, goal))
        return result

    (array,) = lay_out(here, copies, [w_proj, *came, swapped], [(2, 1024, 1024)])
    return array


def on_device(
    inputs,
    segment_ids,
    cotangent,
    ln1_gain,
    ln1_bias,
    w_qkv,
    qv_bias,
    w_out,
    out_bias,
    ln2_gain,
    ln2_bias,
    w_fc,
    fc_bias,
    w_proj,
    proj_bias,
):
    pipe = lax.axis_index("pipe")
    tensor = lax.axis_index("tensor")
    dp = lax.axis_index("dp")
    x, high, core = tensor // 2, tensor % 2, dp % 2
    here = (pipe, high, core)
    stream = turned(pick(inputs, pipe).reshape(BLOCK, WIDTH)).astype(f32)
    cotangent_rows = turned(pick(cotangent, pipe).reshape(BLOCK, WIDTH)).astype(f32)
    segments = pick(segment_ids, pipe).reshape(8, BLOCK)
    segments = jnp.where(high == core, segments, other_core(segments))
    slots = ((x - jnp.arange(4)) % 4) * 2
    blocks = jnp.concatenate([slots + core, slots + 1 - core])
    numbers = segments[blocks].reshape(-1)
    positions = (blocks[:, None] * BLOCK + jnp.arange(BLOCK)[None]).reshape(-1)
    allowed = (numbers[: 4 * BLOCK, None] == numbers[None]) & (
        positions[None] <= positions[: 4 * BLOCK, None]
    )

    smalls = jnp.concatenate(
        [
            ln1_gain,
            ln1_bias,
            out_bias,
            ln2_gain,
            ln2_bias,
            proj_bias,
            qv_bias.reshape(1, 256),
            fc_bias,
            jnp.zeros((1, 16 * 512 - 6912), bf16),
        ],
        axis=1,
    ).reshape(16, 512)
    before = along_z(smalls, 1)
    flat_w_qkv, turned_out = w_qkv[0].reshape(WIDTH, 384), w_out[0].T
    came_first = send_first(core, flat_w_qkv, turned_out, smalls)
    half_fc = lax.dynamic_slice_in_dim(w_fc[0], core * 512, 512, 0)
    half_proj = lax.dynamic_slice_in_dim(w_proj[0], core * 256, 256, 0)
    coming, laid = {}, {}

    def biases(all_small, layer):
        flat = all_small[layer].reshape(2, -1).astype(f32)
        pairs = flat[:, 6144:6400].reshape(2, 2, 128)
        none = jnp.zeros((2, 128), f32)
        qkv_bias = jnp.stack([pairs[:, 0], none, pairs[:, 1]], axis=1).reshape(-1)
        return qkv_bias, flat[:, 6400:6912].reshape(-1)

    def first_hook(step, value):
        if step == -1:
            laid["first"], value = lay_first(
                here, flat_w_qkv, turned_out, smalls, came_first, value
            )
            return second_hook(step, value, 0)
        if step == 0:
            sent, *laid["first"] = tied(half_fc, *laid["first"])
            value, *coming["fc"] = tied(value, *[along_z(sent, by) for by in ORDER[:2]])
            return value
        if step == 1:
            sent, *came = tied(half_fc, *coming["fc"])
            value, *coming["fc"] = tied(value, *came, along_z(sent, ORDER[2]))
            return value
        if step == 2:
            sent, *coming["fc"] = tied(half_proj, *coming["fc"])
            laid["fc"] = lay_fc(here, w_fc[0], coming["fc"])
            value, *coming["proj"] = tied(value, *[along_z(sent, by) for by in ORDER[:2]])
            return value
        sent, *came = tied(half_proj, *coming["proj"])
        value, last = tied(value, along_z(sent, ORDER[2]))
        laid["proj"] = lay_proj(here, w_proj[0], came + [last])
        return value, laid["fc"][0], laid["proj"][0]

    def second_hook(step, value, layer=1):
        if step == -1:
            all_qkv, all_out, all_small = laid["first"]
            return (value, all_qkv[layer], all_out[layer]) + biases(all_small, layer)
        return value if step < 3 else (value, laid["fc"][1], laid["proj"][1])

    vectors = []
    for layer in range(2):
        flat = jnp.where(pipe == layer, smalls, before).astype(f32).reshape(-1)
        vectors.append(tuple(flat[i * WIDTH : (i + 1) * WIDTH] for i in range(6)))

    first, weights_first, saved_first = layer_forward(
        stream, allowed, vectors[0], first_hook
    )
    second, weights_second, saved_second = layer_forward(
        first.astype(f32),
        allowed,
        vectors[1],
        second_hook,
    )
    waiting = {}

    def keep(step, value, group=None):
        if group is not None:
            waiting[step] = group
        return value

    middle_grad, early_one, late_one = layer_backward(
        cotangent_rows, allowed, vectors[1], weights_second, saved_second, keep
    )
    middle_low = middle_grad.astype(bf16)
    groups_one = (waiting[1], waiting[4])
    kept = {}

    def reduce_along(step, value, group=None):
        if step == 0:
            halved = [over_cores(item, core) for item in groups_one]
            value, kept["one"] = tied(value, jnp.concatenate(halved, axis=2))
            return value
        if step == 1:
            kept["near"] = near_y(kept["one"])
            kept["feed"] = group
            return value
        if step == 2:
            value, kept["near"] = tied(value, kept["near"])
            return value
        if step == 3:
            kept["one"] = far_y(kept["one"], kept["near"])
            value, kept["feed"] = tied(value, over_cores(kept["feed"], core))
            return value
        kept["one"], kept["feed"] = tied(kept["one"], kept["feed"])
        kept["near"] = near_y(kept["feed"])
        value, kept["attention"] = tied(value, over_cores(group, core))
        return value

    last_grad, early_zero, late_zero = layer_backward(
        middle_low.astype(f32), allowed, vectors[0], weights_first, saved_first, reduce_along
    )
    last_low = last_grad.astype(bf16)
    y = dp // 2
    near = jnp.concatenate([kept["near"], near_y(kept["attention"])], axis=1)
    far = [pick(kept[name], (y + 2) % 4, 1) for name in ("feed", "attention")]
    zero = near + along_y(jnp.concatenate(far, axis=1), 2).astype(f32)
    total = back_over_y(over_z(zero.astype(bf16), kept["one"], pipe, high))

    def bias_rows(fc_bias_grad):
        return place(jnp.zeros((4, WIDTH), f32), fc_bias_grad[None], (x, 0))

    def late_rows(late):
        gain_grad, shift_grad, qkv_grad = late
        parts = qkv_grad.reshape(2, 3, 128)
        pairs = jnp.stack([parts[:, 0], parts[:, 2]]).reshape(2, 256)
        wide = place(jnp.zeros((2, WIDTH), f32), pairs, (0, x * 256))
        return jnp.concatenate([gain_grad[None], shift_grad[None], wide])

    small = jnp.stack(
        [
            jnp.concatenate([jnp.stack(early[:4]), bias_rows(early[4]), late_rows(late)])
            for early, late in ((early_zero, late_zero), (early_one, late_one))
        ]
    )
    small = everywhere(small, pipe)
    early, late = small[:8], small[8:]

    feed_total = total[:, :, :128].reshape(2, 512, WIDTH)
    attention_total = total[:, :, 128:].reshape(2, 256, WIDTH)
    w_fc_grad = feed_total[:, :256].reshape(512, WIDTH).T.astype(f32)
    w_proj_grad = feed_total[:, 256:].reshape(512, WIDTH).astype(f32)
    w_qkv_grad = attention_total[:, :192].reshape(384, WIDTH).T.reshape(WIDTH, 3, 128).astype(f32)
    w_out_grad = attention_total[:, 192:].reshape(128, WIDTH).astype(f32)
    fc_bias_grad = lax.dynamic_slice(early[4:], (x, high * 512), (1, 512))[0]
    qv_bias_grad = lax.dynamic_slice(late[2:], (0, tensor * 128), (2, 128))

    def placed(own, other):
        def crossed(array):
            return move(
                array,
                AXES,
                lambda x, z, y, core: (x, core * 2 + 1 - z % 2, y, z // 2),
            )

        stays = turned(own)
        comes = crossed(other)
        return jnp.where(pipe == 0, jnp.stack([stays, comes]), jnp.stack([comes, stays]))

    activations = placed(
        jnp.where(pipe == 0, first, second), jnp.where(pipe == 0, second, first)
    )
    in_grads = placed(
        jnp.where(pipe == 0, last_low, middle_low), jnp.where(pipe == 0, middle_low, last_low)
    )
    return (
        activations[None, :, :, None],
        in_grads[None, :, :, None],
        late[0][None],
        late[1][None],
        w_qkv_grad[None],
        qv_bias_grad[None],
        w_out_grad[None],
        early[0][None],
        early[1][None],
        early[2][None],
        w_fc_grad[None],
        fc_bias_grad[None],
        w_proj_grad[None],
        early[3][None],
    )


def solution(mesh):
    return jax.shard_map(
        on_device,
        mesh=mesh,
        in_specs=(
            P(None, "tensor", "dp", None),
            P(None, "dp", None),
            P(None, "tensor", "dp", None),
            P("pipe", None),
            P("pipe", None),
            P("pipe", None, None, "tensor"),
            P("pipe", None, "tensor"),
            P("pipe", "tensor", None),
            P("pipe", None),
            P("pipe", None),
            P("pipe", None),
            P("pipe", None, "tensor"),
            P("pipe", "tensor"),
            P("pipe", "tensor", None),
            P("pipe", None),
        ),
        out_specs=(
            P("pipe", None, "tensor", "dp", None),
            P("pipe", None, "tensor", "dp", None),
            P("pipe", None),
            P("pipe", None),
            P("pipe", None, None, "tensor"),
            P("pipe", None, "tensor"),
            P("pipe", "tensor", None),
            P("pipe", None),
            P("pipe", None),
            P("pipe", None),
            P("pipe", None, "tensor"),
            P("pipe", "tensor"),
            P("pipe", "tensor", None),
            P("pipe", None),
        ),
        check_vma=False,
    )
```
